1024 devices in a mesh: ctx: 64 (over y, z_hi, core), tp: 16 (over x, z_lo).
Axes of the slice: x: 4, y: 8, z: 16 (z_hi: 4, z_lo: 4; z = z_hi * 4 + z_lo), core: 2. Of those that a mesh axis runs over, the one named last changes fastest.
Arguments:
- tokens: bfloat16 [8192, 4096], P('ctx', 'tp'), may hold values from -6 to 6
- cotangent: bfloat16 [8192, 4096], P('ctx', 'tp'), may hold values from -6 to 6
- input_weight: bfloat16 [4096, 3, 4096], P(None, None, 'tp'), may hold values from -0.09375 to 0.09375
- output_weight: bfloat16 [4096, 4096], P('tp'), may hold values from -0.09375 to 0.09375
- short_taps: float32 [3, 4096, 3], P(None, 'tp'), may hold values from -3 to 3
- residues: float32 [4096, 16], P('tp'), may hold values from -0.34 to 0.34
- decay_rates: float32 [4096, 16], P('tp'), may hold values from 6.1035156e-05 to 0.05
- skip_gain: float32 [4096], P('tp'), may hold values from 0.1 to 1.9
Outputs:
- mixed: bfloat16 [8192, 4096], P('ctx', 'tp')
- grad_tokens: bfloat16 [8192, 4096], P('ctx', 'tp')
The draws below stay inside these ranges and needn't reach their ends.
All inputs are finite; a program needn't handle non-finite values.
Results may differ from the reference program's by a relative error of at most 0.022.
Values may be sent and summed in bfloat16 or wider, within the bound.
No kernel may reach another device: no remote copies, remote signals or barrier semaphores. Data moves between devices by JAX's collectives and lax.ppermute only.
A program may use at most 64 MiB of HBM per device.

```python
import jax
import jax.numpy as jnp
from jax import lax

D = 4096
ORDER = 16
KSHORT = 3
TOKENS = 8192
N_TP = 16


def mode_rates(key):
    lowest = jnp.log(jnp.float32(0.5 / TOKENS))
    highest = jnp.log(jnp.float32(0.05))
    spread = jax.random.uniform(key, (D, ORDER), jnp.float32, lowest, highest)
    return jnp.clip(jnp.exp(spread), 0.5 / TOKENS, 0.05)


def draw_decay_rates(key, part):
    return mode_rates(key)


def draw_residues(key, part):
    rates = mode_rates(key)
    key = jax.random.fold_in(key, 7)
    weight = jnp.clip(0.35 * jax.random.normal(key, (D, ORDER), jnp.float32), -1.05, 1.05)
    return weight * jnp.sqrt(2.0 * rates)


def levels(rng, dims, split, low, top_value):
    level, own = 1.0, jax.random.fold_in(rng, 6)
    for dim, blocks in split:
        steps = jnp.exp(jax.random.uniform(jax.random.fold_in(own, dim), (blocks,), jnp.float32, low / len(split), top_value / len(split)))
        level = level * jnp.repeat(steps, dims[dim] // blocks).reshape([-1 if axis == dim else 1 for axis in range(len(dims))])
    return level


def centred(own_key, shape, deviation, most, shards=(), kind=jnp.bfloat16):
    entries = deviation * jax.random.normal(own_key, shape, jnp.float32)
    if shards:
        entries = entries * levels(own_key, shape, shards, -0.22, 0.18)
    return jnp.clip(entries, -most, most).astype(kind)


def setup_inputs(seed: int = 0) -> dict:
    arg_keys = jax.random.split(jax.random.key(seed), 9)
    tokens = centred(arg_keys[0], (TOKENS, D), 1.0, 6.0, ((0, 64), (1, 16)))
    cotangent = centred(arg_keys[1], (TOKENS, D), 1.0, 6.0, ((0, 64), (1, 16)))
    input_weight = centred(arg_keys[2], (D, 3, D), D ** -0.5, 0.09375, ((2, 16),))
    output_weight = centred(arg_keys[3], (D, D), D ** -0.5, 0.09375, ((0, 16),))
    short_taps = centred(arg_keys[4], (3, D, KSHORT), 0.6, 3.0, ((1, 16),), jnp.float32)
    residues = draw_residues(jax.random.fold_in(arg_keys[8], 71), 0)
    decay_rates = draw_decay_rates(jax.random.fold_in(arg_keys[8], 71), 0)
    skip_gain = jnp.clip(1.0 + 0.18 * jax.random.normal(arg_keys[7], (D,), jnp.float32), 0.1, 1.9)
    return dict(tokens=tokens, cotangent=cotangent, input_weight=input_weight, output_weight=output_weight, short_taps=short_taps, residues=residues, decay_rates=decay_rates, skip_gain=skip_gain)


def short_forward(pieces, short_taps):
    tap_count = short_taps.shape[2]
    length = pieces.shape[2]
    padded = jnp.pad(pieces, ((0, 0), (0, 0), (tap_count - 1, 0)))
    total_sum = jnp.zeros(pieces.shape, jnp.float32)
    for tap_index in range(tap_count):
        start_at = tap_count - 1 - tap_index
        total_sum = total_sum + short_taps[:, :, tap_index:tap_index + 1] * padded[:, :, start_at:start_at + length]
    return total_sum


def short_adjoint(grads, short_taps):
    tap_count = short_taps.shape[2]
    length = grads.shape[2]
    padded = jnp.pad(grads, ((0, 0), (0, 0), (0, tap_count - 1)))
    total_sum = jnp.zeros(grads.shape, jnp.float32)
    for tap_index in range(tap_count):
        total_sum = total_sum + short_taps[:, :, tap_index:tap_index + 1] * padded[:, :, tap_index:tap_index + length]
    return total_sum


def long_filters(residues, decay_rates, length):
    offsets = jnp.arange(length).astype(jnp.float32)
    total_sum = jnp.zeros((residues.shape[0], length), jnp.float32)
    for order_index in range(residues.shape[1]):
        total_sum = total_sum + residues[:, order_index:order_index + 1] * jnp.exp(-decay_rates[:, order_index:order_index + 1] * offsets[None, :])
    return total_sum


def spectral_conv(signal, spectrum, length):
    return jnp.fft.irfft(jnp.fft.rfft(signal, 2 * length, axis=1) * spectrum, 2 * length, axis=1)[:, :length]


def tensor_sum(make_term):
    block_width = D // N_TP

    def step(index, total_sum):
        start_at = index * block_width
        term = make_term(start_at, block_width)
        rounded = lax.optimization_barrier(term.astype(jnp.bfloat16))
        return total_sum + rounded.astype(jnp.float32)

    return lax.fori_loop(0, N_TP, step, jnp.zeros((TOKENS, D), jnp.float32))


def reference(tokens, cotangent, input_weight, output_weight, short_taps, residues, decay_rates, skip_gain):
    length = tokens.shape[0]
    projected = jnp.einsum("td,dpc->pct", tokens.astype(jnp.float32), input_weight.astype(jnp.float32)).astype(jnp.bfloat16)
    back_grad = jnp.einsum("td,cd->ct", cotangent.astype(jnp.float32), output_weight.astype(jnp.float32)).astype(jnp.bfloat16)
    featured = short_forward(projected.astype(jnp.float32), short_taps)
    query, key_part, value_part = featured[0], featured[1], featured[2]
    gated_in = key_part * value_part
    spectrum = jnp.fft.rfft(long_filters(residues, decay_rates, length), 2 * length, axis=1)
    skip_col = skip_gain[:, None]
    conv_out = spectral_conv(gated_in, spectrum, length) + skip_col * gated_in
    hidden = (query * conv_out).astype(jnp.bfloat16)
    back_float = back_grad.astype(jnp.float32)
    grad_conv = back_float * query
    grad_query = back_float * conv_out
    grad_gated = spectral_conv(grad_conv, jnp.conj(spectrum), length) + skip_col * grad_conv
    grad_feat = jnp.stack([grad_query, grad_gated * value_part, grad_gated * key_part])
    grad_proj = short_adjoint(grad_feat, short_taps).astype(jnp.bfloat16)

    def mixed_term(start_at, block_width):
        hidden_block = lax.dynamic_slice_in_dim(hidden, start_at, block_width, 0)
        weight_block = lax.dynamic_slice_in_dim(output_weight, start_at, block_width, 0)
        return jnp.dot(hidden_block.T, weight_block, preferred_element_type=jnp.float32)

    def grad_term(start_at, block_width):
        grad_block = lax.dynamic_slice_in_dim(grad_proj, start_at, block_width, 1)
        weight_block = lax.dynamic_slice_in_dim(input_weight, start_at, block_width, 2)
        return jnp.einsum("pct,epc->te", grad_block.astype(jnp.float32), weight_block.astype(jnp.float32))

    mixed = tensor_sum(mixed_term).astype(jnp.bfloat16)
    grad_tokens = tensor_sum(grad_term).astype(jnp.bfloat16)
    return mixed, grad_tokens
```

```python
import functools

import jax
import jax.numpy as jnp
from jax import lax
from jax.experimental import pallas as pl
from jax.experimental.pallas import tpu as pltpu
from jax.sharding import Mesh
from jax.sharding import PartitionSpec as P

CTX = ("y", "zh", "core")
TP = ("x", "zl")
EDGE = 16
AHEAD = 2
BF16 = jnp.bfloat16
F32 = jnp.float32


def table_kernel(rates_ref, res_ref, up_ref, down_ref, filt_ref):
    order, rows, _ = up_ref.shape
    row = lax.broadcasted_iota(jnp.int32, (rows, 1), 0).astype(F32)
    span = rows - 8 + AHEAD
    total = jnp.zeros(filt_ref.shape, F32)
    for r in range(order):
        rate = rates_ref[r : r + 1, :]
        up = jnp.exp(-rate * (row + 1.0))
        up_ref[r] = up
        down_ref[r] = jnp.exp(-rate * (span - row))
        total = total + res_ref[r : r + 1, :] * up
    filt_ref[...] = total


def features(ext, proj_ref, prev_ref, next_ref, taps_ref, rows):
    block = proj_ref.shape[1]
    out = []
    for p in range(3):
        ext[p, :EDGE] = prev_ref[p].astype(F32)
        ext[p, EDGE : EDGE + block] = proj_ref[p].astype(F32)
        ext[p, EDGE + block :] = next_ref[p].astype(F32)
        total = taps_ref[p, 0:1, :] * ext[p, EDGE : EDGE + rows]
        for k in range(1, 3):
            total = total + taps_ref[p, k : k + 1, :] * ext[p, EDGE - k : EDGE - k + rows]
        out.append(total)
    return out


def back_rows(back_ref, back_next_ref, rows):
    whole = jnp.concatenate([back_ref[...].astype(F32), back_next_ref[...].astype(F32)], axis=0)
    row = lax.broadcasted_iota(jnp.int32, (rows, 1), 0)
    return jnp.where(row < back_ref.shape[0] + AHEAD, whole[:rows], 0.0), row


def state_kernel(
    proj_ref, prev_ref, next_ref, back_ref, back_next_ref, taps_ref, rates_ref, up_ref, down_ref,
    fwd_ref, bwd_ref, ext,
):
    order, rows, _ = up_ref.shape
    block = proj_ref.shape[1]
    query, key_part, value_part = features(ext, proj_ref, prev_ref, next_ref, taps_ref, rows)
    back, row = back_rows(back_ref, back_next_ref, rows)
    gated = jnp.where(row < block, key_part * value_part, 0.0)
    grad_conv = jnp.where(row >= AHEAD, back * query, 0.0)
    for r in range(order):
        scale = jnp.exp(rates_ref[r : r + 1, :] * (AHEAD + 1.0))
        fwd_ref[r : r + 1, :] = scale * jnp.sum(down_ref[r] * gated, axis=0, keepdims=True)
        bwd_ref[r : r + 1, :] = scale * jnp.sum(up_ref[r] * grad_conv, axis=0, keepdims=True)


def local_kernel(
    proj_ref, prev_ref, next_ref, back_ref, back_next_ref, taps_ref, res_ref, skip_ref, filt_ref,
    conv_ref, grad_ref, ext, pad,
):
    rows, width = conv_ref.shape
    query, key_part, value_part = features(ext, proj_ref, prev_ref, next_ref, taps_ref, rows)
    back, _ = back_rows(back_ref, back_next_ref, rows)
    zero = jnp.zeros((8, width), F32)
    pad[0, :8] = zero
    pad[0, 8:] = key_part * value_part
    pad[1, :rows] = back * query
    pad[1, rows:] = zero
    direct = skip_ref[...] + jnp.sum(res_ref[...], axis=0, keepdims=True)
    for lane in range(0, width, 128):
        lanes = slice(lane, lane + 128)
        total = direct[:, lanes] * pad[0, 8:, lanes]
        for m in range(1, 9):
            moved = pad[0, 8 - m : 8 - m + rows, lanes]
            for q in range(0, rows, 8):
                tap = filt_ref[q + m - 1 : q + m, lanes]
                part = total[q:] + tap * moved[: rows - q]
                total = part if q == 0 else jnp.concatenate([total[:q], part], axis=0)
        conv_ref[:, lanes] = total
        total = direct[:, lanes] * pad[1, :rows, lanes]
        for m in range(1, 9):
            moved = pad[1, m : m + rows, lanes]
            for q in range(0, rows, 8):
                tap = filt_ref[q + m - 1 : q + m, lanes]
                part = total[: rows - q] + tap * moved[q:]
                total = part if q == 0 else jnp.concatenate([part, total[rows - q :]], axis=0)
        grad_ref[:, lanes] = total


def finish_kernel(
    proj_ref, prev_ref, next_ref, back_ref, back_next_ref, taps_ref, res_ref, up_ref, down_ref,
    conv_ref, grad_ref, ahead_ref, behind_ref,
    hidden_ref, out_ref, ext, feat,
):
    order, rows, _ = up_ref.shape
    block = proj_ref.shape[1]
    query, key_part, value_part = features(ext, proj_ref, prev_ref, next_ref, taps_ref, rows)
    back, _ = back_rows(back_ref, back_next_ref, rows)
    conv_out = conv_ref[...]
    grad_gated = grad_ref[...]
    for r in range(order):
        res = res_ref[r : r + 1, :]
        conv_out = conv_out + (res * ahead_ref[r : r + 1, :]) * up_ref[r]
        grad_gated = grad_gated + (res * behind_ref[r : r + 1, :]) * down_ref[r]
    hidden_ref[...] = (query * conv_out)[:block].astype(BF16)
    feat[0] = back * conv_out
    feat[1] = grad_gated * value_part
    feat[2] = grad_gated * key_part
    for p in range(3):
        total = taps_ref[p, 0:1, :] * feat[p, :block]
        for k in range(1, 3):
            total = total + taps_ref[p, k : k + 1, :] * feat[p, k : k + block]
        out_ref[p] = total.astype(BF16)


def call(kernel, outs, scratch, *args):
    return pl.pallas_call(
        kernel,
        out_shape=outs,
        scratch_shapes=scratch,
        in_specs=[pl.BlockSpec(memory_space=pltpu.VMEM)] * len(args),
        out_specs=jax.tree.map(lambda _: pl.BlockSpec(memory_space=pltpu.VMEM), outs),
        compiler_params=pltpu.CompilerParams(vmem_limit_bytes=40 * 2**20),
    )(*args)


def shape(*dims, dtype=F32):
    return jax.ShapeDtypeStruct(dims, dtype)


def spread(array, axis, count):
    copies = jnp.broadcast_to(array[None], (count,) + array.shape)
    return lax.all_to_all(copies, axis, 0, 0, tiled=True)


def scan_states(sizes, fwd, bwd, rates, block):
    n_y, n_z = sizes["y"], sizes["zh"]
    core = lax.axis_index("core")
    y = lax.axis_index("y")
    zh = lax.axis_index("zh")
    later = core == 1
    swap = [(0, 1), (1, 0)]

    def fade(tokens):
        return jnp.exp(-rates * jnp.asarray(tokens, F32))

    beside = lax.ppermute(jnp.where(later, bwd, fwd), "core", swap)
    chip = jnp.where(later, fwd, bwd) + fade(block) * beside
    place = jnp.where(later, zh, n_z - 1 - zh)
    before = jnp.zeros_like(chip)
    whole = fade(2 * block * (n_z - 1 - place)) * chip
    for k in range(1, n_z):
        pairs = [
            (2 * i + c, 2 * ((i + k if c else i - k) % n_z) + c)
            for i in range(n_z)
            for c in range(2)
        ]
        got = lax.ppermute(chip, ("zh", "core"), pairs)
        source = lax.rem(place - k + n_z, n_z)
        whole = whole + fade(2 * block * (n_z - 1 - source)) * got
        before = before + jnp.where(k <= place, fade(2 * block * (k - 1)) * got, 0.0)
    groups = spread(whole, "y", n_y)
    mine = jnp.where(later, y, n_y - 1 - y)
    far = jnp.zeros_like(chip)
    for i in range(n_y):
        source = jnp.where(later, i, n_y - 1 - i)
        gap = 2 * n_z * block * jnp.maximum(mine - 1 - source, 0)
        far = far + jnp.where(source < mine, fade(gap) * groups[i], 0.0)
    enter = before + fade(2 * block * place) * far
    other = lax.ppermute(enter, "core", swap)
    own = beside + fade(block) * enter
    return jnp.where(later, own, other), jnp.where(later, other, own)


def shards(
    sizes,
    tokens,
    cotangent,
    input_weight,
    output_weight,
    short_taps,
    residues,
    decay_rates,
    skip_gain,
):
    n_x, n_zl = sizes["x"], sizes["zl"]
    n_ctx = sizes["y"] * sizes["zh"] * sizes["core"]
    block, part = tokens.shape
    width = output_weight.shape[0]
    order = residues.shape[1]
    rows = block + 8
    taps = short_taps.transpose(0, 2, 1)
    rates = decay_rates.T
    res = residues.T
    skip = skip_gain[None]
    up, down, filt = call(
        table_kernel,
        [shape(order, rows, width), shape(order, rows, width), shape(rows, width)],
        [],
        rates,
        res,
    )
    both = jnp.concatenate([tokens, cotangent], axis=0)
    both = spread(spread(both, "zl", n_zl), "x", n_x)
    weight_in = input_weight.reshape(n_x, n_zl, part, 3, width)
    weight_out = output_weight.reshape(width, n_x, n_zl, part)
    proj = jnp.einsum(
        "xztf,xzfpc->ptc", both[:, :, :block], weight_in, preferred_element_type=F32
    ).astype(BF16)
    back = jnp.einsum(
        "xztf,cxzf->tc", both[:, :, block:], weight_out, preferred_element_type=F32
    ).astype(BF16)
    to_next = [(i, i + 1) for i in range(n_ctx - 1)]
    to_prev = [(i + 1, i) for i in range(n_ctx - 1)]
    prev = lax.ppermute(proj[:, block - EDGE :], CTX, to_next)
    first = jnp.concatenate([proj[:, :EDGE], back[None, :EDGE]], axis=0)
    first = lax.ppermute(first, CTX, to_prev)
    common = (proj, prev, first[:3], back, first[3], taps)
    ext = pltpu.VMEM((3, block + 2 * EDGE, width), F32)
    fwd, bwd = call(
        state_kernel,
        [shape(order, width), shape(order, width)],
        [ext],
        *common,
        rates,
        up,
        down,
    )
    conv, grad = call(
        local_kernel,
        [shape(rows, width), shape(rows, width)],
        [ext, pltpu.VMEM((2, rows + 8, width), F32)],
        *common,
        res,
        skip,
        filt,
    )
    ahead, behind = scan_states(sizes, fwd, bwd, rates, block)
    hidden, grad_proj = call(
        finish_kernel,
        [shape(block, width, dtype=BF16), shape(3, block, width, dtype=BF16)],
        [ext, pltpu.VMEM((3, rows, width), F32)],
        *common,
        res,
        up,
        down,
        conv,
        grad,
        ahead,
        behind,
    )
    mixed = jnp.einsum("tc,cxzf->xztf", hidden, weight_out, preferred_element_type=F32)
    grad_tok = jnp.einsum("ptc,xzfpc->xztf", grad_proj, weight_in, preferred_element_type=F32)
    terms = jnp.concatenate([mixed.astype(BF16), grad_tok.astype(BF16)], axis=2)
    terms = lax.all_to_all(terms, "x", 0, 0, tiled=True)
    terms = jnp.sum(terms.astype(F32), axis=0).astype(BF16)
    terms = lax.all_to_all(terms, "zl", 0, 0, tiled=True)
    total = jnp.sum(terms.astype(F32), axis=0).astype(BF16)
    return total[:block], total[block:]


def solution(mesh, dims=(8, 4, 2, 4, 4)):
    fine = Mesh(mesh.devices.reshape(dims), CTX + TP)
    sizes = dict(zip(CTX + TP, dims))
    return jax.shard_map(
        functools.partial(shards, sizes),
        mesh=fine,
        in_specs=(
            P(CTX, TP),
            P(CTX, TP),
            P(None, None, TP),
            P(TP, None),
            P(None, TP, None),
            P(TP, None),
            P(TP, None),
            P(TP),
        ),
        out_specs=(P(CTX, TP), P(CTX, TP)),
        check_vma=False,
    )
```

```python
import functools

import jax
import jax.numpy as jnp
from jax import lax
from jax.experimental import pallas as pl
from jax.experimental.pallas import tpu as pltpu
from jax.sharding import Mesh
from jax.sharding import PartitionSpec as P

CTX = ("y", "zh", "core")
TP = ("x", "zl")
EDGE = 16
AHEAD = 2
BF16 = jnp.bfloat16
F32 = jnp.float32


def table_kernel(rates_ref, res_ref, up_ref, down_ref, filt_ref):
    order, rows, _ = up_ref.shape
    row = lax.broadcasted_iota(jnp.int32, (rows, 1), 0).astype(F32)
    span = rows - 8 + AHEAD
    total = jnp.zeros(filt_ref.shape, F32)
    for r in range(order):
        rate = rates_ref[r : r + 1, :]
        up = jnp.exp(-rate * (row + 1.0))
        up_ref[r] = up
        down_ref[r] = jnp.exp(-rate * (span - row))
        total = total + res_ref[r : r + 1, :] * up
    filt_ref[...] = total


def features(ext, proj_ref, prev_ref, next_ref, taps_ref, rows):
    block = proj_ref.shape[1]
    out = []
    for p in range(3):
        ext[p, :EDGE] = prev_ref[p].astype(F32)
        ext[p, EDGE : EDGE + block] = proj_ref[p].astype(F32)
        ext[p, EDGE + block :] = next_ref[p].astype(F32)
        total = taps_ref[p, 0:1, :] * ext[p, EDGE : EDGE + rows]
        for k in range(1, 3):
            total = total + taps_ref[p, k : k + 1, :] * ext[p, EDGE - k : EDGE - k + rows]
        out.append(total)
    return out


def back_rows(back_ref, back_next_ref, rows):
    whole = jnp.concatenate([back_ref[...].astype(F32), back_next_ref[...].astype(F32)], axis=0)
    row = lax.broadcasted_iota(jnp.int32, (rows, 1), 0)
    return jnp.where(row < back_ref.shape[0] + AHEAD, whole[:rows], 0.0), row


def state_kernel(
    place_ref, proj_ref, prev_ref, next_ref, back_ref, back_next_ref, taps_ref, rates_ref, up_ref, down_ref,
    fwd_ref, bwd_ref, send_ref, ext,
):
    order, rows, _ = up_ref.shape
    block = proj_ref.shape[1]
    query, key_part, value_part = features(ext, proj_ref, prev_ref, next_ref, taps_ref, rows)
    back, row = back_rows(back_ref, back_next_ref, rows)
    gated = jnp.where(row < block, key_part * value_part, 0.0)
    grad_conv = jnp.where(row >= AHEAD, back * query, 0.0)
    for r in range(order):
        scale = jnp.exp(rates_ref[r : r + 1, :] * (AHEAD + 1.0))
        fwd_ref[r : r + 1, :] = scale * jnp.sum(down_ref[r] * gated, axis=0, keepdims=True)
        bwd_ref[r : r + 1, :] = scale * jnp.sum(up_ref[r] * grad_conv, axis=0, keepdims=True)
    for i in range(send_ref.shape[0]):
        send_ref[i] = jnp.where(place_ref[0] < i, fwd_ref[...], bwd_ref[...]).astype(BF16)


def chain_kernel(block, place_ref, rates_ref, fwd_ref, bwd_ref, got_ref, send_ref):
    rates = rates_ref[...]
    order = rates.shape[0]
    groups, members = got_ref.shape[0], send_ref.shape[0]
    group, member = place_ref[0], place_ref[1]

    def fade(blocks):
        return jnp.exp(-rates * (block * jnp.maximum(blocks, 0)).astype(F32))

    fwd, bwd = fwd_ref[...], bwd_ref[...]
    before = jnp.zeros_like(fwd)
    after = jnp.zeros_like(bwd)
    for i in range(groups):
        got = got_ref[i].astype(F32)
        before = before + jnp.where(i < group, fade(members * (group - 1 - i)) * got, 0.0)
        after = after + jnp.where(i > group, fade(members * (i - 1 - group)) * got, 0.0)
    for i in range(members):
        ahead = fade(members - 1 + i - member) * before
        ahead = ahead + jnp.where(i > member, fade(i - member - 1) * fwd, 0.0)
        behind = fade(members - 1 + member - i) * after
        behind = behind + jnp.where(i < member, fade(member - i - 1) * bwd, 0.0)
        send_ref[i, :order] = ahead.astype(BF16)
        send_ref[i, order:] = behind.astype(BF16)


def local_kernel(
    proj_ref, prev_ref, next_ref, back_ref, back_next_ref, taps_ref, res_ref, skip_ref, filt_ref,
    conv_ref, grad_ref, ext, pad,
):
    rows, width = conv_ref.shape
    query, key_part, value_part = features(ext, proj_ref, prev_ref, next_ref, taps_ref, rows)
    back, _ = back_rows(back_ref, back_next_ref, rows)
    zero = jnp.zeros((8, width), F32)
    pad[0, :8] = zero
    pad[0, 8:] = key_part * value_part
    pad[1, :rows] = back * query
    pad[1, rows:] = zero
    direct = skip_ref[...] + jnp.sum(res_ref[...], axis=0, keepdims=True)
    for lane in range(0, width, 128):
        lanes = slice(lane, lane + 128)
        total = direct[:, lanes] * pad[0, 8:, lanes]
        for m in range(1, 9):
            moved = pad[0, 8 - m : 8 - m + rows, lanes]
            for q in range(0, rows, 8):
                tap = filt_ref[q + m - 1 : q + m, lanes]
                part = total[q:] + tap * moved[: rows - q]
                total = part if q == 0 else jnp.concatenate([total[:q], part], axis=0)
        conv_ref[:, lanes] = total
        total = direct[:, lanes] * pad[1, :rows, lanes]
        for m in range(1, 9):
            moved = pad[1, m : m + rows, lanes]
            for q in range(0, rows, 8):
                tap = filt_ref[q + m - 1 : q + m, lanes]
                part = total[: rows - q] + tap * moved[q:]
                total = part if q == 0 else jnp.concatenate([part, total[rows - q :]], axis=0)
        grad_ref[:, lanes] = total


def finish_kernel(
    proj_ref, prev_ref, next_ref, back_ref, back_next_ref, taps_ref, res_ref, up_ref, down_ref,
    conv_ref, grad_ref, got_ref,
    hidden_ref, out_ref, ext, feat,
):
    order, rows, _ = up_ref.shape
    block = proj_ref.shape[1]
    query, key_part, value_part = features(ext, proj_ref, prev_ref, next_ref, taps_ref, rows)
    back, _ = back_rows(back_ref, back_next_ref, rows)
    conv_out = conv_ref[...]
    grad_gated = grad_ref[...]
    states = jnp.sum(got_ref[...].astype(F32), axis=0)
    ahead, behind = states[:order], states[order:]
    for r in range(order):
        res = res_ref[r : r + 1, :]
        conv_out = conv_out + (res * ahead[r : r + 1]) * up_ref[r]
        grad_gated = grad_gated + (res * behind[r : r + 1]) * down_ref[r]
    hidden_ref[...] = (query * conv_out)[:block].astype(BF16)
    feat[0] = back * conv_out
    feat[1] = grad_gated * value_part
    feat[2] = grad_gated * key_part
    for p in range(3):
        total = taps_ref[p, 0:1, :] * feat[p, :block]
        for k in range(1, 3):
            total = total + taps_ref[p, k : k + 1, :] * feat[p, k : k + block]
        out_ref[p] = total.astype(BF16)


def call(kernel, outs, scratch, *args, flops=0):
    whole = pl.BlockSpec(memory_space=pltpu.VMEM)
    specs = [
        pl.BlockSpec(memory_space=pltpu.SMEM) if a.dtype == jnp.int32 else whole for a in args
    ]
    cost = pl.CostEstimate(flops=flops, bytes_accessed=0, transcendentals=0) if flops else None
    return pl.pallas_call(
        kernel,
        out_shape=outs,
        scratch_shapes=scratch,
        in_specs=specs,
        out_specs=jax.tree.map(lambda _: whole, outs),
        cost_estimate=cost,
        compiler_params=pltpu.CompilerParams(vmem_limit_bytes=40 * 2**20),
    )(*args)


def shape(*dims, dtype=F32):
    return jax.ShapeDtypeStruct(dims, dtype)


def spread(array, axis, count):
    copies = jnp.broadcast_to(array[None], (count,) + array.shape)
    return lax.all_to_all(copies, axis, 0, 0, tiled=True)


def shards(
    sizes,
    tokens,
    cotangent,
    input_weight,
    output_weight,
    short_taps,
    residues,
    decay_rates,
    skip_gain,
):
    n_x, n_zl = sizes["x"], sizes["zl"]
    n_ctx = sizes["y"] * sizes["zh"] * sizes["core"]
    block, part = tokens.shape
    width = output_weight.shape[0]
    order = residues.shape[1]
    rows = block + 8
    taps = short_taps.transpose(0, 2, 1)
    rates = decay_rates.T
    res = residues.T
    skip = skip_gain[None]
    up, down, filt = call(
        table_kernel,
        [shape(order, rows, width), shape(order, rows, width), shape(rows, width)],
        [],
        rates,
        res,
    )
    both = jnp.concatenate([tokens, cotangent], axis=0)
    both = spread(spread(both, "zl", n_zl), "x", n_x)
    weight_in = input_weight.reshape(n_x, n_zl, part, 3, width)
    weight_out = output_weight.reshape(width, n_x, n_zl, part)
    proj = jnp.einsum(
        "xztf,xzfpc->ptc", both[:, :, :block], weight_in, preferred_element_type=F32
    ).astype(BF16)
    back = jnp.einsum(
        "xztf,cxzf->tc", both[:, :, block:], weight_out, preferred_element_type=F32
    ).astype(BF16)
    to_next = [(i, i + 1) for i in range(n_ctx - 1)]
    to_prev = [(i + 1, i) for i in range(n_ctx - 1)]
    prev = lax.ppermute(proj[:, block - EDGE :], CTX, to_next)
    first = jnp.concatenate([proj[:, :EDGE], back[None, :EDGE]], axis=0)
    first = lax.ppermute(first, CTX, to_prev)
    common = (proj, prev, first[:3], back, first[3], taps)
    ext = pltpu.VMEM((3, block + 2 * EDGE, width), F32)
    group = lax.axis_index("y")
    member = lax.axis_index("zh") * sizes["core"] + lax.axis_index("core")
    place = jnp.stack([group, member]).astype(jnp.int32)
    fwd, bwd, send = call(
        state_kernel,
        [shape(order, width), shape(order, width), shape(sizes["y"], order, width, dtype=BF16)],
        [ext],
        place,
        *common,
        rates,
        up,
        down,
    )
    conv, grad = call(
        local_kernel,
        [shape(rows, width), shape(rows, width)],
        [ext, pltpu.VMEM((2, rows + 8, width), F32)],
        *common,
        res,
        skip,
        filt,
        flops=3 * 10**9,
    )
    got = lax.all_to_all(send, "y", 0, 0, tiled=True)
    send = call(
        functools.partial(chain_kernel, block),
        shape(sizes["zh"] * sizes["core"], 2 * order, width, dtype=BF16),
        [],
        place,
        rates,
        fwd,
        bwd,
        got,
    )
    states = lax.all_to_all(send, ("zh", "core"), 0, 0, tiled=True)
    hidden, grad_proj = call(
        finish_kernel,
        [shape(block, width, dtype=BF16), shape(3, block, width, dtype=BF16)],
        [ext, pltpu.VMEM((3, rows, width), F32)],
        *common,
        res,
        up,
        down,
        conv,
        grad,
        states,
    )
    mixed = jnp.einsum("tc,cxzf->xztf", hidden, weight_out, preferred_element_type=F32)
    grad_tok = jnp.einsum("ptc,xzfpc->xztf", grad_proj, weight_in, preferred_element_type=F32)
    terms = jnp.concatenate([mixed.astype(BF16), grad_tok.astype(BF16)], axis=2)
    terms = lax.all_to_all(terms, "x", 0, 0, tiled=True)
    terms = jnp.sum(terms.astype(F32), axis=0).astype(BF16)
    terms = lax.all_to_all(terms, "zl", 0, 0, tiled=True)
    total = jnp.sum(terms.astype(F32), axis=0).astype(BF16)
    return total[:block], total[block:]


def solution(mesh, dims=(8, 4, 2, 4, 4)):
    fine = Mesh(mesh.devices.reshape(dims), CTX + TP)
    sizes = dict(zip(CTX + TP, dims))
    return jax.shard_map(
        functools.partial(shards, sizes),
        mesh=fine,
        in_specs=(
            P(CTX, TP),
            P(CTX, TP),
            P(None, None, TP),
            P(TP, None),
            P(None, TP, None),
            P(TP, None),
            P(TP, None),
            P(TP),
        ),
        out_specs=(P(CTX, TP), P(CTX, TP)),
        check_vma=False,
    )
```

```python
import functools

import jax
import jax.numpy as jnp
from jax import lax
from jax.experimental import pallas as pl
from jax.experimental.pallas import tpu as pltpu
from jax.sharding import Mesh
from jax.sharding import PartitionSpec as P

CTX = ("y", "zh", "core")
TP = ("x", "zl")
EDGE = 8
NEAR = 4
AHEAD = 2
BF16 = jnp.bfloat16
F32 = jnp.float32


def table_kernel(rates_ref, res_ref, up_ref, down_ref, filt_ref):
    order, rows, _ = up_ref.shape
    row = lax.broadcasted_iota(jnp.int32, (rows, 1), 0).astype(F32)
    span = rows - 8 + AHEAD
    total = jnp.zeros(filt_ref.shape, F32)
    for r in range(order):
        rate = rates_ref[r : r + 1, :]
        up = jnp.exp(-rate * (row + 1.0))
        up_ref[r] = up
        down_ref[r] = jnp.exp(-rate * (span - row))
        total = total + res_ref[r : r + 1, :] * up
    filt_ref[...] = total


def features(ext, proj_ref, taps_ref, rows):
    block = proj_ref.shape[1] - EDGE - 2 * NEAR
    out = []
    for p in range(3):
        proj = proj_ref[p].astype(F32)
        edge = proj[block : block + EDGE]
        near = proj[block + EDGE :]
        ext[p, :EDGE] = edge
        ext[p, EDGE : EDGE + block] = proj[:block]
        ext[p, EDGE + block :] = near
        total = taps_ref[p, 0:1, :] * ext[p, EDGE : EDGE + rows]
        for k in range(1, 3):
            total = total + taps_ref[p, k : k + 1, :] * ext[p, EDGE - k : EDGE - k + rows]
        out.append(total)
    return out


def back_rows(back_ref, rows):
    block = back_ref.shape[0] - EDGE - 2 * NEAR
    back = back_ref[...].astype(F32)
    near = pltpu.roll(back[block + EDGE :], NEAR, 0)
    row = lax.broadcasted_iota(jnp.int32, (rows, 1), 0)
    whole = jnp.concatenate([back[:block], near], axis=0)
    return jnp.where(row < block + AHEAD, whole, 0.0), row


def state_kernel(
    place_ref, proj_ref, back_ref, taps_ref, rates_ref, up_ref, down_ref,
    fwd_ref, bwd_ref, send_ref, ext,
):
    order, rows, _ = up_ref.shape
    block = rows - 8
    query, key_part, value_part = features(ext, proj_ref, taps_ref, rows)
    back, row = back_rows(back_ref, rows)
    gated = jnp.where(row < block, key_part * value_part, 0.0)
    grad_conv = jnp.where(row >= AHEAD, back * query, 0.0)
    for r in range(order):
        scale = jnp.exp(rates_ref[r : r + 1, :] * (AHEAD + 1.0))
        fwd_ref[r : r + 1, :] = scale * jnp.sum(down_ref[r] * gated, axis=0, keepdims=True)
        bwd_ref[r : r + 1, :] = scale * jnp.sum(up_ref[r] * grad_conv, axis=0, keepdims=True)
    for i in range(send_ref.shape[0]):
        send_ref[i] = jnp.where(place_ref[0] < i, fwd_ref[...], bwd_ref[...]).astype(BF16)


def chain_kernel(block, place_ref, rates_ref, fwd_ref, bwd_ref, got_ref, send_ref):
    rates = rates_ref[...]
    order = rates.shape[0]
    groups, members = got_ref.shape[0], send_ref.shape[0]
    group, member = place_ref[0], place_ref[1]

    def fade(blocks):
        return jnp.exp(-rates * (block * jnp.maximum(blocks, 0)).astype(F32))

    fwd, bwd = fwd_ref[...], bwd_ref[...]
    before = jnp.zeros_like(fwd)
    after = jnp.zeros_like(bwd)
    for i in range(groups):
        got = got_ref[i].astype(F32)
        before = before + jnp.where(i < group, fade(members * (group - 1 - i)) * got, 0.0)
        after = after + jnp.where(i > group, fade(members * (i - 1 - group)) * got, 0.0)
    for i in range(members):
        ahead = fade(members - 1 + i - member) * before
        ahead = ahead + jnp.where(i > member, fade(i - member - 1) * fwd, 0.0)
        behind = fade(members - 1 + member - i) * after
        behind = behind + jnp.where(i < member, fade(member - i - 1) * bwd, 0.0)
        send_ref[i, :order] = ahead.astype(BF16)
        send_ref[i, order:] = behind.astype(BF16)


def local_kernel(
    proj_ref, back_ref, taps_ref, res_ref, skip_ref, filt_ref,
    conv_ref, grad_ref, ext, pad,
):
    rows, width = conv_ref.shape
    query, key_part, value_part = features(ext, proj_ref, taps_ref, rows)
    back, _ = back_rows(back_ref, rows)
    zero = jnp.zeros((8, width), F32)
    pad[0, :8] = zero
    pad[0, 8:] = key_part * value_part
    pad[1, :rows] = back * query
    pad[1, rows:] = zero
    direct = skip_ref[...] + jnp.sum(res_ref[...], axis=0, keepdims=True)
    for lane in range(0, width, 128):
        lanes = slice(lane, lane + 128)
        total = direct[:, lanes] * pad[0, 8:, lanes]
        for m in range(1, 9):
            moved = pad[0, 8 - m : 8 - m + rows, lanes]
            for q in range(0, rows, 8):
                tap = filt_ref[q + m - 1 : q + m, lanes]
                part = total[q:] + tap * moved[: rows - q]
                total = part if q == 0 else jnp.concatenate([total[:q], part], axis=0)
        conv_ref[:, lanes] = total
        total = direct[:, lanes] * pad[1, :rows, lanes]
        for m in range(1, 9):
            moved = pad[1, m : m + rows, lanes]
            for q in range(0, rows, 8):
                tap = filt_ref[q + m - 1 : q + m, lanes]
                part = total[: rows - q] + tap * moved[q:]
                total = part if q == 0 else jnp.concatenate([part, total[rows - q :]], axis=0)
        grad_ref[:, lanes] = total


def finish_kernel(
    proj_ref, back_ref, taps_ref, res_ref, up_ref, down_ref,
    conv_ref, grad_ref, got_ref,
    hidden_ref, out_ref, ext, feat,
):
    order, rows, _ = up_ref.shape
    block = rows - 8
    query, key_part, value_part = features(ext, proj_ref, taps_ref, rows)
    back, _ = back_rows(back_ref, rows)
    conv_out = conv_ref[...]
    grad_gated = grad_ref[...]
    states = jnp.sum(got_ref[...].astype(F32), axis=0)
    ahead, behind = states[:order], states[order:]
    for r in range(order):
        res = res_ref[r : r + 1, :]
        conv_out = conv_out + (res * ahead[r : r + 1]) * up_ref[r]
        grad_gated = grad_gated + (res * behind[r : r + 1]) * down_ref[r]
    hidden_ref[...] = (query * conv_out)[:block].astype(BF16)
    feat[0] = back * conv_out
    feat[1] = grad_gated * value_part
    feat[2] = grad_gated * key_part
    for p in range(3):
        total = taps_ref[p, 0:1, :] * feat[p, :block]
        for k in range(1, 3):
            total = total + taps_ref[p, k : k + 1, :] * feat[p, k : k + block]
        out_ref[p] = total.astype(BF16)


def call(kernel, outs, scratch, *args, flops=0):
    whole = pl.BlockSpec(memory_space=pltpu.VMEM)
    specs = [
        pl.BlockSpec(memory_space=pltpu.SMEM) if a.dtype == jnp.int32 else whole for a in args
    ]
    cost = pl.CostEstimate(flops=flops, bytes_accessed=0, transcendentals=0) if flops else None
    return pl.pallas_call(
        kernel,
        out_shape=outs,
        scratch_shapes=scratch,
        in_specs=specs,
        out_specs=jax.tree.map(lambda _: whole, outs),
        cost_estimate=cost,
        compiler_params=pltpu.CompilerParams(vmem_limit_bytes=40 * 2**20),
    )(*args)


def shape(*dims, dtype=F32):
    return jax.ShapeDtypeStruct(dims, dtype)


def spread(array, axis, count):
    copies = jnp.broadcast_to(array[None], (count,) + array.shape)
    return lax.all_to_all(copies, axis, 0, 0, tiled=True)


def shards(
    sizes,
    tokens,
    cotangent,
    input_weight,
    output_weight,
    short_taps,
    residues,
    decay_rates,
    skip_gain,
):
    n_x, n_zl = sizes["x"], sizes["zl"]
    n_ctx = sizes["y"] * sizes["zh"] * sizes["core"]
    block, part = tokens.shape
    width = output_weight.shape[0]
    order = residues.shape[1]
    rows = block + 8
    taps = short_taps.transpose(0, 2, 1)
    rates = decay_rates.T
    res = residues.T
    skip = skip_gain[None]
    up, down, filt = call(
        table_kernel,
        [shape(order, rows, width), shape(order, rows, width), shape(rows, width)],
        [],
        rates,
        res,
    )
    to_next = [(i, i + 1) for i in range(n_ctx - 1)]
    to_prev = [(i + 1, i) for i in range(n_ctx - 1)]
    edge = lax.ppermute(tokens[block - EDGE :], CTX, to_next)
    near = jnp.concatenate([tokens[:NEAR], cotangent[:NEAR]], axis=0)
    near = lax.ppermute(near, CTX, to_prev)
    both = jnp.concatenate([tokens, edge, near, cotangent], axis=0)
    both = spread(spread(both, "zl", n_zl), "x", n_x)
    ends = block + EDGE + 2 * NEAR
    whole_in = both[:, :, :ends]
    whole_grad = jnp.concatenate([both[:, :, ends:], both[:, :, block:ends]], axis=2)
    weight_in = input_weight.reshape(n_x, n_zl, part, 3, width)
    weight_out = output_weight.reshape(width, n_x, n_zl, part)
    proj = jnp.einsum(
        "xztf,xzfpc->ptc", whole_in, weight_in, preferred_element_type=F32
    ).astype(BF16)
    back = jnp.einsum(
        "xztf,cxzf->tc", whole_grad, weight_out, preferred_element_type=F32
    ).astype(BF16)
    common = (proj, back, taps)
    ext = pltpu.VMEM((3, rows + EDGE, width), F32)
    group = lax.axis_index("y")
    member = lax.axis_index("zh") * sizes["core"] + lax.axis_index("core")
    place = jnp.stack([group, member]).astype(jnp.int32)
    fwd, bwd, send = call(
        state_kernel,
        [shape(order, width), shape(order, width), shape(sizes["y"], order, width, dtype=BF16)],
        [ext],
        place,
        *common,
        rates,
        up,
        down,
    )
    conv, grad = call(
        local_kernel,
        [shape(rows, width), shape(rows, width)],
        [ext, pltpu.VMEM((2, rows + 8, width), F32)],
        *common,
        res,
        skip,
        filt,
        flops=3 * 10**9,
    )
    got = lax.all_to_all(send, "y", 0, 0, tiled=True)
    send = call(
        functools.partial(chain_kernel, block),
        shape(sizes["zh"] * sizes["core"], 2 * order, width, dtype=BF16),
        [],
        place,
        rates,
        fwd,
        bwd,
        got,
    )
    states = lax.all_to_all(send, ("zh", "core"), 0, 0, tiled=True)
    hidden, grad_proj = call(
        finish_kernel,
        [shape(block, width, dtype=BF16), shape(3, block, width, dtype=BF16)],
        [ext, pltpu.VMEM((3, rows, width), F32)],
        *common,
        res,
        up,
        down,
        conv,
        grad,
        states,
    )
    mixed = jnp.einsum("tc,cxzf->xztf", hidden, weight_out, preferred_element_type=F32)
    grad_tok = jnp.einsum("ptc,xzfpc->xztf", grad_proj, weight_in, preferred_element_type=F32)
    terms = jnp.concatenate([mixed.astype(BF16), grad_tok.astype(BF16)], axis=2)
    terms = lax.all_to_all(terms, "x", 0, 0, tiled=True)
    terms = jnp.sum(terms.astype(F32), axis=0).astype(BF16)
    terms = lax.all_to_all(terms, "zl", 0, 0, tiled=True)
    total = jnp.sum(terms.astype(F32), axis=0).astype(BF16)
    return total[:block], total[block:]


def solution(mesh, dims=(8, 4, 2, 4, 4)):
    fine = Mesh(mesh.devices.reshape(dims), CTX + TP)
    sizes = dict(zip(CTX + TP, dims))
    return jax.shard_map(
        functools.partial(shards, sizes),
        mesh=fine,
        in_specs=(
            P(CTX, TP),
            P(CTX, TP),
            P(None, None, TP),
            P(TP, None),
            P(None, TP, None),
            P(TP, None),
            P(TP, None),
            P(TP),
        ),
        out_specs=(P(CTX, TP), P(CTX, TP)),
        check_vma=False,
    )
```

```python
import functools

import jax
import jax.numpy as jnp
from jax import lax
from jax.experimental import pallas as pl
from jax.experimental.pallas import tpu as pltpu
from jax.sharding import Mesh
from jax.sharding import PartitionSpec as P

CTX = ("y", "zh", "core")
TP = ("x", "zl")
EDGE = 8
NEAR = 4
AHEAD = 2
GRANT = 16 * 2**20
BF16 = jnp.bfloat16
F32 = jnp.float32


def table_kernel(rates_ref, res_ref, up_ref, down_ref, filt_ref):
    order, rows, _ = up_ref.shape
    row = lax.broadcasted_iota(jnp.int32, (rows, 1), 0).astype(F32)
    span = rows - 8 + AHEAD
    total = jnp.zeros(filt_ref.shape, F32)
    for r in range(order):
        rate = rates_ref[r : r + 1, :]
        up = jnp.exp(-rate * (row + 1.0))
        up_ref[r] = up
        down_ref[r] = jnp.exp(-rate * (span - row))
        total = total + res_ref[r : r + 1, :] * up
    filt_ref[...] = total


def features(ext, proj_ref, taps_ref, rows):
    block = proj_ref.shape[1] - EDGE - 2 * NEAR
    out = []
    for p in range(3):
        proj = proj_ref[p].astype(F32)
        edge = proj[block : block + EDGE]
        near = proj[block + EDGE :]
        ext[p, :EDGE] = edge
        ext[p, EDGE : EDGE + block] = proj[:block]
        ext[p, EDGE + block :] = near
        total = taps_ref[p, 0:1, :] * ext[p, EDGE : EDGE + rows]
        for k in range(1, 3):
            total = total + taps_ref[p, k : k + 1, :] * ext[p, EDGE - k : EDGE - k + rows]
        out.append(total)
    return out


def back_rows(back_ref, rows):
    ends = EDGE + 2 * NEAR
    back = back_ref[...].astype(F32)
    near = pltpu.roll(back[EDGE:ends], NEAR, 0)
    row = lax.broadcasted_iota(jnp.int32, (rows, 1), 0)
    whole = jnp.concatenate([back[ends:], near], axis=0)
    return jnp.where(row < back_ref.shape[0] - ends + AHEAD, whole, 0.0), row


def state_kernel(
    place_ref, proj_ref, back_ref, taps_ref, rates_ref, up_ref, down_ref,
    fwd_ref, bwd_ref, send_ref, ext,
):
    order, rows, _ = up_ref.shape
    block = rows - 8
    query, key_part, value_part = features(ext, proj_ref, taps_ref, rows)
    back, row = back_rows(back_ref, rows)
    gated = jnp.where(row < block, key_part * value_part, 0.0)
    grad_conv = jnp.where(row >= AHEAD, back * query, 0.0)
    for r in range(order):
        scale = jnp.exp(rates_ref[r : r + 1, :] * (AHEAD + 1.0))
        fwd_ref[r : r + 1, :] = scale * jnp.sum(down_ref[r] * gated, axis=0, keepdims=True)
        bwd_ref[r : r + 1, :] = scale * jnp.sum(up_ref[r] * grad_conv, axis=0, keepdims=True)
    for i in range(send_ref.shape[0]):
        send_ref[i] = jnp.where(place_ref[0] < i, fwd_ref[...], bwd_ref[...]).astype(BF16)


def chain_kernel(block, place_ref, rates_ref, fwd_ref, bwd_ref, got_ref, send_ref):
    rates = rates_ref[...]
    order = rates.shape[0]
    groups, members = got_ref.shape[0], send_ref.shape[0]
    group, member = place_ref[0], place_ref[1]

    def fade(blocks):
        return jnp.exp(-rates * (block * jnp.maximum(blocks, 0)).astype(F32))

    fwd, bwd = fwd_ref[...], bwd_ref[...]
    before = jnp.zeros_like(fwd)
    after = jnp.zeros_like(bwd)
    for i in range(groups):
        got = got_ref[i].astype(F32)
        before = before + jnp.where(i < group, fade(members * (group - 1 - i)) * got, 0.0)
        after = after + jnp.where(i > group, fade(members * (i - 1 - group)) * got, 0.0)
    for i in range(members):
        ahead = fade(members - 1 + i - member) * before
        ahead = ahead + jnp.where(i > member, fade(i - member - 1) * fwd, 0.0)
        behind = fade(members - 1 + member - i) * after
        behind = behind + jnp.where(i < member, fade(member - i - 1) * bwd, 0.0)
        send_ref[i, :order] = ahead.astype(BF16)
        send_ref[i, order:] = behind.astype(BF16)


def local_kernel(
    proj_ref, back_ref, taps_ref, res_ref, skip_ref, filt_ref,
    conv_ref, grad_ref, ext, pad,
):
    rows, width = conv_ref.shape
    query, key_part, value_part = features(ext, proj_ref, taps_ref, rows)
    back, _ = back_rows(back_ref, rows)
    zero = jnp.zeros((8, width), F32)
    pad[0, :8] = zero
    pad[0, 8:] = key_part * value_part
    pad[1, :rows] = back * query
    pad[1, rows:] = zero
    direct = skip_ref[...] + jnp.sum(res_ref[...], axis=0, keepdims=True)
    for lane in range(0, width, 128):
        lanes = slice(lane, lane + 128)
        total = direct[:, lanes] * pad[0, 8:, lanes]
        for m in range(1, 9):
            moved = pad[0, 8 - m : 8 - m + rows, lanes]
            for q in range(0, rows, 8):
                tap = filt_ref[q + m - 1 : q + m, lanes]
                part = total[q:] + tap * moved[: rows - q]
                total = part if q == 0 else jnp.concatenate([total[:q], part], axis=0)
        conv_ref[:, lanes] = total
        total = direct[:, lanes] * pad[1, :rows, lanes]
        for m in range(1, 9):
            moved = pad[1, m : m + rows, lanes]
            for q in range(0, rows, 8):
                tap = filt_ref[q + m - 1 : q + m, lanes]
                part = total[: rows - q] + tap * moved[q:]
                total = part if q == 0 else jnp.concatenate([part, total[rows - q :]], axis=0)
        grad_ref[:, lanes] = total


def finish_kernel(
    proj_ref, back_ref, taps_ref, res_ref, up_ref, down_ref,
    conv_ref, grad_ref, got_ref,
    hidden_ref, out_ref, ext, feat,
):
    order, rows, _ = up_ref.shape
    block = rows - 8
    query, key_part, value_part = features(ext, proj_ref, taps_ref, rows)
    back, _ = back_rows(back_ref, rows)
    conv_out = conv_ref[...]
    grad_gated = grad_ref[...]
    states = jnp.sum(got_ref[...].astype(F32), axis=0)
    ahead, behind = states[:order], states[order:]
    for r in range(order):
        res = res_ref[r : r + 1, :]
        conv_out = conv_out + (res * ahead[r : r + 1]) * up_ref[r]
        grad_gated = grad_gated + (res * behind[r : r + 1]) * down_ref[r]
    hidden_ref[...] = (query * conv_out)[:block].astype(BF16)
    feat[0] = back * conv_out
    feat[1] = grad_gated * value_part
    feat[2] = grad_gated * key_part
    for p in range(3):
        total = taps_ref[p, 0:1, :] * feat[p, :block]
        for k in range(1, 3):
            total = total + taps_ref[p, k : k + 1, :] * feat[p, k : k + block]
        out_ref[p] = total.astype(BF16)


def call(kernel, outs, scratch, *args, flops=0):
    whole = pl.BlockSpec(memory_space=pltpu.VMEM)
    specs = [
        pl.BlockSpec(memory_space=pltpu.SMEM) if a.dtype == jnp.int32 else whole for a in args
    ]
    cost = pl.CostEstimate(flops=flops, bytes_accessed=0, transcendentals=0) if flops else None
    return pl.pallas_call(
        kernel,
        out_shape=outs,
        scratch_shapes=scratch,
        in_specs=specs,
        out_specs=jax.tree.map(lambda _: whole, outs),
        cost_estimate=cost,
        compiler_params=pltpu.CompilerParams(vmem_limit_bytes=GRANT),
    )(*args)


def project_kernel(counts, rows, first, index_ref, *refs):
    pieces, refs = refs[: len(counts)], refs[len(counts) :]
    weight_in, weight_out = refs[:2]
    old = refs[2] if not first else None
    total = refs[-2] if len(refs) == 5 else refs[-1]
    step = pl.program_id(0)

    @pl.when(step == 0)
    def _():
        total[...] = jnp.zeros_like(total) if first else old[...]

    start = 0
    for piece, count in zip(pieces, counts):

        @pl.when((step >= start) & (step < start + count))
        def _(piece=piece, start=start):
            part = piece[step - start]
            for p in range(3):
                total[p] += jnp.dot(part[:rows], weight_in[p], preferred_element_type=F32)
            total[3] += lax.dot_general(
                part[-rows:], weight_out[...], (((1,), (1,)), ((), ())), preferred_element_type=F32
            )

        start += count


def project_last_kernel(counts, rows, index_ref, *refs):
    out, total = refs[-2:]
    project_kernel(counts, rows, False, index_ref, *refs[:-2], total)

    @pl.when(pl.program_id(0) == sum(counts) - 1)
    def _():
        out[...] = total[...].astype(BF16)


def project(index, pieces, weight_in, weight_out, rows, old=None, last=False):
    counts = [piece.shape[0] for piece in pieces]
    width = weight_out.shape[0]
    part = pieces[0].shape[2]
    whole = pl.BlockSpec(memory_space=pltpu.VMEM)
    if last:
        kernel = functools.partial(project_last_kernel, counts, rows)
    else:
        kernel = functools.partial(project_kernel, counts, rows, old is None)
    return pl.pallas_call(
        kernel,
        grid_spec=pltpu.PrefetchScalarGridSpec(
            num_scalar_prefetch=1,
            grid=(sum(counts),),
            in_specs=[whole] * len(pieces)
            + [
                pl.BlockSpec((3, part, width), lambda s, index: (0, index[s], 0)),
                pl.BlockSpec((width, part), lambda s, index: (0, index[s])),
            ]
            + [whole] * (old is not None),
            out_specs=whole,
            scratch_shapes=[pltpu.VMEM((4, rows, width), F32)] if last else [],
        ),
        out_shape=shape(4, rows, width, dtype=BF16 if last else F32),
        cost_estimate=pl.CostEstimate(
            flops=8 * sum(counts) * rows * part * width,
            bytes_accessed=8 * sum(counts) * part * width,
            transcendentals=0,
        ),
        compiler_params=pltpu.CompilerParams(vmem_limit_bytes=GRANT),
    )(index, *pieces, weight_in, weight_out, *([] if old is None else [old]))


def partials_kernel(index_ref, hidden, grad, weight_in, weight_out, out):
    block = hidden.shape[0]
    mixed = jnp.dot(hidden[...], weight_out[...], preferred_element_type=F32)
    out[0, :block] = mixed.astype(BF16)
    total = jnp.zeros_like(mixed)
    for p in range(3):
        total = total + lax.dot_general(
            grad[p], weight_in[p], (((1,), (1,)), ((), ())), preferred_element_type=F32
        )
    out[0, block:] = total.astype(BF16)


def partials(index, count, hidden, grad, weight_in, weight_out, part):
    block, width = hidden.shape
    whole = pl.BlockSpec(memory_space=pltpu.VMEM)
    return pl.pallas_call(
        partials_kernel,
        grid_spec=pltpu.PrefetchScalarGridSpec(
            num_scalar_prefetch=1,
            grid=(count,),
            in_specs=[
                whole,
                whole,
                pl.BlockSpec((3, part, width), lambda s, index: (0, index[s], 0)),
                pl.BlockSpec((width, part), lambda s, index: (0, index[s])),
            ],
            out_specs=pl.BlockSpec((1, 2 * block, part), lambda s, index: (s, 0, 0)),
        ),
        out_shape=shape(count, 2 * block, part, dtype=BF16),
        cost_estimate=pl.CostEstimate(
            flops=8 * count * block * part * width,
            bytes_accessed=8 * count * part * width,
            transcendentals=0,
        ),
        compiler_params=pltpu.CompilerParams(vmem_limit_bytes=GRANT),
    )(index, hidden, grad, weight_in, weight_out)


def shape(*dims, dtype=F32):
    return jax.ShapeDtypeStruct(dims, dtype)


def spread(array, axis, count):
    copies = jnp.broadcast_to(array[None], (count,) + array.shape)
    return lax.all_to_all(copies, axis, 0, 0, tiled=True)


def shards(
    sizes,
    tokens,
    cotangent,
    input_weight,
    output_weight,
    short_taps,
    residues,
    decay_rates,
    skip_gain,
):
    n_x, n_zl = sizes["x"], sizes["zl"]
    n_ctx = sizes["y"] * sizes["zh"] * sizes["core"]
    block, part = tokens.shape
    width = output_weight.shape[0]
    order = residues.shape[1]
    rows = block + 8
    taps = short_taps.transpose(0, 2, 1)
    rates = decay_rates.T
    res = residues.T
    skip = skip_gain[None]
    up, down, filt = call(
        table_kernel,
        [shape(order, rows, width), shape(order, rows, width), shape(rows, width)],
        [],
        rates,
        res,
    )
    to_next = [(i, i + 1) for i in range(n_ctx - 1)]
    to_prev = [(i + 1, i) for i in range(n_ctx - 1)]
    edge = lax.ppermute(tokens[block - EDGE :], CTX, to_next)
    near = jnp.concatenate([tokens[:NEAR], cotangent[:NEAR]], axis=0)
    near = lax.ppermute(near, CTX, to_prev)
    both = jnp.concatenate([tokens, edge, near, cotangent], axis=0)
    near_pieces = spread(both, "zl", n_zl)
    half = n_zl // 2
    right = [(i, (i + 1) % n_x) for i in range(n_x)]
    left = [(i, (i - 1) % n_x) for i in range(n_x)]
    from_left = lax.ppermute(near_pieces, "x", right)
    from_right = lax.ppermute(near_pieces, "x", left)
    far_left = lax.ppermute(from_left[:half], "x", right)
    far_right = lax.ppermute(from_right[half:], "x", left)
    x = lax.axis_index("x")
    own, after, far, before = (
        (lax.rem(x + k, n_x) * n_zl + jnp.arange(n_zl)).astype(jnp.int32) for k in range(n_x)
    )
    weight_in = input_weight.transpose(1, 0, 2)
    weights = (weight_in, output_weight, block + EDGE + 2 * NEAR)
    total = project(own, [near_pieces], *weights)
    total = project(
        jnp.concatenate([before, after]), [from_left, from_right], *weights, old=total
    )
    total = project(far, [far_left, far_right], *weights, old=total, last=True)
    proj, back = total[:3], total[3]
    common = (proj, back, taps)
    ext = pltpu.VMEM((3, rows + EDGE, width), F32)
    group = lax.axis_index("y")
    member = lax.axis_index("zh") * sizes["core"] + lax.axis_index("core")
    place = jnp.stack([group, member]).astype(jnp.int32)
    fwd, bwd, send = call(
        state_kernel,
        [shape(order, width), shape(order, width), shape(sizes["y"], order, width, dtype=BF16)],
        [ext],
        place,
        *common,
        rates,
        up,
        down,
    )
    conv, grad = call(
        local_kernel,
        [shape(rows, width), shape(rows, width)],
        [ext, pltpu.VMEM((2, rows + 8, width), F32)],
        *common,
        res,
        skip,
        filt,
        flops=3 * 10**9,
    )
    got = lax.all_to_all(send, "y", 0, 0, tiled=True)
    send = call(
        functools.partial(chain_kernel, block),
        shape(sizes["zh"] * sizes["core"], 2 * order, width, dtype=BF16),
        [],
        place,
        rates,
        fwd,
        bwd,
        got,
    )
    states = lax.all_to_all(send, ("zh", "core"), 0, 0, tiled=True)
    hidden, grad_proj = call(
        finish_kernel,
        [shape(block, width, dtype=BF16), shape(3, block, width, dtype=BF16)],
        [ext, pltpu.VMEM((3, rows, width), F32)],
        *common,
        res,
        up,
        down,
        conv,
        grad,
        states,
    )
    def terms(index):
        return partials(
            index, index.shape[0], hidden, grad_proj, weight_in, output_weight, part
        )

    def add(*arrays):
        return sum(a.astype(F32) for a in arrays).astype(BF16)

    far_right = lax.ppermute(terms(far[:half]), "x", right)
    far_left = lax.ppermute(terms(far[half:]), "x", left)
    to_right = terms(after)
    to_left = terms(before)
    to_right = jnp.concatenate([add(to_right[:half], far_right), to_right[half:]], axis=0)
    to_left = jnp.concatenate([to_left[:half], add(to_left[half:], far_left)], axis=0)
    from_left = lax.ppermute(to_right, "x", right)
    from_right = lax.ppermute(to_left, "x", left)
    summed = add(terms(own), from_left, from_right)
    summed = lax.all_to_all(summed, "zl", 0, 0, tiled=True)
    total = jnp.sum(summed.astype(F32), axis=0).astype(BF16)
    return total[:block], total[block:]


def solution(mesh, dims=(8, 4, 2, 4, 4)):
    fine = Mesh(mesh.devices.reshape(dims), CTX + TP)
    sizes = dict(zip(CTX + TP, dims))
    return jax.shard_map(
        functools.partial(shards, sizes),
        mesh=fine,
        in_specs=(
            P(CTX, TP),
            P(CTX, TP),
            P(None, None, TP),
            P(TP, None),
            P(None, TP, None),
            P(TP, None),
            P(TP, None),
            P(TP),
        ),
        out_specs=(P(CTX, TP), P(CTX, TP)),
        check_vma=False,
    )
```

```python
import functools

import jax
import jax.numpy as jnp
from jax import lax
from jax.experimental import pallas as pl
from jax.experimental.pallas import tpu as pltpu
from jax.sharding import Mesh
from jax.sharding import PartitionSpec as P

CTX = ("y", "zh", "core")
TP = ("x", "zl")
EDGE = 8
NEAR = 4
AHEAD = 2
GRANT = 16 * 2**20
BF16 = jnp.bfloat16
F32 = jnp.float32


def edge_kernel(tokens, cotangent, copies, edge, near):
    block = tokens.shape[0]
    for i in range(copies.shape[0]):
        copies[i, :block] = tokens[...]
        copies[i, block:] = cotangent[...]
    edge[...] = tokens[block - 2 * EDGE :]
    ours = tokens[: 2 * EDGE].astype(F32)
    other = pltpu.roll(cotangent[: 2 * EDGE].astype(F32), NEAR, 0)
    row = lax.broadcasted_iota(jnp.int32, ours.shape, 0)
    near[...] = jnp.where(row < NEAR, ours, other).astype(BF16)


def halo_kernel(edge, near, copies):
    both = jnp.concatenate([edge[...].astype(F32)[EDGE:], near[...].astype(F32)[:EDGE]], axis=0)
    for i in range(copies.shape[0]):
        copies[i] = both.astype(BF16)


def features(ext, proj_ref, taps_ref, rows):
    block = proj_ref.shape[1] - EDGE - 2 * NEAR
    out = []
    for p in range(3):
        proj = proj_ref[p].astype(F32)
        edge = proj[block : block + EDGE]
        near = proj[block + EDGE :]
        ext[p, :EDGE] = edge
        ext[p, EDGE : EDGE + block] = proj[:block]
        ext[p, EDGE + block :] = near
        total = taps_ref[p, 0:1, :] * ext[p, EDGE : EDGE + rows]
        for k in range(1, 3):
            total = total + taps_ref[p, k : k + 1, :] * ext[p, EDGE - k : EDGE - k + rows]
        out.append(total)
    return out


def back_rows(back_ref, rows):
    ends = EDGE + 2 * NEAR
    back = back_ref[...].astype(F32)
    near = pltpu.roll(back[EDGE:ends], NEAR, 0)
    row = lax.broadcasted_iota(jnp.int32, (rows, 1), 0)
    whole = jnp.concatenate([back[ends:], near], axis=0)
    return jnp.where(row < back_ref.shape[0] - ends + AHEAD, whole, 0.0), row


def state_kernel(
    place_ref, proj_ref, back_ref, taps_ref, rates_ref,
    fwd_ref, bwd_ref, send_ref, ext,
):
    order = rates_ref.shape[0]
    block = proj_ref.shape[1] - EDGE - 2 * NEAR
    rows = block + 8
    query, key_part, value_part = features(ext, proj_ref, taps_ref, rows)
    back, row = back_rows(back_ref, rows)
    gated = jnp.where(row < block, key_part * value_part, 0.0)
    grad_conv = jnp.where(row >= AHEAD, back * query, 0.0)
    time = row.astype(F32)
    for r in range(order):
        rate = rates_ref[r : r + 1, :]
        fwd = jnp.exp(-rate * (block - 1.0 - time)) * gated
        bwd = jnp.exp(-rate * (time - AHEAD)) * grad_conv
        fwd_ref[r : r + 1, :] = jnp.sum(fwd, axis=0, keepdims=True)
        bwd_ref[r : r + 1, :] = jnp.sum(bwd, axis=0, keepdims=True)
    for i in range(send_ref.shape[0]):
        send_ref[i] = jnp.where(place_ref[0] < i, fwd_ref[...], bwd_ref[...]).astype(BF16)


def chain_kernel(block, place_ref, rates_ref, fwd_ref, bwd_ref, got_ref, send_ref):
    rates = rates_ref[...]
    order = rates.shape[0]
    groups, members = got_ref.shape[0], send_ref.shape[0]
    group, member = place_ref[0], place_ref[1]

    def fade(blocks):
        return jnp.exp(-rates * (block * jnp.maximum(blocks, 0)).astype(F32))

    fwd, bwd = fwd_ref[...], bwd_ref[...]
    before = jnp.zeros_like(fwd)
    after = jnp.zeros_like(bwd)
    for i in range(groups):
        got = got_ref[i].astype(F32)
        before = before + jnp.where(i < group, fade(members * (group - 1 - i)) * got, 0.0)
        after = after + jnp.where(i > group, fade(members * (i - 1 - group)) * got, 0.0)
    for i in range(members):
        ahead = fade(members - 1 + i - member) * before
        ahead = ahead + jnp.where(i > member, fade(i - member - 1) * fwd, 0.0)
        behind = fade(members - 1 + member - i) * after
        behind = behind + jnp.where(i < member, fade(member - i - 1) * bwd, 0.0)
        send_ref[i, :order] = ahead.astype(BF16)
        send_ref[i, order:] = behind.astype(BF16)


def local_kernel(
    proj_ref, back_ref, taps_ref, rates_ref, res_ref, skip_ref,
    conv_ref, grad_ref, ext, pad, filt_ref,
):
    rows, width = conv_ref.shape
    time = lax.broadcasted_iota(jnp.int32, (rows, 1), 0).astype(F32)
    taps = jnp.zeros((rows, width), F32)
    for r in range(rates_ref.shape[0]):
        taps = taps + res_ref[r : r + 1, :] * jnp.exp(-rates_ref[r : r + 1, :] * (time + 1.0))
    filt_ref[...] = taps
    query, key_part, value_part = features(ext, proj_ref, taps_ref, rows)
    back, _ = back_rows(back_ref, rows)
    zero = jnp.zeros((8, width), F32)
    pad[0, :8] = zero
    pad[0, 8:] = key_part * value_part
    pad[1, :rows] = back * query
    pad[1, rows:] = zero
    direct = skip_ref[...] + jnp.sum(res_ref[...], axis=0, keepdims=True)
    for lane in range(0, width, 128):
        lanes = slice(lane, lane + 128)
        total = direct[:, lanes] * pad[0, 8:, lanes]
        for m in range(1, 9):
            moved = pad[0, 8 - m : 8 - m + rows, lanes]
            for q in range(0, rows, 8):
                tap = filt_ref[q + m - 1 : q + m, lanes]
                part = total[q:] + tap * moved[: rows - q]
                total = part if q == 0 else jnp.concatenate([total[:q], part], axis=0)
        conv_ref[:, lanes] = total
        total = direct[:, lanes] * pad[1, :rows, lanes]
        for m in range(1, 9):
            moved = pad[1, m : m + rows, lanes]
            for q in range(0, rows, 8):
                tap = filt_ref[q + m - 1 : q + m, lanes]
                part = total[: rows - q] + tap * moved[q:]
                total = part if q == 0 else jnp.concatenate([part, total[rows - q :]], axis=0)
        grad_ref[:, lanes] = total


def finish_kernel(
    proj_ref, back_ref, taps_ref, rates_ref, res_ref,
    conv_ref, grad_ref, got_ref,
    hidden_ref, out_ref, ext, feat,
):
    order = rates_ref.shape[0]
    rows = conv_ref.shape[0]
    block = rows - 8
    query, key_part, value_part = features(ext, proj_ref, taps_ref, rows)
    back, row = back_rows(back_ref, rows)
    time = row.astype(F32)
    conv_out = conv_ref[...]
    grad_gated = grad_ref[...]
    states = jnp.sum(got_ref[...].astype(F32), axis=0)
    ahead, behind = states[:order], states[order:]
    for r in range(order):
        res = res_ref[r : r + 1, :]
        rate = rates_ref[r : r + 1, :]
        conv_out = conv_out + (res * ahead[r : r + 1]) * jnp.exp(-rate * (time + 1.0))
        past = jnp.exp(-rate * (block + AHEAD - time))
        grad_gated = grad_gated + (res * behind[r : r + 1]) * past
    hidden_ref[...] = (query * conv_out)[:block].astype(BF16)
    feat[0] = back * conv_out
    feat[1] = grad_gated * value_part
    feat[2] = grad_gated * key_part
    for p in range(3):
        total = taps_ref[p, 0:1, :] * feat[p, :block]
        for k in range(1, 3):
            total = total + taps_ref[p, k : k + 1, :] * feat[p, k : k + block]
        out_ref[p] = total.astype(BF16)


def call(kernel, outs, scratch, *args, flops=0):
    whole = pl.BlockSpec(memory_space=pltpu.VMEM)
    specs = [
        pl.BlockSpec(memory_space=pltpu.SMEM) if a.dtype == jnp.int32 else whole for a in args
    ]
    cost = pl.CostEstimate(flops=flops, bytes_accessed=0, transcendentals=0) if flops else None
    return pl.pallas_call(
        kernel,
        out_shape=outs,
        scratch_shapes=scratch,
        in_specs=specs,
        out_specs=jax.tree.map(lambda _: whole, outs),
        cost_estimate=cost,
        compiler_params=pltpu.CompilerParams(vmem_limit_bytes=GRANT),
    )(*args)


def load_weights(blocks, weight_in, weight_out, held_in, held_out, sems):
    part = held_in.shape[2]
    copies = []
    for s, block in enumerate(blocks):
        at = pl.ds(pl.multiple_of(block * part, part), part)
        copies.append(
            (
                pltpu.make_async_copy(weight_in.at[:, at, :], held_in.at[s], sems.at[s, 0]),
                pltpu.make_async_copy(weight_out.at[:, at], held_out.at[s], sems.at[s, 1]),
            )
        )
        for copy in copies[-1]:
            copy.start()

    def ready(s):
        for copy in copies[s]:
            copy.wait()

    return ready


def project_kernel(sizes, offsets, first, last, place_ref, *refs):
    n_x, n_zl = sizes["x"], sizes["zl"]
    pieces, refs = refs[: len(offsets)], refs[len(offsets) :]
    halo, weight_in, weight_out = refs[:3]
    old = None if first else refs[3]
    out, held_in, held_out, sems = refs[3 + (not first) : 7 + (not first)]
    total = refs[-1] if last else out
    block = pieces[0].shape[1] // 2
    work = [
        (piece, j, lax.rem(place_ref[2] + k, n_x) * n_zl + start + j)
        for piece, (k, start) in zip(pieces, offsets)
        for j in range(piece.shape[0])
    ]
    ready = load_weights([w[2] for w in work], weight_in, weight_out, held_in, held_out, sems)
    for s, (piece, j, index) in enumerate(work):
        ready(s)
        ends = halo[index]
        part_in = jnp.concatenate([piece[j, :block], ends], axis=0)
        part_grad = jnp.concatenate([ends, piece[j, block:]], axis=0)
        for p in range(4):
            if p < 3:
                term = jnp.dot(part_in, held_in[s, p], preferred_element_type=F32)
            else:
                term = lax.dot_general(
                    part_grad,
                    held_out[s],
                    (((1,), (1,)), ((), ())),
                    preferred_element_type=F32,
                )
            if s == 0 and first:
                total[p] = term
            else:
                total[p] = (old if s == 0 else total)[p] + term
    if last:
        out[...] = total[...].astype(BF16)


def project(sizes, place, offsets, pieces, halo, weights, old=None, last=False):
    weight_in, weight_out = weights
    count = sum(piece.shape[0] for piece in pieces)
    rows = pieces[0].shape[1] // 2 + halo.shape[1]
    part = pieces[0].shape[2]
    width = weight_out.shape[0]
    whole = pl.BlockSpec(memory_space=pltpu.VMEM)
    far = pl.BlockSpec(memory_space=pltpu.HBM)
    scratch = [
        pltpu.VMEM((count, 3, part, width), BF16),
        pltpu.VMEM((count, width, part), BF16),
        pltpu.SemaphoreType.DMA((count, 2)),
    ]
    return pl.pallas_call(
        functools.partial(project_kernel, sizes, offsets, old is None, last),
        in_specs=[pl.BlockSpec(memory_space=pltpu.SMEM)]
        + [whole] * (len(pieces) + 1)
        + [far, far]
        + [whole] * (old is not None),
        out_specs=whole,
        scratch_shapes=scratch + ([pltpu.VMEM((4, rows, width), F32)] if last else []),
        out_shape=shape(4, rows, width, dtype=BF16 if last else F32),
        cost_estimate=pl.CostEstimate(
            flops=8 * count * rows * part * width,
            bytes_accessed=8 * count * part * width,
            transcendentals=0,
        ),
        compiler_params=pltpu.CompilerParams(vmem_limit_bytes=GRANT),
    )(place, *pieces, halo, weight_in, weight_out, *([] if old is None else [old]))


def partials_kernel(
    sizes, offset, place_ref, hidden, grad, weight_in, weight_out, out, held_in, held_out, sems
):
    n_x, n_zl = sizes["x"], sizes["zl"]
    block = hidden.shape[0]
    k, start = offset
    base = lax.rem(place_ref[2] + k, n_x) * n_zl + start
    count = out.shape[0]
    ready = load_weights(
        [base + j for j in range(count)], weight_in, weight_out, held_in, held_out, sems
    )
    for s in range(count):
        ready(s)
        mixed = jnp.dot(hidden[...], held_out[s], preferred_element_type=F32)
        out[s, :block] = mixed.astype(BF16)
        total = None
        for p in range(3):
            term = lax.dot_general(
                grad[p], held_in[s, p], (((1,), (1,)), ((), ())), preferred_element_type=F32
            )
            total = term if p == 0 else total + term
        out[s, block:] = total.astype(BF16)


def partials(sizes, place, offset, count, hidden, grad, weights, part):
    block, width = hidden.shape
    whole = pl.BlockSpec(memory_space=pltpu.VMEM)
    far = pl.BlockSpec(memory_space=pltpu.HBM)
    return pl.pallas_call(
        functools.partial(partials_kernel, sizes, offset),
        in_specs=[pl.BlockSpec(memory_space=pltpu.SMEM), whole, whole, far, far],
        out_specs=whole,
        scratch_shapes=[
            pltpu.VMEM((count, 3, part, width), BF16),
            pltpu.VMEM((count, width, part), BF16),
            pltpu.SemaphoreType.DMA((count, 2)),
        ],
        out_shape=shape(count, 2 * block, part, dtype=BF16),
        cost_estimate=pl.CostEstimate(
            flops=8 * count * block * part * width,
            bytes_accessed=8 * count * part * width,
            transcendentals=0,
        ),
        compiler_params=pltpu.CompilerParams(vmem_limit_bytes=GRANT),
    )(place, hidden, grad, *weights)


def shape(*dims, dtype=F32):
    return jax.ShapeDtypeStruct(dims, dtype)


def shards(
    sizes,
    tokens,
    cotangent,
    input_weight,
    output_weight,
    short_taps,
    residues,
    decay_rates,
    skip_gain,
):
    n_x, n_zl = sizes["x"], sizes["zl"]
    n_ctx = sizes["y"] * sizes["zh"] * sizes["core"]
    block, part = tokens.shape
    width = output_weight.shape[0]
    order = residues.shape[1]
    rows = block + 8
    taps = short_taps.transpose(0, 2, 1)
    rates = decay_rates.T
    res = residues.T
    skip = skip_gain[None]
    place = jnp.stack(
        [
            lax.axis_index("y"),
            lax.axis_index("zh") * sizes["core"] + lax.axis_index("core"),
            lax.axis_index("x"),
        ]
    ).astype(jnp.int32)
    to_next = [(i, i + 1) for i in range(n_ctx - 1)]
    to_prev = [(i + 1, i) for i in range(n_ctx - 1)]
    copies, edge, near = call(
        edge_kernel,
        [
            shape(n_zl, 2 * block, part, dtype=BF16),
            shape(2 * EDGE, part, dtype=BF16),
            shape(2 * EDGE, part, dtype=BF16),
        ],
        [],
        tokens,
        cotangent,
    )
    edge = lax.ppermute(edge, CTX, to_next)
    near = lax.ppermute(near, CTX, to_prev)
    pieces = lax.all_to_all(copies, "zl", 0, 0, tiled=True)
    ends = call(halo_kernel, shape(n_x * n_zl, 2 * EDGE, part, dtype=BF16), [], edge, near)
    ends, _ = lax.optimization_barrier((ends, pieces))
    halo = lax.all_to_all(ends, TP, 0, 0, tiled=True)
    half = n_zl // 2
    right = [(i, (i + 1) % n_x) for i in range(n_x)]
    left = [(i, (i - 1) % n_x) for i in range(n_x)]
    from_left = lax.ppermute(pieces, "x", right)
    from_right = lax.ppermute(pieces, "x", left)
    far_left = lax.ppermute(from_left[:half], "x", right)
    far_right = lax.ppermute(from_right[half:], "x", left)
    weights = (input_weight.transpose(1, 0, 2), output_weight)
    total = project(sizes, place, [(0, 0)], [pieces], halo, weights)
    total = project(
        sizes, place, [(n_x - 1, 0), (1, 0)], [from_left, from_right], halo, weights, total
    )
    total = project(
        sizes, place, [(2, 0), (2, half)], [far_left, far_right], halo, weights, total, True
    )
    proj, back = total[:3], total[3]
    common = (proj, back, taps, rates)
    ext = pltpu.VMEM((3, rows + EDGE, width), F32)
    fwd, bwd, send = call(
        state_kernel,
        [shape(order, width), shape(order, width), shape(sizes["y"], order, width, dtype=BF16)],
        [ext],
        place,
        *common,
    )
    conv, grad = call(
        local_kernel,
        [shape(rows, width), shape(rows, width)],
        [ext, pltpu.VMEM((2, rows + 8, width), F32), pltpu.VMEM((rows, width), F32)],
        *common,
        res,
        skip,
        flops=3 * 10**9,
    )
    got = lax.all_to_all(send, "y", 0, 0, tiled=True)
    send = call(
        functools.partial(chain_kernel, block),
        shape(sizes["zh"] * sizes["core"], 2 * order, width, dtype=BF16),
        [],
        place,
        rates,
        fwd,
        bwd,
        got,
    )
    states = lax.all_to_all(send, ("zh", "core"), 0, 0, tiled=True)
    hidden, grad_proj = call(
        finish_kernel,
        [shape(block, width, dtype=BF16), shape(3, block, width, dtype=BF16)],
        [ext, pltpu.VMEM((3, rows, width), F32)],
        *common,
        res,
        conv,
        grad,
        states,
    )
    def terms(offset, count):
        return partials(sizes, place, offset, count, hidden, grad_proj, weights, part)

    def add(*arrays):
        return sum(a.astype(F32) for a in arrays).astype(BF16)

    far_right = lax.ppermute(terms((2, 0), half), "x", right)
    far_left = lax.ppermute(terms((2, half), half), "x", left)
    to_right = terms((1, 0), n_zl)
    to_left = terms((n_x - 1, 0), n_zl)
    to_right = jnp.concatenate([add(to_right[:half], far_right), to_right[half:]], axis=0)
    to_left = jnp.concatenate([to_left[:half], add(to_left[half:], far_left)], axis=0)
    from_left = lax.ppermute(to_right, "x", right)
    from_right = lax.ppermute(to_left, "x", left)
    summed = add(terms((0, 0), n_zl), from_left, from_right)
    summed = lax.all_to_all(summed, "zl", 0, 0, tiled=True)
    total = jnp.sum(summed.astype(F32), axis=0).astype(BF16)
    return total[:block], total[block:]


def solution(mesh, dims=(8, 4, 2, 4, 4)):
    fine = Mesh(mesh.devices.reshape(dims), CTX + TP)
    sizes = dict(zip(CTX + TP, dims))
    return jax.shard_map(
        functools.partial(shards, sizes),
        mesh=fine,
        in_specs=(
            P(CTX, TP),
            P(CTX, TP),
            P(None, None, TP),
            P(TP, None),
            P(None, TP, None),
            P(TP, None),
            P(TP, None),
            P(TP),
        ),
        out_specs=(P(CTX, TP), P(CTX, TP)),
        check_vma=False,
    )
```

```python
import functools

import jax
import jax.numpy as jnp
from jax import lax
from jax.experimental import pallas as pl
from jax.experimental.pallas import tpu as pltpu
from jax.sharding import Mesh
from jax.sharding import PartitionSpec as P

CTX = ("y", "zh", "core")
TP = ("x", "zl")
TILE = 8
AHEAD = 2
GRANT = 16 * 2**20
BF16 = jnp.bfloat16
F32 = jnp.float32


def copy_kernel(tokens, cotangent, copies):
    block = tokens.shape[0]
    for i in range(copies.shape[0]):
        copies[i, :block] = tokens[...]
        copies[i, block:] = cotangent[...]


def features(ext, proj_ref, taps_ref, rows, last=None, first=None):
    block, width = proj_ref.shape[1:]
    zero = jnp.zeros((TILE, width), F32)
    out = []
    for p in range(3):
        ext[p, :TILE] = zero
        ext[p, TILE : TILE + block] = proj_ref[p].astype(F32)
        ext[p, TILE + block :] = zero
        if last is not None:
            ext[p, TILE - AHEAD : TILE] = last[AHEAD * p : AHEAD * (p + 1)]
            ext[p, TILE + block : TILE + block + AHEAD] = first[AHEAD * p : AHEAD * (p + 1)]
        total = taps_ref[p, 0:1, :] * ext[p, TILE : TILE + rows]
        for k in range(1, 3):
            total = total + taps_ref[p, k : k + 1, :] * ext[p, TILE - k : TILE - k + rows]
        out.append(total)
    return out


def inner_rows(ext, proj_ref, taps_ref, rows):
    block, width = proj_ref.shape[1:]
    query, key_part, value_part = features(ext, proj_ref, taps_ref, rows)
    row = lax.broadcasted_iota(jnp.int32, (rows, 1), 0)
    inside = (row >= AHEAD) & (row < block)
    back = jnp.concatenate([proj_ref[3].astype(F32), jnp.zeros((TILE, width), F32)], axis=0)
    gated = jnp.where(inside, key_part * value_part, 0.0)
    return gated, jnp.where(inside, back * query, 0.0), row.astype(F32)


def state_kernel(proj_ref, taps_ref, rates_ref, send_ref, ext, pack):
    order = rates_ref.shape[0]
    block = proj_ref.shape[1]
    gated, grad_conv, time = inner_rows(ext, proj_ref, taps_ref, block + TILE)
    for r in range(order):
        rate = rates_ref[r : r + 1, :]
        fwd = jnp.exp(-rate * (block - 1.0 - time)) * gated
        bwd = jnp.exp(-rate * (time - AHEAD)) * grad_conv
        pack[r : r + 1] = jnp.sum(fwd, axis=0, keepdims=True)
        pack[order + r : order + r + 1] = jnp.sum(bwd, axis=0, keepdims=True)
    at = 2 * order
    pack[at + TILE :] = jnp.zeros((TILE, pack.shape[1]), F32)
    for p in range(4):
        rows = proj_ref[p].astype(F32)
        pack[at + AHEAD * p : at + AHEAD * (p + 1)] = rows[:AHEAD]
        if p < 3:
            ends = at + TILE + AHEAD * p
            pack[ends : ends + AHEAD] = rows[block - AHEAD :]
    for i in range(send_ref.shape[0]):
        send_ref[i] = pack[...].astype(BF16)


def joint(taps_ref, first, last):
    row = []
    for p in range(3):
        a, b = first[AHEAD * p : AHEAD * p + 1], first[AHEAD * p + 1 : AHEAD * p + 2]
        c, d = last[AHEAD * p : AHEAD * p + 1], last[AHEAD * p + 1 : AHEAD * p + 2]
        t = [taps_ref[p, k : k + 1, :] for k in range(3)]
        row.append((t[0] * a + t[1] * d + t[2] * c, t[0] * b + t[1] * a + t[2] * d))
    back = (first[3 * AHEAD : 3 * AHEAD + 1], first[3 * AHEAD + 1 : 3 * AHEAD + 2])
    gated = tuple(row[1][i] * row[2][i] for i in range(AHEAD))
    return gated, tuple(back[i] * row[0][i] for i in range(AHEAD))


def fader(rates, block):
    def fade(blocks):
        if isinstance(blocks, int):
            return jnp.exp(-rates * float(block * blocks))
        return jnp.exp(-rates * (block * jnp.maximum(blocks, 0)).astype(F32))

    return fade


def group_states(block, taps_ref, rates, got_ref):
    order = rates.shape[0]
    members = got_ref.shape[0]
    fwd, bwd, firsts, lasts = [], [], [], []
    for j in range(members):
        got = got_ref[j].astype(F32)
        fwd.append(got[:order])
        bwd.append(got[order : 2 * order])
        firsts.append(got[2 * order : 2 * order + TILE])
        lasts.append(got[2 * order + TILE :])
    near, far = jnp.exp(-rates * (block - 2.0)), jnp.exp(-rates * (block - 1.0))
    for j in range(1, members):
        gated, grad_conv = joint(taps_ref, firsts[j], lasts[j - 1])
        fwd[j] = fwd[j] + far * gated[0] + near * gated[1]
        bwd[j - 1] = bwd[j - 1] + near * grad_conv[0] + far * grad_conv[1]
    return fwd, bwd, firsts, lasts, near, far


def chain_kernel(block, place_ref, taps_ref, rates_ref, got_ref, send_ref):
    rates = rates_ref[...]
    order = rates.shape[0]
    fade = fader(rates, block)
    fwd, bwd, firsts, lasts, _, _ = group_states(block, taps_ref, rates, got_ref)
    members = len(fwd)
    total_fwd = sum(fade(members - 1 - j) * fwd[j] for j in range(members))
    total_bwd = sum(fade(j) * bwd[j] for j in range(members))
    ends = jnp.concatenate([firsts[0], lasts[-1]], axis=0).astype(BF16)
    for i in range(send_ref.shape[0]):
        send_ref[i, :order] = jnp.where(place_ref[0] < i, total_fwd, total_bwd).astype(BF16)
        send_ref[i, order:] = ends


def local_kernel(
    proj_ref, taps_ref, rates_ref, res_ref, skip_ref, conv_ref, grad_ref, ext, pad, filt_ref
):
    rows, width = conv_ref.shape
    gated, grad_conv, time = inner_rows(ext, proj_ref, taps_ref, rows)
    taps = jnp.zeros((rows, width), F32)
    for r in range(rates_ref.shape[0]):
        taps = taps + res_ref[r : r + 1, :] * jnp.exp(-rates_ref[r : r + 1, :] * (time + 1.0))
    filt_ref[...] = taps
    zero = jnp.zeros((TILE, width), F32)
    pad[0, :TILE] = zero
    pad[0, TILE:] = gated
    pad[1, :rows] = grad_conv
    pad[1, rows:] = zero
    direct = skip_ref[...] + jnp.sum(res_ref[...], axis=0, keepdims=True)
    for lane in range(0, width, 128):
        lanes = slice(lane, lane + 128)
        total = direct[:, lanes] * pad[0, TILE:, lanes]
        for m in range(1, TILE + 1):
            moved = pad[0, TILE - m : TILE - m + rows, lanes]
            for q in range(0, rows, TILE):
                tap = filt_ref[q + m - 1 : q + m, lanes]
                part = total[q:] + tap * moved[: rows - q]
                total = part if q == 0 else jnp.concatenate([total[:q], part], axis=0)
        conv_ref[:, lanes] = total
        total = direct[:, lanes] * pad[1, :rows, lanes]
        for m in range(1, TILE + 1):
            moved = pad[1, m : m + rows, lanes]
            for q in range(0, rows, TILE):
                tap = filt_ref[q + m - 1 : q + m, lanes]
                part = total[: rows - q] + tap * moved[q:]
                total = part if q == 0 else jnp.concatenate([part, total[rows - q :]], axis=0)
        grad_ref[:, lanes] = total


def finish_kernel(
    place_ref, proj_ref, taps_ref, rates_ref, res_ref, skip_ref, conv_ref, grad_ref,
    near_ref, far_ref, hidden_ref, out_ref, ext, feat,
):
    rates = rates_ref[...]
    res_all = res_ref[...]
    skip = skip_ref[...]
    order, width = rates.shape
    rows = conv_ref.shape[0]
    block = rows - TILE
    group, member = place_ref[0], place_ref[1]
    groups, members = far_ref.shape[0], near_ref.shape[0]
    fade = fader(rates, block)
    fwd, bwd, firsts, lasts, near, far = group_states(block, taps_ref, rates, near_ref)

    def rows_of(ref, index, start, there):
        got = ref[jnp.where(there, index, 0)].astype(F32)
        return jnp.where(there, got[start : start + TILE], 0.0)

    nothing = jnp.zeros((TILE, width), F32)
    whole = [far_ref[i].astype(F32) for i in range(groups)]
    head = [w[order : order + TILE] for w in whole] + [nothing]
    tail = [nothing] + [w[order + TILE :] for w in whole]
    ahead = jnp.zeros_like(rates)
    behind = jnp.zeros_like(rates)
    for i in range(groups):
        gated, _ = joint(taps_ref, head[i], tail[i])
        total = whole[i][:order] + fade(members - 1) * (far * gated[0] + near * gated[1])
        ahead = ahead + jnp.where(i < group, fade(members * (group - 1 - i)) * total, 0.0)
        _, grad_conv = joint(taps_ref, head[i + 1], tail[i + 1])
        total = whole[i][:order] + fade(members - 1) * (near * grad_conv[0] + far * grad_conv[1])
        behind = behind + jnp.where(i > group, fade(members * (i - 1 - group)) * total, 0.0)
    tail_before = rows_of(far_ref, group - 1, order + TILE, group > 0)
    head_behind = rows_of(far_ref, group + 1, order, group < groups - 1)
    gated, _ = joint(taps_ref, firsts[0], tail_before)
    _, grad_conv = joint(taps_ref, head_behind, lasts[-1])
    fwd[0] = fwd[0] + far * gated[0] + near * gated[1]
    bwd[-1] = bwd[-1] + near * grad_conv[0] + far * grad_conv[1]
    ahead = fade(member) * ahead
    behind = fade(members - 1 - member) * behind
    for j in range(members):
        ahead = ahead + jnp.where(j < member, fade(member - 1 - j) * fwd[j], 0.0)
        behind = behind + jnp.where(j > member, fade(j - 1 - member) * bwd[j], 0.0)

    last = rows_of(near_ref, member - 1, 2 * order + TILE, member > 0)
    last = jnp.where(member > 0, last, tail_before)
    first = rows_of(near_ref, member + 1, 2 * order, member < members - 1)
    first = jnp.where(member < members - 1, first, head_behind)
    query, key_part, value_part = features(ext, proj_ref, taps_ref, rows, last, first)
    row = lax.broadcasted_iota(jnp.int32, (TILE, 1), 0)
    next_back = jnp.where(row < AHEAD, pltpu.roll(first, AHEAD, 0), 0.0)
    back = jnp.concatenate([proj_ref[3].astype(F32), next_back], axis=0)
    gated = key_part * value_part
    grad_conv = back * query

    g = [gated[i : i + 1] for i in (0, 1, block, block + 1)]
    h = [grad_conv[i : i + 1] for i in (0, 1, block, block + 1)]
    grow = jnp.exp(rates)
    ahead = ahead + grow * g[0] + (grow * grow) * g[1]
    behind = behind + (grow * grow) * h[2] + grow * h[3]
    lag0 = skip + jnp.sum(res_all, axis=0, keepdims=True)
    lag1 = jnp.sum(res_all * jnp.exp(-rates), axis=0, keepdims=True)
    less = jnp.sum(res_all * grow, axis=0, keepdims=True)

    def two(a, b):
        return jnp.where(row == 0, a, jnp.where(row == 1, b, 0.0))

    def with_ends(array, top, bottom):
        return jnp.concatenate(
            [array[:TILE] + top, array[TILE:block], array[block:] + bottom], axis=0
        )

    conv_out = with_ends(
        conv_ref[...],
        two(skip * g[0] - less * g[1], skip * g[1]),
        two(lag0 * g[2], lag0 * g[3] + lag1 * g[2]),
    )
    grad_gated = with_ends(
        grad_ref[...],
        two(lag0 * h[0] + lag1 * h[1], lag0 * h[1]),
        two(skip * h[2], skip * h[3] - less * h[2]),
    )
    time = lax.broadcasted_iota(jnp.int32, (rows, 1), 0).astype(F32)
    ahead = res_all * ahead
    behind = res_all * behind
    for r in range(order):
        rate = rates[r : r + 1]
        conv_out = conv_out + ahead[r : r + 1] * jnp.exp(-rate * (time + 1.0))
        past = jnp.exp(-rate * (block + AHEAD - time))
        grad_gated = grad_gated + behind[r : r + 1] * past
    hidden_ref[...] = (query * conv_out)[:block].astype(BF16)
    feat[0] = back * conv_out
    feat[1] = grad_gated * value_part
    feat[2] = grad_gated * key_part
    for p in range(3):
        total = taps_ref[p, 0:1, :] * feat[p, :block]
        for k in range(1, 3):
            total = total + taps_ref[p, k : k + 1, :] * feat[p, k : k + block]
        out_ref[p] = total.astype(BF16)


def call(kernel, outs, scratch, *args, flops=0):
    whole = pl.BlockSpec(memory_space=pltpu.VMEM)
    specs = [
        pl.BlockSpec(memory_space=pltpu.SMEM) if a.dtype == jnp.int32 else whole for a in args
    ]
    cost = pl.CostEstimate(flops=flops, bytes_accessed=0, transcendentals=0) if flops else None
    return pl.pallas_call(
        kernel,
        out_shape=outs,
        scratch_shapes=scratch,
        in_specs=specs,
        out_specs=jax.tree.map(lambda _: whole, outs),
        cost_estimate=cost,
        compiler_params=pltpu.CompilerParams(vmem_limit_bytes=GRANT),
    )(*args)


def load_weights(blocks, weight_in, weight_out, held_in, held_out, sems):
    part = held_in.shape[2]
    copies = []
    for s, block in enumerate(blocks):
        at = pl.ds(pl.multiple_of(block * part, part), part)
        copies.append(
            (
                pltpu.make_async_copy(weight_in.at[:, at, :], held_in.at[s], sems.at[s, 0]),
                pltpu.make_async_copy(weight_out.at[:, at], held_out.at[s], sems.at[s, 1]),
            )
        )
        for copy in copies[-1]:
            copy.start()

    def ready(s):
        for copy in copies[s]:
            copy.wait()

    return ready


def project_kernel(sizes, offsets, first, last, place_ref, *refs):
    n_x, n_zl = sizes["x"], sizes["zl"]
    pieces, refs = refs[: len(offsets)], refs[len(offsets) :]
    weight_in, weight_out = refs[:2]
    old = None if first else refs[2]
    out, held_in, held_out, sems = refs[2 + (not first) : 6 + (not first)]
    total = refs[-1] if last else out
    block = pieces[0].shape[1] // 2
    work = [
        (piece, j, lax.rem(place_ref[2] + k, n_x) * n_zl + start + j)
        for piece, (k, start) in zip(pieces, offsets)
        for j in range(piece.shape[0])
    ]
    ready = load_weights([w[2] for w in work], weight_in, weight_out, held_in, held_out, sems)
    for s, (piece, j, _) in enumerate(work):
        ready(s)
        part_in = piece[j, :block]
        part_grad = piece[j, block:]
        for p in range(4):
            if p < 3:
                term = jnp.dot(part_in, held_in[s, p], preferred_element_type=F32)
            else:
                term = lax.dot_general(
                    part_grad,
                    held_out[s],
                    (((1,), (1,)), ((), ())),
                    preferred_element_type=F32,
                )
            if s == 0 and first:
                total[p] = term
            else:
                total[p] = (old if s == 0 else total)[p] + term
    if last:
        out[...] = total[...].astype(BF16)


def project(sizes, place, offsets, pieces, weights, old=None, last=False):
    weight_in, weight_out = weights
    count = sum(piece.shape[0] for piece in pieces)
    rows = pieces[0].shape[1] // 2
    part = pieces[0].shape[2]
    width = weight_out.shape[0]
    whole = pl.BlockSpec(memory_space=pltpu.VMEM)
    far = pl.BlockSpec(memory_space=pltpu.HBM)
    scratch = [
        pltpu.VMEM((count, 3, part, width), BF16),
        pltpu.VMEM((count, width, part), BF16),
        pltpu.SemaphoreType.DMA((count, 2)),
    ]
    return pl.pallas_call(
        functools.partial(project_kernel, sizes, offsets, old is None, last),
        in_specs=[pl.BlockSpec(memory_space=pltpu.SMEM)]
        + [whole] * len(pieces)
        + [far, far]
        + [whole] * (old is not None),
        out_specs=whole,
        scratch_shapes=scratch + ([pltpu.VMEM((4, rows, width), F32)] if last else []),
        out_shape=shape(4, rows, width, dtype=BF16 if last else F32),
        cost_estimate=pl.CostEstimate(
            flops=8 * count * rows * part * width,
            bytes_accessed=8 * count * part * width,
            transcendentals=0,
        ),
        compiler_params=pltpu.CompilerParams(vmem_limit_bytes=GRANT),
    )(place, *pieces, weight_in, weight_out, *([] if old is None else [old]))


def partials_kernel(
    sizes, offset, place_ref, hidden, grad, weight_in, weight_out, out, held_in, held_out, sems
):
    n_x, n_zl = sizes["x"], sizes["zl"]
    block = hidden.shape[0]
    k, start = offset
    base = lax.rem(place_ref[2] + k, n_x) * n_zl + start
    count = out.shape[0]
    ready = load_weights(
        [base + j for j in range(count)], weight_in, weight_out, held_in, held_out, sems
    )
    for s in range(count):
        ready(s)
        mixed = jnp.dot(hidden[...], held_out[s], preferred_element_type=F32)
        out[s, :block] = mixed.astype(BF16)
        total = None
        for p in range(3):
            term = lax.dot_general(
                grad[p], held_in[s, p], (((1,), (1,)), ((), ())), preferred_element_type=F32
            )
            total = term if p == 0 else total + term
        out[s, block:] = total.astype(BF16)


def partials(sizes, place, offset, count, hidden, grad, weights, part):
    block, width = hidden.shape
    whole = pl.BlockSpec(memory_space=pltpu.VMEM)
    far = pl.BlockSpec(memory_space=pltpu.HBM)
    return pl.pallas_call(
        functools.partial(partials_kernel, sizes, offset),
        in_specs=[pl.BlockSpec(memory_space=pltpu.SMEM), whole, whole, far, far],
        out_specs=whole,
        scratch_shapes=[
            pltpu.VMEM((count, 3, part, width), BF16),
            pltpu.VMEM((count, width, part), BF16),
            pltpu.SemaphoreType.DMA((count, 2)),
        ],
        out_shape=shape(count, 2 * block, part, dtype=BF16),
        cost_estimate=pl.CostEstimate(
            flops=8 * count * block * part * width,
            bytes_accessed=8 * count * part * width,
            transcendentals=0,
        ),
        compiler_params=pltpu.CompilerParams(vmem_limit_bytes=GRANT),
    )(place, hidden, grad, *weights)


def shape(*dims, dtype=F32):
    return jax.ShapeDtypeStruct(dims, dtype)


def shards(
    sizes,
    tokens,
    cotangent,
    input_weight,
    output_weight,
    short_taps,
    residues,
    decay_rates,
    skip_gain,
):
    n_x, n_zl = sizes["x"], sizes["zl"]
    block, part = tokens.shape
    width = output_weight.shape[0]
    order = residues.shape[1]
    rows = block + TILE
    taps = short_taps.transpose(0, 2, 1)
    rates = decay_rates.T
    res = residues.T
    skip = skip_gain[None]
    place = jnp.stack(
        [
            lax.axis_index("y"),
            lax.axis_index("zh") * sizes["core"] + lax.axis_index("core"),
            lax.axis_index("x"),
        ]
    ).astype(jnp.int32)
    copies = call(
        copy_kernel, shape(n_zl, 2 * block, part, dtype=BF16), [], tokens, cotangent
    )
    pieces = lax.all_to_all(copies, "zl", 0, 0, tiled=True)
    half = n_zl // 2
    right = [(i, (i + 1) % n_x) for i in range(n_x)]
    left = [(i, (i - 1) % n_x) for i in range(n_x)]
    from_left = lax.ppermute(pieces, "x", right)
    from_right = lax.ppermute(pieces, "x", left)
    weights = tuple(
        pltpu.with_memory_space_constraint(w, pltpu.HBM)
        for w in (input_weight.transpose(1, 0, 2), output_weight)
    )
    total = project(sizes, place, [(0, 0)], [pieces], weights)
    from_left, from_right, total = lax.optimization_barrier((from_left, from_right, total))
    far_left = lax.ppermute(from_left[:half], "x", right)
    far_right = lax.ppermute(from_right[half:], "x", left)
    total = project(
        sizes, place, [(n_x - 1, 0), (1, 0)], [from_left, from_right], weights, total
    )
    total = project(
        sizes, place, [(2, 0), (2, half)], [far_left, far_right], weights, total, True
    )
    proj = total
    ext = pltpu.VMEM((3, rows + TILE, width), F32)
    members = sizes["zh"] * sizes["core"]
    pack = 2 * order + 2 * TILE
    send = call(
        state_kernel,
        shape(members, pack, width, dtype=BF16),
        [ext, pltpu.VMEM((pack, width), F32)],
        proj,
        taps,
        rates,
    )
    conv, grad = call(
        local_kernel,
        [shape(rows, width), shape(rows, width)],
        [ext, pltpu.VMEM((2, rows + TILE, width), F32), pltpu.VMEM((rows, width), F32)],
        proj,
        taps,
        rates,
        res,
        skip,
        flops=3 * 10**9,
    )
    near_states = lax.all_to_all(send, ("zh", "core"), 0, 0, tiled=True)
    send = call(
        functools.partial(chain_kernel, block),
        shape(sizes["y"], order + 2 * TILE, width, dtype=BF16),
        [],
        place,
        taps,
        rates,
        near_states,
    )
    far_states = lax.all_to_all(send, "y", 0, 0, tiled=True)
    hidden, grad_proj = call(
        finish_kernel,
        [shape(block, width, dtype=BF16), shape(3, block, width, dtype=BF16)],
        [ext, pltpu.VMEM((3, rows, width), F32)],
        place,
        proj,
        taps,
        rates,
        res,
        skip,
        conv,
        grad,
        near_states,
        far_states,
    )

    def terms(offset, count, order_by=place):
        return partials(sizes, order_by, offset, count, hidden, grad_proj, weights, part)

    def add(*arrays):
        return sum(a.astype(F32) for a in arrays).astype(BF16)

    far_right = lax.ppermute(terms((2, 0), half), "x", right)
    far_left, later = lax.optimization_barrier((terms((2, half), half), place))
    far_left = lax.ppermute(far_left, "x", left)
    to_right = terms((1, 0), n_zl, later)
    to_left = terms((n_x - 1, 0), n_zl, later)
    to_right = jnp.concatenate([add(to_right[:half], far_right), to_right[half:]], axis=0)
    to_left = jnp.concatenate([to_left[:half], add(to_left[half:], far_left)], axis=0)
    from_left = lax.ppermute(to_right, "x", right)
    from_right = lax.ppermute(to_left, "x", left)
    summed = add(terms((0, 0), n_zl, later), from_left, from_right)
    summed = lax.all_to_all(summed, "zl", 0, 0, tiled=True)
    total = jnp.sum(summed.astype(F32), axis=0).astype(BF16)
    return total[:block], total[block:]


def solution(mesh, dims=(8, 4, 2, 4, 4)):
    fine = Mesh(mesh.devices.reshape(dims), CTX + TP)
    sizes = dict(zip(CTX + TP, dims))
    return jax.shard_map(
        functools.partial(shards, sizes),
        mesh=fine,
        in_specs=(
            P(CTX, TP),
            P(CTX, TP),
            P(None, None, TP),
            P(TP, None),
            P(None, TP, None),
            P(TP, None),
            P(TP, None),
            P(TP),
        ),
        out_specs=(P(CTX, TP), P(CTX, TP)),
        check_vma=False,
    )
```

```python
import functools

import jax
import jax.numpy as jnp
from jax import lax
from jax.experimental import pallas as pl
from jax.experimental.pallas import tpu as pltpu
from jax.sharding import Mesh
from jax.sharding import PartitionSpec as P

CTX = ("y", "zh", "core")
TP = ("x", "zl")
TILE = 8
AHEAD = 2
GRANT = 16 * 2**20
BF16 = jnp.bfloat16
F32 = jnp.float32


def copy_kernel(tokens, cotangent, copies, sems):
    block = tokens.shape[0]
    moves = []
    for i in range(copies.shape[0]):
        for k, rows in enumerate((tokens, cotangent)):
            there = copies.at[i, pl.ds(k * block, block)]
            moves.append(pltpu.make_async_copy(rows, there, sems.at[i, k]))
            moves[-1].start()
    for move in moves:
        move.wait()


def features(ext, proj_ref, taps_ref, rows, last=None, first=None):
    block, width = proj_ref.shape[1:]
    zero = jnp.zeros((TILE, width), F32)
    out = []
    for p in range(3):
        ext[p, :TILE] = zero
        ext[p, TILE : TILE + block] = proj_ref[p].astype(F32)
        ext[p, TILE + block :] = zero
        if last is not None:
            ext[p, TILE - AHEAD : TILE] = last[AHEAD * p : AHEAD * (p + 1)]
            ext[p, TILE + block : TILE + block + AHEAD] = first[AHEAD * p : AHEAD * (p + 1)]
        total = taps_ref[p, 0:1, :] * ext[p, TILE : TILE + rows]
        for k in range(1, 3):
            total = total + taps_ref[p, k : k + 1, :] * ext[p, TILE - k : TILE - k + rows]
        out.append(total)
    return out


def inner_rows(ext, proj_ref, taps_ref, rows):
    block, width = proj_ref.shape[1:]
    query, key_part, value_part = features(ext, proj_ref, taps_ref, rows)
    row = lax.broadcasted_iota(jnp.int32, (rows, 1), 0)
    inside = (row >= AHEAD) & (row < block)
    back = jnp.concatenate([proj_ref[3].astype(F32), jnp.zeros((TILE, width), F32)], axis=0)
    gated = jnp.where(inside, key_part * value_part, 0.0)
    return gated, jnp.where(inside, back * query, 0.0), row.astype(F32)


def state_kernel(proj_ref, taps_ref, rates_ref, send_ref, ext, pack):
    order = rates_ref.shape[0]
    block = proj_ref.shape[1]
    gated, grad_conv, time = inner_rows(ext, proj_ref, taps_ref, block + TILE)
    for r in range(order):
        rate = rates_ref[r : r + 1, :]
        fwd = jnp.exp(-rate * (block - 1.0 - time)) * gated
        bwd = jnp.exp(-rate * (time - AHEAD)) * grad_conv
        pack[r : r + 1] = jnp.sum(fwd, axis=0, keepdims=True)
        pack[order + r : order + r + 1] = jnp.sum(bwd, axis=0, keepdims=True)
    at = 2 * order
    pack[at + TILE :] = jnp.zeros((TILE, pack.shape[1]), F32)
    for p in range(4):
        rows = proj_ref[p].astype(F32)
        pack[at + AHEAD * p : at + AHEAD * (p + 1)] = rows[:AHEAD]
        if p < 3:
            ends = at + TILE + AHEAD * p
            pack[ends : ends + AHEAD] = rows[block - AHEAD :]
    for i in range(send_ref.shape[0]):
        send_ref[i] = pack[...].astype(BF16)


def joint(taps_ref, first, last):
    row = []
    for p in range(3):
        a, b = first[AHEAD * p : AHEAD * p + 1], first[AHEAD * p + 1 : AHEAD * p + 2]
        c, d = last[AHEAD * p : AHEAD * p + 1], last[AHEAD * p + 1 : AHEAD * p + 2]
        t = [taps_ref[p, k : k + 1, :] for k in range(3)]
        row.append((t[0] * a + t[1] * d + t[2] * c, t[0] * b + t[1] * a + t[2] * d))
    back = (first[3 * AHEAD : 3 * AHEAD + 1], first[3 * AHEAD + 1 : 3 * AHEAD + 2])
    gated = tuple(row[1][i] * row[2][i] for i in range(AHEAD))
    return gated, tuple(back[i] * row[0][i] for i in range(AHEAD))


def fader(rates, block):
    def fade(blocks):
        if isinstance(blocks, int):
            return jnp.exp(-rates * float(block * blocks))
        return jnp.exp(-rates * (block * jnp.maximum(blocks, 0)).astype(F32))

    return fade


def group_states(block, taps_ref, rates, got_ref):
    order = rates.shape[0]
    members = got_ref.shape[0]
    fwd, bwd, firsts, lasts = [], [], [], []
    for j in range(members):
        got = got_ref[j].astype(F32)
        fwd.append(got[:order])
        bwd.append(got[order : 2 * order])
        firsts.append(got[2 * order : 2 * order + TILE])
        lasts.append(got[2 * order + TILE :])
    near, far = jnp.exp(-rates * (block - 2.0)), jnp.exp(-rates * (block - 1.0))
    for j in range(1, members):
        gated, grad_conv = joint(taps_ref, firsts[j], lasts[j - 1])
        fwd[j] = fwd[j] + far * gated[0] + near * gated[1]
        bwd[j - 1] = bwd[j - 1] + near * grad_conv[0] + far * grad_conv[1]
    return fwd, bwd, firsts, lasts, near, far


def chain_kernel(block, place_ref, taps_ref, rates_ref, got_ref, send_ref):
    rates = rates_ref[...]
    order = rates.shape[0]
    fade = fader(rates, block)
    fwd, bwd, firsts, lasts, _, _ = group_states(block, taps_ref, rates, got_ref)
    members = len(fwd)
    total_fwd = sum(fade(members - 1 - j) * fwd[j] for j in range(members))
    total_bwd = sum(fade(j) * bwd[j] for j in range(members))
    ends = jnp.concatenate([firsts[0], lasts[-1]], axis=0).astype(BF16)
    for i in range(send_ref.shape[0]):
        send_ref[i, :order] = jnp.where(place_ref[0] < i, total_fwd, total_bwd).astype(BF16)
        send_ref[i, order:] = ends


def local_kernel(
    proj_ref, taps_ref, rates_ref, res_ref, skip_ref, conv_ref, grad_ref, ext, pad, filt_ref
):
    rows, width = conv_ref.shape
    gated, grad_conv, time = inner_rows(ext, proj_ref, taps_ref, rows)
    taps = jnp.zeros((rows, width), F32)
    for r in range(rates_ref.shape[0]):
        taps = taps + res_ref[r : r + 1, :] * jnp.exp(-rates_ref[r : r + 1, :] * (time + 1.0))
    filt_ref[...] = taps
    zero = jnp.zeros((TILE, width), F32)
    pad[0, :TILE] = zero
    pad[0, TILE:] = gated
    pad[1, :rows] = grad_conv
    pad[1, rows:] = zero
    direct = skip_ref[...] + jnp.sum(res_ref[...], axis=0, keepdims=True)
    for lane in range(0, width, 128):
        lanes = slice(lane, lane + 128)
        total = direct[:, lanes] * pad[0, TILE:, lanes]
        for m in range(1, TILE + 1):
            moved = pad[0, TILE - m : TILE - m + rows, lanes]
            for q in range(0, rows, TILE):
                tap = filt_ref[q + m - 1 : q + m, lanes]
                part = total[q:] + tap * moved[: rows - q]
                total = part if q == 0 else jnp.concatenate([total[:q], part], axis=0)
        conv_ref[:, lanes] = total
        total = direct[:, lanes] * pad[1, :rows, lanes]
        for m in range(1, TILE + 1):
            moved = pad[1, m : m + rows, lanes]
            for q in range(0, rows, TILE):
                tap = filt_ref[q + m - 1 : q + m, lanes]
                part = total[: rows - q] + tap * moved[q:]
                total = part if q == 0 else jnp.concatenate([part, total[rows - q :]], axis=0)
        grad_ref[:, lanes] = total


def finish_kernel(
    place_ref, proj_ref, taps_ref, rates_ref, res_ref, skip_ref, conv_ref, grad_ref,
    near_ref, far_ref, hidden_ref, out_ref, ext, feat,
):
    rates = rates_ref[...]
    res_all = res_ref[...]
    skip = skip_ref[...]
    order, width = rates.shape
    rows = conv_ref.shape[0]
    block = rows - TILE
    group, member = place_ref[0], place_ref[1]
    groups, members = far_ref.shape[0], near_ref.shape[0]
    fade = fader(rates, block)
    fwd, bwd, firsts, lasts, near, far = group_states(block, taps_ref, rates, near_ref)

    def rows_of(ref, index, start, there):
        got = ref[jnp.where(there, index, 0)].astype(F32)
        return jnp.where(there, got[start : start + TILE], 0.0)

    nothing = jnp.zeros((TILE, width), F32)
    whole = [far_ref[i].astype(F32) for i in range(groups)]
    head = [w[order : order + TILE] for w in whole] + [nothing]
    tail = [nothing] + [w[order + TILE :] for w in whole]
    ahead = jnp.zeros_like(rates)
    behind = jnp.zeros_like(rates)
    for i in range(groups):
        gated, _ = joint(taps_ref, head[i], tail[i])
        total = whole[i][:order] + fade(members - 1) * (far * gated[0] + near * gated[1])
        ahead = ahead + jnp.where(i < group, fade(members * (group - 1 - i)) * total, 0.0)
        _, grad_conv = joint(taps_ref, head[i + 1], tail[i + 1])
        total = whole[i][:order] + fade(members - 1) * (near * grad_conv[0] + far * grad_conv[1])
        behind = behind + jnp.where(i > group, fade(members * (i - 1 - group)) * total, 0.0)
    tail_before = rows_of(far_ref, group - 1, order + TILE, group > 0)
    head_behind = rows_of(far_ref, group + 1, order, group < groups - 1)
    gated, _ = joint(taps_ref, firsts[0], tail_before)
    _, grad_conv = joint(taps_ref, head_behind, lasts[-1])
    fwd[0] = fwd[0] + far * gated[0] + near * gated[1]
    bwd[-1] = bwd[-1] + near * grad_conv[0] + far * grad_conv[1]
    ahead = fade(member) * ahead
    behind = fade(members - 1 - member) * behind
    for j in range(members):
        ahead = ahead + jnp.where(j < member, fade(member - 1 - j) * fwd[j], 0.0)
        behind = behind + jnp.where(j > member, fade(j - 1 - member) * bwd[j], 0.0)

    last = rows_of(near_ref, member - 1, 2 * order + TILE, member > 0)
    last = jnp.where(member > 0, last, tail_before)
    first = rows_of(near_ref, member + 1, 2 * order, member < members - 1)
    first = jnp.where(member < members - 1, first, head_behind)
    query, key_part, value_part = features(ext, proj_ref, taps_ref, rows, last, first)
    row = lax.broadcasted_iota(jnp.int32, (TILE, 1), 0)
    next_back = jnp.where(row < AHEAD, pltpu.roll(first, AHEAD, 0), 0.0)
    back = jnp.concatenate([proj_ref[3].astype(F32), next_back], axis=0)
    gated = key_part * value_part
    grad_conv = back * query

    g = [gated[i : i + 1] for i in (0, 1, block, block + 1)]
    h = [grad_conv[i : i + 1] for i in (0, 1, block, block + 1)]
    grow = jnp.exp(rates)
    ahead = ahead + grow * g[0] + (grow * grow) * g[1]
    behind = behind + (grow * grow) * h[2] + grow * h[3]
    lag0 = skip + jnp.sum(res_all, axis=0, keepdims=True)
    lag1 = jnp.sum(res_all * jnp.exp(-rates), axis=0, keepdims=True)
    less = jnp.sum(res_all * grow, axis=0, keepdims=True)

    def two(a, b):
        return jnp.where(row == 0, a, jnp.where(row == 1, b, 0.0))

    def with_ends(array, top, bottom):
        return jnp.concatenate(
            [array[:TILE] + top, array[TILE:block], array[block:] + bottom], axis=0
        )

    conv_out = with_ends(
        conv_ref[...],
        two(skip * g[0] - less * g[1], skip * g[1]),
        two(lag0 * g[2], lag0 * g[3] + lag1 * g[2]),
    )
    grad_gated = with_ends(
        grad_ref[...],
        two(lag0 * h[0] + lag1 * h[1], lag0 * h[1]),
        two(skip * h[2], skip * h[3] - less * h[2]),
    )
    time = lax.broadcasted_iota(jnp.int32, (rows, 1), 0).astype(F32)
    ahead = res_all * ahead
    behind = res_all * behind
    for r in range(order):
        rate = rates[r : r + 1]
        conv_out = conv_out + ahead[r : r + 1] * jnp.exp(-rate * (time + 1.0))
        past = jnp.exp(-rate * (block + AHEAD - time))
        grad_gated = grad_gated + behind[r : r + 1] * past
    hidden_ref[...] = (query * conv_out)[:block].astype(BF16)
    feat[0] = back * conv_out
    feat[1] = grad_gated * value_part
    feat[2] = grad_gated * key_part
    for p in range(3):
        total = taps_ref[p, 0:1, :] * feat[p, :block]
        for k in range(1, 3):
            total = total + taps_ref[p, k : k + 1, :] * feat[p, k : k + block]
        out_ref[p] = total.astype(BF16)


def in_hbm(array):
    return pltpu.with_memory_space_constraint(array, pltpu.HBM)


def call(kernel, outs, scratch, *args, flops=0, hbm=0):
    whole = pl.BlockSpec(memory_space=pltpu.VMEM)
    far = pl.BlockSpec(memory_space=pltpu.HBM)
    scalar = pl.BlockSpec(memory_space=pltpu.SMEM)
    specs = [
        scalar if a.dtype == jnp.int32 else far if i >= len(args) - hbm else whole
        for i, a in enumerate(args)
    ]
    cost = pl.CostEstimate(flops=flops, bytes_accessed=0, transcendentals=0) if flops else None
    return pl.pallas_call(
        kernel,
        out_shape=outs,
        scratch_shapes=scratch,
        in_specs=specs,
        out_specs=jax.tree.map(lambda _: whole, outs),
        cost_estimate=cost,
        compiler_params=pltpu.CompilerParams(vmem_limit_bytes=GRANT),
    )(*args)


def load_weights(blocks, weight_in, weight_out, held_in, held_out, sems, ahead=3):
    part = held_in.shape[2]
    copies = []
    for s, block in enumerate(blocks):
        at = pl.ds(pl.multiple_of(block * part, part), part)
        copies.append(
            (
                pltpu.make_async_copy(weight_in.at[:, at, :], held_in.at[s], sems.at[s, 0]),
                pltpu.make_async_copy(weight_out.at[:, at], held_out.at[s], sems.at[s, 1]),
            )
        )

    def start(s):
        for copy in copies[s]:
            copy.start()

    for s in range(min(ahead, len(copies))):
        start(s)

    def ready(s):
        for copy in copies[s]:
            copy.wait()
        if s + ahead < len(copies):
            start(s + ahead)

    return ready


def held_weights(count, part, width):
    return [
        pltpu.VMEM((count, 3, part, width), BF16),
        pltpu.VMEM((count, width, part), BF16),
        pltpu.SemaphoreType.DMA((count, 2)),
    ]


def project(sizes, offsets, place_ref, pieces, weights, old, total, held_in, held_out, sems):
    n_x, n_zl = sizes["x"], sizes["zl"]
    block = pieces[0].shape[1] // 2
    work = [
        (piece, j, lax.rem(place_ref[2] + k, n_x) * n_zl + start + j)
        for piece, (k, start) in zip(pieces, offsets)
        for j in range(piece.shape[0])
    ]
    ready = load_weights([w[2] for w in work], *weights, held_in, held_out, sems)
    for s, (piece, j, _) in enumerate(work):
        ready(s)
        for p in range(4):
            if p < 3:
                term = jnp.dot(piece[j, :block], held_in[s, p], preferred_element_type=F32)
            else:
                term = lax.dot_general(
                    piece[j, block:],
                    held_out[s],
                    (((1,), (1,)), ((), ())),
                    preferred_element_type=F32,
                )
            if s == 0 and old is None:
                total[p] = term
            else:
                total[p] = (old if s == 0 else total)[p] + term


def near_kernel(sizes, place, piece, weight_in, weight_out, total, *held):
    project(sizes, [(0, 0)], place, [piece], (weight_in, weight_out), None, total, *held)


def side_kernel(sizes, place, left, right, old, weight_in, weight_out, total, *held):
    offsets = [(sizes["x"] - 1, 0), (1, 0)]
    weights = (weight_in, weight_out)
    project(sizes, offsets, place, [left, right], weights, old, total, *held)


def far_kernel(
    sizes, place, left, right, old, taps, rates, weight_in, weight_out, proj, send, total, ext, pack, *held
):
    offsets = [(2, 0), (2, left.shape[0])]
    weights = (weight_in, weight_out)
    project(sizes, offsets, place, [left, right], weights, old, total, *held)
    proj[...] = total[...].astype(BF16)
    state_kernel(proj, taps, rates, send, ext, pack)


def partials(held, start, out, hidden, grad, ready):
    held_in, held_out = held[:2]
    block = hidden.shape[0]
    for j in range(out.shape[0]):
        s = start + j
        ready(s)
        mixed = jnp.dot(hidden[...], held_out[s], preferred_element_type=F32)
        out[j, :block] = mixed.astype(BF16)
        total = None
        for p in range(3):
            term = lax.dot_general(
                grad[p], held_in[s, p], (((1,), (1,)), ((), ())), preferred_element_type=F32
            )
            total = term if p == 0 else total + term
        out[j, block:] = total.astype(BF16)


def partials_kernel(sizes, offsets, place, hidden, grad, weight_in, weight_out, *refs):
    outs, held = refs[:-3], refs[-3:]
    n_x, n_zl = sizes["x"], sizes["zl"]
    blocks = [
        lax.rem(place[2] + k, n_x) * n_zl + j
        for k, out in zip(offsets, outs)
        for j in range(out.shape[0])
    ]
    ready = load_weights(blocks, weight_in, weight_out, *held)
    start = 0
    for out in outs:
        partials(held, start, out, hidden, grad, ready)
        start += out.shape[0]


def last_kernel(
    sizes, place, proj, taps, rates, res, skip, conv, grad, near, far, weight_in, weight_out,
    hidden, out, to_right, to_left, ext, feat, *held,
):
    n_x, n_zl = sizes["x"], sizes["zl"]
    blocks = [lax.rem(place[2] + 2, n_x) * n_zl + j for j in range(n_zl)]
    ready = load_weights(blocks, weight_in, weight_out, *held, ahead=n_zl)
    finish_kernel(
        place, proj, taps, rates, res, skip, conv, grad, near, far, hidden, out, ext, feat
    )
    partials(held, 0, to_right, hidden, out, ready)
    partials(held, to_right.shape[0], to_left, hidden, out, ready)


def join_kernel(start, terms, got, out):
    count = got.shape[0]
    for i in range(terms.shape[0]):
        if start <= i < start + count:
            both = terms[i].astype(F32) + got[i - start].astype(F32)
            out[i] = both.astype(BF16)
        else:
            out[i] = terms[i]


def shape(*dims, dtype=F32):
    return jax.ShapeDtypeStruct(dims, dtype)


def shards(
    sizes,
    tokens,
    cotangent,
    input_weight,
    output_weight,
    short_taps,
    residues,
    decay_rates,
    skip_gain,
):
    n_x, n_zl = sizes["x"], sizes["zl"]
    block, part = tokens.shape
    width = output_weight.shape[0]
    order = residues.shape[1]
    rows = block + TILE
    taps = short_taps.transpose(0, 2, 1)
    rates = decay_rates.T
    res = residues.T
    skip = skip_gain[None]
    place = jnp.stack(
        [
            lax.axis_index("y"),
            lax.axis_index("zh") * sizes["core"] + lax.axis_index("core"),
            lax.axis_index("x"),
        ]
    ).astype(jnp.int32)
    copies = call(
        copy_kernel,
        shape(n_zl, 2 * block, part, dtype=BF16),
        [pltpu.SemaphoreType.DMA((n_zl, 2))],
        in_hbm(tokens),
        in_hbm(cotangent),
        hbm=2,
    )
    pieces = lax.all_to_all(copies, "zl", 0, 0, tiled=True)
    half = n_zl // 2

    def products(count):
        return 8 * count * block * part * width

    right = [(i, (i + 1) % n_x) for i in range(n_x)]
    left = [(i, (i - 1) % n_x) for i in range(n_x)]
    from_left = lax.ppermute(pieces, "x", right)
    from_right = lax.ppermute(pieces, "x", left)
    weights = (in_hbm(input_weight.transpose(1, 0, 2)), in_hbm(output_weight))
    total = call(
        functools.partial(near_kernel, sizes),
        shape(4, block, width),
        held_weights(n_zl, part, width),
        place,
        pieces,
        *weights,
        flops=products(n_zl),
        hbm=2,
    )
    from_left, from_right, total = lax.optimization_barrier((from_left, from_right, total))
    far_left = lax.ppermute(from_left[:half], "x", right)
    far_right = lax.ppermute(from_right[half:], "x", left)
    total = call(
        functools.partial(side_kernel, sizes),
        shape(4, block, width),
        held_weights(2 * n_zl, part, width),
        place,
        from_left,
        from_right,
        total,
        *weights,
        flops=products(2 * n_zl),
        hbm=2,
    )
    ext = pltpu.VMEM((3, rows + TILE, width), F32)
    members = sizes["zh"] * sizes["core"]
    pack = 2 * order + 2 * TILE
    proj, send = call(
        functools.partial(far_kernel, sizes),
        [shape(4, block, width, dtype=BF16), shape(members, pack, width, dtype=BF16)],
        [pltpu.VMEM((4, block, width), F32), ext, pltpu.VMEM((pack, width), F32)]
        + held_weights(n_zl, part, width),
        place,
        far_left,
        far_right,
        total,
        taps,
        rates,
        *weights,
        flops=products(n_zl),
        hbm=2,
    )
    conv, grad = call(
        local_kernel,
        [shape(rows, width), shape(rows, width)],
        [ext, pltpu.VMEM((2, rows + TILE, width), F32), pltpu.VMEM((rows, width), F32)],
        proj,
        taps,
        rates,
        res,
        skip,
        flops=3 * 10**9,
    )
    near_states = lax.all_to_all(send, ("zh", "core"), 0, 0, tiled=True)
    send = call(
        functools.partial(chain_kernel, block),
        shape(sizes["y"], order + 2 * TILE, width, dtype=BF16),
        [],
        place,
        taps,
        rates,
        near_states,
    )
    far_states = lax.all_to_all(send, "y", 0, 0, tiled=True)
    piece = shape(n_zl, 2 * block, part, dtype=BF16)
    half_piece = shape(half, 2 * block, part, dtype=BF16)
    hidden, grad_proj, to_right, to_left = call(
        functools.partial(last_kernel, sizes),
        [
            shape(block, width, dtype=BF16),
            shape(3, block, width, dtype=BF16),
            half_piece,
            half_piece,
        ],
        [ext, pltpu.VMEM((3, rows, width), F32)] + held_weights(n_zl, part, width),
        place,
        proj,
        taps,
        rates,
        res,
        skip,
        conv,
        grad,
        near_states,
        far_states,
        *weights,
        flops=products(n_zl),
        hbm=2,
    )
    far_right = lax.ppermute(to_right, "x", right)
    far_left = lax.ppermute(to_left, "x", left)
    to_right, to_left = call(
        functools.partial(partials_kernel, sizes, [1, n_x - 1]),
        [piece, piece],
        held_weights(2 * n_zl, part, width),
        place,
        hidden,
        grad_proj,
        *weights,
        flops=products(2 * n_zl),
        hbm=2,
    )
    to_right = call(functools.partial(join_kernel, 0), piece, [], to_right, far_right)
    from_left = lax.ppermute(to_right, "x", right)
    to_left = call(functools.partial(join_kernel, half), piece, [], to_left, far_left)
    from_right = lax.ppermute(to_left, "x", left)
    (own,) = call(
        functools.partial(partials_kernel, sizes, [0]),
        [piece],
        held_weights(n_zl, part, width),
        place,
        hidden,
        grad_proj,
        *weights,
        flops=products(n_zl),
        hbm=2,
    )
    summed = sum(a.astype(F32) for a in (own, from_left, from_right)).astype(BF16)
    summed = lax.all_to_all(summed, "zl", 0, 0, tiled=True)
    total = jnp.sum(summed.astype(F32), axis=0).astype(BF16)
    return total[:block], total[block:]


def solution(mesh, dims=(8, 4, 2, 4, 4)):
    fine = Mesh(mesh.devices.reshape(dims), CTX + TP)
    sizes = dict(zip(CTX + TP, dims))
    return jax.shard_map(
        functools.partial(shards, sizes),
        mesh=fine,
        in_specs=(
            P(CTX, TP),
            P(CTX, TP),
            P(None, None, TP),
            P(TP, None),
            P(None, TP, None),
            P(TP, None),
            P(TP, None),
            P(TP),
        ),
        out_specs=(P(CTX, TP), P(CTX, TP)),
        check_vma=False,
    )
```

```python
import functools

import jax
import jax.numpy as jnp
from jax import lax
from jax.experimental import pallas as pl
from jax.experimental.pallas import tpu as pltpu
from jax.sharding import Mesh
from jax.sharding import PartitionSpec as P

CTX = ("y", "zh", "core")
TP = ("x", "zl")
TILE = 8
AHEAD = 2
GRANT = 16 * 2**20
PAIR = 2
BF16 = jnp.bfloat16
F32 = jnp.float32


def copy_kernel(tokens, cotangent, copies, sems):
    block = tokens.shape[0]
    moves = []
    for i in range(copies.shape[0]):
        for k, rows in enumerate((tokens, cotangent)):
            there = copies.at[i, pl.ds(k * block, block)]
            moves.append(pltpu.make_async_copy(rows, there, sems.at[i, k]))
            moves[-1].start()
    for move in moves:
        move.wait()


def features(ext, proj_ref, taps_ref, rows, last=None, first=None):
    block, width = proj_ref.shape[1:]
    zero = jnp.zeros((TILE, width), F32)
    out = []
    for p in range(3):
        ext[p, :TILE] = zero
        ext[p, TILE : TILE + block] = proj_ref[p].astype(F32)
        ext[p, TILE + block :] = zero
        if last is not None:
            ext[p, TILE - AHEAD : TILE] = last[AHEAD * p : AHEAD * (p + 1)]
            ext[p, TILE + block : TILE + block + AHEAD] = first[AHEAD * p : AHEAD * (p + 1)]
        total = taps_ref[p, 0:1, :] * ext[p, TILE : TILE + rows]
        for k in range(1, 3):
            total = total + taps_ref[p, k : k + 1, :] * ext[p, TILE - k : TILE - k + rows]
        out.append(total)
    return out


def inner_rows(ext, proj_ref, taps_ref, rows):
    block, width = proj_ref.shape[1:]
    query, key_part, value_part = features(ext, proj_ref, taps_ref, rows)
    row = lax.broadcasted_iota(jnp.int32, (rows, 1), 0)
    inside = (row >= AHEAD) & (row < block)
    back = jnp.concatenate([proj_ref[3].astype(F32), jnp.zeros((TILE, width), F32)], axis=0)
    gated = jnp.where(inside, key_part * value_part, 0.0)
    return gated, jnp.where(inside, back * query, 0.0), row.astype(F32)


def state_kernel(proj_ref, taps_ref, rates_ref, send_ref, ext, pack):
    order = rates_ref.shape[0]
    block = proj_ref.shape[1]
    gated, grad_conv, time = inner_rows(ext, proj_ref, taps_ref, block + TILE)
    for r in range(order):
        rate = rates_ref[r : r + 1, :]
        fwd = jnp.exp(-rate * (block - 1.0 - time)) * gated
        bwd = jnp.exp(-rate * (time - AHEAD)) * grad_conv
        pack[r : r + 1] = jnp.sum(fwd, axis=0, keepdims=True)
        pack[order + r : order + r + 1] = jnp.sum(bwd, axis=0, keepdims=True)
    at = 2 * order
    pack[at + TILE :] = jnp.zeros((TILE, pack.shape[1]), F32)
    for p in range(4):
        rows = proj_ref[p].astype(F32)
        pack[at + AHEAD * p : at + AHEAD * (p + 1)] = rows[:AHEAD]
        if p < 3:
            ends = at + TILE + AHEAD * p
            pack[ends : ends + AHEAD] = rows[block - AHEAD :]
    for i in range(send_ref.shape[0]):
        send_ref[i] = pack[...].astype(BF16)


def joint(taps_ref, first, last):
    row = []
    for p in range(3):
        a, b = first[AHEAD * p : AHEAD * p + 1], first[AHEAD * p + 1 : AHEAD * p + 2]
        c, d = last[AHEAD * p : AHEAD * p + 1], last[AHEAD * p + 1 : AHEAD * p + 2]
        t = [taps_ref[p, k : k + 1, :] for k in range(3)]
        row.append((t[0] * a + t[1] * d + t[2] * c, t[0] * b + t[1] * a + t[2] * d))
    back = (first[3 * AHEAD : 3 * AHEAD + 1], first[3 * AHEAD + 1 : 3 * AHEAD + 2])
    gated = tuple(row[1][i] * row[2][i] for i in range(AHEAD))
    return gated, tuple(back[i] * row[0][i] for i in range(AHEAD))


def fader(rates, block):
    def fade(blocks):
        if isinstance(blocks, int):
            return jnp.exp(-rates * float(block * blocks))
        return jnp.exp(-rates * (block * jnp.maximum(blocks, 0)).astype(F32))

    return fade


def group_states(block, taps_ref, rates, got_ref):
    order = rates.shape[0]
    members = got_ref.shape[0]
    fwd, bwd, firsts, lasts = [], [], [], []
    for j in range(members):
        got = got_ref[j].astype(F32)
        fwd.append(got[:order])
        bwd.append(got[order : 2 * order])
        firsts.append(got[2 * order : 2 * order + TILE])
        lasts.append(got[2 * order + TILE :])
    near, far = jnp.exp(-rates * (block - 2.0)), jnp.exp(-rates * (block - 1.0))
    for j in range(1, members):
        gated, grad_conv = joint(taps_ref, firsts[j], lasts[j - 1])
        fwd[j] = fwd[j] + far * gated[0] + near * gated[1]
        bwd[j - 1] = bwd[j - 1] + near * grad_conv[0] + far * grad_conv[1]
    return fwd, bwd, firsts, lasts, near, far


def chain_kernel(block, place_ref, taps_ref, rates_ref, got_ref, send_ref):
    rates = rates_ref[...]
    order = rates.shape[0]
    fade = fader(rates, block)
    fwd, bwd, firsts, lasts, _, _ = group_states(block, taps_ref, rates, got_ref)
    members = len(fwd)
    total_fwd = sum(fade(members - 1 - j) * fwd[j] for j in range(members))
    total_bwd = sum(fade(j) * bwd[j] for j in range(members))
    ends = jnp.concatenate([firsts[0], lasts[-1]], axis=0).astype(BF16)
    for i in range(send_ref.shape[0]):
        send_ref[i, :order] = jnp.where(place_ref[0] < i, total_fwd, total_bwd).astype(BF16)
        send_ref[i, order:] = ends


def local_kernel(
    proj_ref, taps_ref, rates_ref, res_ref, skip_ref, conv_ref, grad_ref, ext, pad, filt_ref
):
    rows, width = conv_ref.shape
    gated, grad_conv, time = inner_rows(ext, proj_ref, taps_ref, rows)
    taps = jnp.zeros((rows, width), F32)
    for r in range(rates_ref.shape[0]):
        taps = taps + res_ref[r : r + 1, :] * jnp.exp(-rates_ref[r : r + 1, :] * (time + 1.0))
    filt_ref[...] = taps
    zero = jnp.zeros((TILE, width), F32)
    pad[0, :TILE] = zero
    pad[0, TILE:] = gated
    pad[1, :rows] = grad_conv
    pad[1, rows:] = zero
    direct = skip_ref[...] + jnp.sum(res_ref[...], axis=0, keepdims=True)
    for lane in range(0, width, 128):
        lanes = slice(lane, lane + 128)
        total = direct[:, lanes] * pad[0, TILE:, lanes]
        for m in range(1, TILE + 1):
            moved = pad[0, TILE - m : TILE - m + rows, lanes]
            for q in range(0, rows, TILE):
                tap = filt_ref[q + m - 1 : q + m, lanes]
                part = total[q:] + tap * moved[: rows - q]
                total = part if q == 0 else jnp.concatenate([total[:q], part], axis=0)
        conv_ref[:, lanes] = total
        total = direct[:, lanes] * pad[1, :rows, lanes]
        for m in range(1, TILE + 1):
            moved = pad[1, m : m + rows, lanes]
            for q in range(0, rows, TILE):
                tap = filt_ref[q + m - 1 : q + m, lanes]
                part = total[: rows - q] + tap * moved[q:]
                total = part if q == 0 else jnp.concatenate([part, total[rows - q :]], axis=0)
        grad_ref[:, lanes] = total


def finish_kernel(
    place_ref, proj_ref, taps_ref, rates_ref, res_ref, skip_ref, conv_ref, grad_ref,
    near_ref, far_ref, hidden_ref, out_ref, ext, feat,
):
    rates = rates_ref[...]
    res_all = res_ref[...]
    skip = skip_ref[...]
    order, width = rates.shape
    rows = conv_ref.shape[0]
    block = rows - TILE
    group, member = place_ref[0], place_ref[1]
    groups, members = far_ref.shape[0], near_ref.shape[0]
    fade = fader(rates, block)
    fwd, bwd, firsts, lasts, near, far = group_states(block, taps_ref, rates, near_ref)

    def rows_of(ref, index, start, there):
        got = ref[jnp.where(there, index, 0)].astype(F32)
        return jnp.where(there, got[start : start + TILE], 0.0)

    nothing = jnp.zeros((TILE, width), F32)
    whole = [far_ref[i].astype(F32) for i in range(groups)]
    head = [w[order : order + TILE] for w in whole] + [nothing]
    tail = [nothing] + [w[order + TILE :] for w in whole]
    ahead = jnp.zeros_like(rates)
    behind = jnp.zeros_like(rates)
    for i in range(groups):
        gated, _ = joint(taps_ref, head[i], tail[i])
        total = whole[i][:order] + fade(members - 1) * (far * gated[0] + near * gated[1])
        ahead = ahead + jnp.where(i < group, fade(members * (group - 1 - i)) * total, 0.0)
        _, grad_conv = joint(taps_ref, head[i + 1], tail[i + 1])
        total = whole[i][:order] + fade(members - 1) * (near * grad_conv[0] + far * grad_conv[1])
        behind = behind + jnp.where(i > group, fade(members * (i - 1 - group)) * total, 0.0)
    tail_before = rows_of(far_ref, group - 1, order + TILE, group > 0)
    head_behind = rows_of(far_ref, group + 1, order, group < groups - 1)
    gated, _ = joint(taps_ref, firsts[0], tail_before)
    _, grad_conv = joint(taps_ref, head_behind, lasts[-1])
    fwd[0] = fwd[0] + far * gated[0] + near * gated[1]
    bwd[-1] = bwd[-1] + near * grad_conv[0] + far * grad_conv[1]
    ahead = fade(member) * ahead
    behind = fade(members - 1 - member) * behind
    for j in range(members):
        ahead = ahead + jnp.where(j < member, fade(member - 1 - j) * fwd[j], 0.0)
        behind = behind + jnp.where(j > member, fade(j - 1 - member) * bwd[j], 0.0)

    last = rows_of(near_ref, member - 1, 2 * order + TILE, member > 0)
    last = jnp.where(member > 0, last, tail_before)
    first = rows_of(near_ref, member + 1, 2 * order, member < members - 1)
    first = jnp.where(member < members - 1, first, head_behind)
    query, key_part, value_part = features(ext, proj_ref, taps_ref, rows, last, first)
    row = lax.broadcasted_iota(jnp.int32, (TILE, 1), 0)
    next_back = jnp.where(row < AHEAD, pltpu.roll(first, AHEAD, 0), 0.0)
    back = jnp.concatenate([proj_ref[3].astype(F32), next_back], axis=0)
    gated = key_part * value_part
    grad_conv = back * query

    g = [gated[i : i + 1] for i in (0, 1, block, block + 1)]
    h = [grad_conv[i : i + 1] for i in (0, 1, block, block + 1)]
    grow = jnp.exp(rates)
    ahead = ahead + grow * g[0] + (grow * grow) * g[1]
    behind = behind + (grow * grow) * h[2] + grow * h[3]
    lag0 = skip + jnp.sum(res_all, axis=0, keepdims=True)
    lag1 = jnp.sum(res_all * jnp.exp(-rates), axis=0, keepdims=True)
    less = jnp.sum(res_all * grow, axis=0, keepdims=True)

    def two(a, b):
        return jnp.where(row == 0, a, jnp.where(row == 1, b, 0.0))

    def with_ends(array, top, bottom):
        return jnp.concatenate(
            [array[:TILE] + top, array[TILE:block], array[block:] + bottom], axis=0
        )

    conv_out = with_ends(
        conv_ref[...],
        two(skip * g[0] - less * g[1], skip * g[1]),
        two(lag0 * g[2], lag0 * g[3] + lag1 * g[2]),
    )
    grad_gated = with_ends(
        grad_ref[...],
        two(lag0 * h[0] + lag1 * h[1], lag0 * h[1]),
        two(skip * h[2], skip * h[3] - less * h[2]),
    )
    time = lax.broadcasted_iota(jnp.int32, (rows, 1), 0).astype(F32)
    ahead = res_all * ahead
    behind = res_all * behind
    for r in range(order):
        rate = rates[r : r + 1]
        conv_out = conv_out + ahead[r : r + 1] * jnp.exp(-rate * (time + 1.0))
        past = jnp.exp(-rate * (block + AHEAD - time))
        grad_gated = grad_gated + behind[r : r + 1] * past
    hidden_ref[...] = (query * conv_out)[:block].astype(BF16)
    feat[0] = back * conv_out
    feat[1] = grad_gated * value_part
    feat[2] = grad_gated * key_part
    for p in range(3):
        total = taps_ref[p, 0:1, :] * feat[p, :block]
        for k in range(1, 3):
            total = total + taps_ref[p, k : k + 1, :] * feat[p, k : k + block]
        out_ref[p] = total.astype(BF16)


def in_hbm(array):
    return pltpu.with_memory_space_constraint(array, pltpu.HBM)


def call(kernel, outs, scratch, *args, flops=0, hbm=0):
    whole = pl.BlockSpec(memory_space=pltpu.VMEM)
    far = pl.BlockSpec(memory_space=pltpu.HBM)
    scalar = pl.BlockSpec(memory_space=pltpu.SMEM)
    specs = [
        scalar if a.dtype == jnp.int32 else far if i >= len(args) - hbm else whole
        for i, a in enumerate(args)
    ]
    cost = pl.CostEstimate(flops=flops, bytes_accessed=0, transcendentals=0) if flops else None
    return pl.pallas_call(
        kernel,
        out_shape=outs,
        scratch_shapes=scratch,
        in_specs=specs,
        out_specs=jax.tree.map(lambda _: whole, outs),
        cost_estimate=cost,
        compiler_params=pltpu.CompilerParams(vmem_limit_bytes=GRANT),
    )(*args)


def load_weights(blocks, weight_in, weight_out, held_in, held_out, sems, ahead=2):
    span = held_in.shape[1]
    width = weight_out.shape[0]
    part = span // PAIR
    copies = []
    for s, block in enumerate(blocks):
        at = pl.ds(pl.multiple_of(block * part, part), span)
        moves = [
            pltpu.make_async_copy(
                weight_in.at[p, at, :],
                held_in.at[s, :, pl.ds(p * width, width)],
                sems.at[s, p],
            )
            for p in range(3)
        ]
        moves.append(
            pltpu.make_async_copy(weight_out.at[:, at], held_out.at[s], sems.at[s, 3])
        )
        copies.append(moves)

    def start(s):
        for copy in copies[s]:
            copy.start()

    for s in range(min(ahead, len(copies))):
        start(s)

    def ready(s):
        for copy in copies[s]:
            copy.wait()
        if s + ahead < len(copies):
            start(s + ahead)

    return ready


def held_weights(count, part, width):
    return [
        pltpu.VMEM((count, PAIR * part, 3 * width), BF16),
        pltpu.VMEM((count, width, PAIR * part), BF16),
        pltpu.SemaphoreType.DMA((count, 4)),
    ]


def project(sizes, offsets, place_ref, pieces, weights, old, total, held_in, held_out, sems):
    n_x, n_zl = sizes["x"], sizes["zl"]
    block = pieces[0].shape[1] // 2
    width = total.shape[2]
    work = [
        (piece, j, lax.rem(place_ref[2] + k, n_x) * n_zl + start + j)
        for piece, (k, start) in zip(pieces, offsets)
        for j in range(0, piece.shape[0], PAIR)
    ]
    ready = load_weights([w[2] for w in work], *weights, held_in, held_out, sems)
    for s, (piece, j, _) in enumerate(work):
        run = range(j, j + PAIR)
        part_in = jnp.concatenate([piece[i, :block] for i in run], axis=1)
        part_grad = jnp.concatenate([piece[i, block:] for i in run], axis=1)
        ready(s)
        term = jnp.dot(part_in, held_in[s], preferred_element_type=F32)
        back = lax.dot_general(
            part_grad, held_out[s], (((1,), (1,)), ((), ())), preferred_element_type=F32
        )
        terms = [term[:, p * width : (p + 1) * width] for p in range(3)] + [back]
        for p in range(4):
            if s == 0 and old is None:
                total[p] = terms[p]
            else:
                total[p] = (old if s == 0 else total)[p] + terms[p]


def near_kernel(sizes, place, piece, weight_in, weight_out, total, *held):
    project(sizes, [(0, 0)], place, [piece], (weight_in, weight_out), None, total, *held)


def side_kernel(sizes, place, left, right, old, weight_in, weight_out, total, *held):
    offsets = [(sizes["x"] - 1, 0), (1, 0)]
    weights = (weight_in, weight_out)
    project(sizes, offsets, place, [left, right], weights, old, total, *held)


def far_kernel(
    sizes, place, left, right, old, taps, rates, weight_in, weight_out, proj, send, total, ext, pack, *held
):
    offsets = [(2, 0), (2, left.shape[0])]
    weights = (weight_in, weight_out)
    project(sizes, offsets, place, [left, right], weights, old, total, *held)
    proj[...] = total[...].astype(BF16)
    state_kernel(proj, taps, rates, send, ext, pack)


def partials(held, start, out, hidden, grad, ready):
    held_in, held_out = held[:2]
    block = hidden.shape[0]
    part = out.shape[2]
    for j in range(0, out.shape[0], PAIR):
        s = start + j // PAIR
        grads = jnp.concatenate([grad[p] for p in range(3)], axis=1)
        ready(s)
        mixed = jnp.dot(hidden[...], held_out[s], preferred_element_type=F32)
        total = lax.dot_general(
            grads, held_in[s], (((1,), (1,)), ((), ())), preferred_element_type=F32
        )
        for i in range(PAIR):
            out[j + i, :block] = mixed[:, i * part : (i + 1) * part].astype(BF16)
            out[j + i, block:] = total[:, i * part : (i + 1) * part].astype(BF16)


def partials_kernel(sizes, offsets, place, hidden, grad, weight_in, weight_out, *refs):
    outs, held = refs[:-3], refs[-3:]
    n_x, n_zl = sizes["x"], sizes["zl"]
    blocks = [
        lax.rem(place[2] + k, n_x) * n_zl + j
        for k, out in zip(offsets, outs)
        for j in range(0, out.shape[0], PAIR)
    ]
    ready = load_weights(blocks, weight_in, weight_out, *held)
    start = 0
    for out in outs:
        partials(held, start, out, hidden, grad, ready)
        start += out.shape[0] // PAIR


def last_kernel(
    sizes, place, proj, taps, rates, res, skip, conv, grad, near, far, weight_in, weight_out,
    hidden, out, to_right, to_left, ext, feat, *held,
):
    n_x, n_zl = sizes["x"], sizes["zl"]
    blocks = [lax.rem(place[2] + 2, n_x) * n_zl + j for j in range(0, n_zl, PAIR)]
    ready = load_weights(blocks, weight_in, weight_out, *held)
    finish_kernel(
        place, proj, taps, rates, res, skip, conv, grad, near, far, hidden, out, ext, feat
    )
    partials(held, 0, to_right, hidden, out, ready)
    partials(held, to_right.shape[0] // PAIR, to_left, hidden, out, ready)


def join_kernel(start, terms, got, out):
    count = got.shape[0]
    for i in range(terms.shape[0]):
        if start <= i < start + count:
            both = terms[i].astype(F32) + got[i - start].astype(F32)
            out[i] = both.astype(BF16)
        else:
            out[i] = terms[i]


def shape(*dims, dtype=F32):
    return jax.ShapeDtypeStruct(dims, dtype)


def shards(
    sizes,
    tokens,
    cotangent,
    input_weight,
    output_weight,
    short_taps,
    residues,
    decay_rates,
    skip_gain,
):
    n_x, n_zl = sizes["x"], sizes["zl"]
    block, part = tokens.shape
    width = output_weight.shape[0]
    order = residues.shape[1]
    rows = block + TILE
    taps = short_taps.transpose(0, 2, 1)
    rates = decay_rates.T
    res = residues.T
    skip = skip_gain[None]
    place = jnp.stack(
        [
            lax.axis_index("y"),
            lax.axis_index("zh") * sizes["core"] + lax.axis_index("core"),
            lax.axis_index("x"),
        ]
    ).astype(jnp.int32)
    copies = call(
        copy_kernel,
        shape(n_zl, 2 * block, part, dtype=BF16),
        [pltpu.SemaphoreType.DMA((n_zl, 2))],
        in_hbm(tokens),
        in_hbm(cotangent),
        hbm=2,
    )
    pieces = lax.all_to_all(copies, "zl", 0, 0, tiled=True)
    half = n_zl // 2

    def products(count):
        return 8 * count * block * part * width

    right = [(i, (i + 1) % n_x) for i in range(n_x)]
    left = [(i, (i - 1) % n_x) for i in range(n_x)]
    from_left = lax.ppermute(pieces, "x", right)
    from_right = lax.ppermute(pieces, "x", left)
    weights = (in_hbm(input_weight.transpose(1, 0, 2)), in_hbm(output_weight))
    total = call(
        functools.partial(near_kernel, sizes),
        shape(4, block, width),
        held_weights(n_zl // PAIR, part, width),
        place,
        pieces,
        *weights,
        flops=products(n_zl),
        hbm=2,
    )
    from_left, from_right, total = lax.optimization_barrier((from_left, from_right, total))
    far_left = lax.ppermute(from_left[:half], "x", right)
    far_right = lax.ppermute(from_right[half:], "x", left)
    total = call(
        functools.partial(side_kernel, sizes),
        shape(4, block, width),
        held_weights(2 * n_zl // PAIR, part, width),
        place,
        from_left,
        from_right,
        total,
        *weights,
        flops=products(2 * n_zl),
        hbm=2,
    )
    ext = pltpu.VMEM((3, rows + TILE, width), F32)
    members = sizes["zh"] * sizes["core"]
    pack = 2 * order + 2 * TILE
    proj, send = call(
        functools.partial(far_kernel, sizes),
        [shape(4, block, width, dtype=BF16), shape(members, pack, width, dtype=BF16)],
        [pltpu.VMEM((4, block, width), F32), ext, pltpu.VMEM((pack, width), F32)]
        + held_weights(n_zl // PAIR, part, width),
        place,
        far_left,
        far_right,
        total,
        taps,
        rates,
        *weights,
        flops=products(n_zl),
        hbm=2,
    )
    conv, grad = call(
        local_kernel,
        [shape(rows, width), shape(rows, width)],
        [ext, pltpu.VMEM((2, rows + TILE, width), F32), pltpu.VMEM((rows, width), F32)],
        proj,
        taps,
        rates,
        res,
        skip,
        flops=3 * 10**9,
    )
    near_states = lax.all_to_all(send, ("zh", "core"), 0, 0, tiled=True)
    send = call(
        functools.partial(chain_kernel, block),
        shape(sizes["y"], order + 2 * TILE, width, dtype=BF16),
        [],
        place,
        taps,
        rates,
        near_states,
    )
    far_states = lax.all_to_all(send, "y", 0, 0, tiled=True)
    piece = shape(n_zl, 2 * block, part, dtype=BF16)
    half_piece = shape(half, 2 * block, part, dtype=BF16)
    hidden, grad_proj, to_right, to_left = call(
        functools.partial(last_kernel, sizes),
        [
            shape(block, width, dtype=BF16),
            shape(3, block, width, dtype=BF16),
            half_piece,
            half_piece,
        ],
        [ext, pltpu.VMEM((3, rows, width), F32)] + held_weights(n_zl // PAIR, part, width),
        place,
        proj,
        taps,
        rates,
        res,
        skip,
        conv,
        grad,
        near_states,
        far_states,
        *weights,
        flops=products(n_zl),
        hbm=2,
    )
    far_right = lax.ppermute(to_right, "x", right)
    far_left = lax.ppermute(to_left, "x", left)
    to_right, to_left = call(
        functools.partial(partials_kernel, sizes, [1, n_x - 1]),
        [piece, piece],
        held_weights(2 * n_zl // PAIR, part, width),
        place,
        hidden,
        grad_proj,
        *weights,
        flops=products(2 * n_zl),
        hbm=2,
    )
    to_right = call(functools.partial(join_kernel, 0), piece, [], to_right, far_right)
    from_left = lax.ppermute(to_right, "x", right)
    to_left = call(functools.partial(join_kernel, half), piece, [], to_left, far_left)
    from_right = lax.ppermute(to_left, "x", left)
    (own,) = call(
        functools.partial(partials_kernel, sizes, [0]),
        [piece],
        held_weights(n_zl // PAIR, part, width),
        place,
        hidden,
        grad_proj,
        *weights,
        flops=products(n_zl),
        hbm=2,
    )
    summed = sum(a.astype(F32) for a in (own, from_left, from_right)).astype(BF16)
    summed = lax.all_to_all(summed, "zl", 0, 0, tiled=True)
    total = jnp.sum(summed.astype(F32), axis=0).astype(BF16)
    return total[:block], total[block:]


def solution(mesh, dims=(8, 4, 2, 4, 4)):
    fine = Mesh(mesh.devices.reshape(dims), CTX + TP)
    sizes = dict(zip(CTX + TP, dims))
    return jax.shard_map(
        functools.partial(shards, sizes),
        mesh=fine,
        in_specs=(
            P(CTX, TP),
            P(CTX, TP),
            P(None, None, TP),
            P(TP, None),
            P(None, TP, None),
            P(TP, None),
            P(TP, None),
            P(TP),
        ),
        out_specs=(P(CTX, TP), P(CTX, TP)),
        check_vma=False,
    )
```

```python
import functools

import jax
import jax.numpy as jnp
from jax import lax
from jax.experimental import pallas as pl
from jax.experimental.pallas import tpu as pltpu
from jax.sharding import Mesh
from jax.sharding import PartitionSpec as P

CTX = ("y", "zh", "core")
TP = ("x", "zl")
TILE = 8
AHEAD = 2
GRANT = 16 * 2**20
PAIR = 2
BF16 = jnp.bfloat16
F32 = jnp.float32


def copy_kernel(tokens, cotangent, copies, sems):
    block = tokens.shape[0]
    moves = []
    for i in range(copies.shape[0]):
        for k, rows in enumerate((tokens, cotangent)):
            there = copies.at[i, pl.ds(k * block, block)]
            moves.append(pltpu.make_async_copy(rows, there, sems.at[i, k]))
            moves[-1].start()
    for move in moves:
        move.wait()


def features(ext, proj_ref, taps_ref, rows, last=None, first=None):
    block, width = proj_ref.shape[1:]
    zero = jnp.zeros((TILE, width), F32)
    out = []
    for p in range(3):
        ext[p, :TILE] = zero
        ext[p, TILE : TILE + block] = proj_ref[p].astype(F32)
        ext[p, TILE + block :] = zero
        if last is not None:
            ext[p, TILE - AHEAD : TILE] = last[AHEAD * p : AHEAD * (p + 1)]
            ext[p, TILE + block : TILE + block + AHEAD] = first[AHEAD * p : AHEAD * (p + 1)]
        total = taps_ref[p, 0:1, :] * ext[p, TILE : TILE + rows]
        for k in range(1, 3):
            total = total + taps_ref[p, k : k + 1, :] * ext[p, TILE - k : TILE - k + rows]
        out.append(total)
    return out


def inner_rows(ext, proj_ref, taps_ref, rows):
    block, width = proj_ref.shape[1:]
    query, key_part, value_part = features(ext, proj_ref, taps_ref, rows)
    row = lax.broadcasted_iota(jnp.int32, (rows, 1), 0)
    inside = (row >= AHEAD) & (row < block)
    back = jnp.concatenate([proj_ref[3].astype(F32), jnp.zeros((TILE, width), F32)], axis=0)
    gated = jnp.where(inside, key_part * value_part, 0.0)
    return gated, jnp.where(inside, back * query, 0.0), row.astype(F32)


def state_kernel(proj_ref, taps_ref, rates_ref, send_ref, ext, pack):
    order = rates_ref.shape[0]
    block = proj_ref.shape[1]
    gated, grad_conv, time = inner_rows(ext, proj_ref, taps_ref, block + TILE)
    for r in range(order):
        rate = rates_ref[r : r + 1, :]
        fwd = jnp.exp(-rate * (block - 1.0 - time)) * gated
        bwd = jnp.exp(-rate * (time - AHEAD)) * grad_conv
        pack[r : r + 1] = jnp.sum(fwd, axis=0, keepdims=True)
        pack[order + r : order + r + 1] = jnp.sum(bwd, axis=0, keepdims=True)
    at = 2 * order
    pack[at + TILE :] = jnp.zeros((TILE, pack.shape[1]), F32)
    for p in range(4):
        rows = proj_ref[p].astype(F32)
        pack[at + AHEAD * p : at + AHEAD * (p + 1)] = rows[:AHEAD]
        if p < 3:
            ends = at + TILE + AHEAD * p
            pack[ends : ends + AHEAD] = rows[block - AHEAD :]
    for i in range(send_ref.shape[0]):
        send_ref[i] = pack[...].astype(BF16)


def joint(taps_ref, first, last):
    row = []
    for p in range(3):
        a, b = first[AHEAD * p : AHEAD * p + 1], first[AHEAD * p + 1 : AHEAD * p + 2]
        c, d = last[AHEAD * p : AHEAD * p + 1], last[AHEAD * p + 1 : AHEAD * p + 2]
        t = [taps_ref[p, k : k + 1, :] for k in range(3)]
        row.append((t[0] * a + t[1] * d + t[2] * c, t[0] * b + t[1] * a + t[2] * d))
    back = (first[3 * AHEAD : 3 * AHEAD + 1], first[3 * AHEAD + 1 : 3 * AHEAD + 2])
    gated = tuple(row[1][i] * row[2][i] for i in range(AHEAD))
    return gated, tuple(back[i] * row[0][i] for i in range(AHEAD))


def fader(rates, block):
    def fade(blocks):
        if isinstance(blocks, int):
            return jnp.exp(-rates * float(block * blocks))
        return jnp.exp(-rates * (block * jnp.maximum(blocks, 0)).astype(F32))

    return fade


def group_states(block, taps_ref, rates, got_ref):
    order = rates.shape[0]
    members = got_ref.shape[0]
    fwd, bwd, firsts, lasts = [], [], [], []
    for j in range(members):
        got = got_ref[j].astype(F32)
        fwd.append(got[:order])
        bwd.append(got[order : 2 * order])
        firsts.append(got[2 * order : 2 * order + TILE])
        lasts.append(got[2 * order + TILE :])
    near, far = jnp.exp(-rates * (block - 2.0)), jnp.exp(-rates * (block - 1.0))
    for j in range(1, members):
        gated, grad_conv = joint(taps_ref, firsts[j], lasts[j - 1])
        fwd[j] = fwd[j] + far * gated[0] + near * gated[1]
        bwd[j - 1] = bwd[j - 1] + near * grad_conv[0] + far * grad_conv[1]
    return fwd, bwd, firsts, lasts, near, far


def chain_kernel(block, place_ref, taps_ref, rates_ref, got_ref, send_ref):
    rates = rates_ref[...]
    order = rates.shape[0]
    fade = fader(rates, block)
    fwd, bwd, firsts, lasts, _, _ = group_states(block, taps_ref, rates, got_ref)
    members = len(fwd)
    total_fwd = sum(fade(members - 1 - j) * fwd[j] for j in range(members))
    total_bwd = sum(fade(j) * bwd[j] for j in range(members))
    ends = jnp.concatenate([firsts[0], lasts[-1]], axis=0).astype(BF16)
    for i in range(send_ref.shape[0]):
        send_ref[i, :order] = jnp.where(place_ref[0] < i, total_fwd, total_bwd).astype(BF16)
        send_ref[i, order:] = ends


def local_kernel(
    proj_ref, taps_ref, rates_ref, res_ref, skip_ref, conv_ref, grad_ref, ext, pad, filt_ref
):
    rows, width = conv_ref.shape
    gated, grad_conv, time = inner_rows(ext, proj_ref, taps_ref, rows)
    taps = jnp.zeros((rows, width), F32)
    for r in range(rates_ref.shape[0]):
        taps = taps + res_ref[r : r + 1, :] * jnp.exp(-rates_ref[r : r + 1, :] * (time + 1.0))
    filt_ref[...] = taps
    zero = jnp.zeros((TILE, width), F32)
    pad[0, :TILE] = zero
    pad[0, TILE:] = gated
    pad[1, :rows] = grad_conv
    pad[1, rows:] = zero
    direct = skip_ref[...] + jnp.sum(res_ref[...], axis=0, keepdims=True)
    for lane in range(0, width, 128):
        lanes = slice(lane, lane + 128)
        total = direct[:, lanes] * pad[0, TILE:, lanes]
        for m in range(1, TILE + 1):
            moved = pad[0, TILE - m : TILE - m + rows, lanes]
            for q in range(0, rows, TILE):
                tap = filt_ref[q + m - 1 : q + m, lanes]
                part = total[q:] + tap * moved[: rows - q]
                total = part if q == 0 else jnp.concatenate([total[:q], part], axis=0)
        conv_ref[:, lanes] = total
        total = direct[:, lanes] * pad[1, :rows, lanes]
        for m in range(1, TILE + 1):
            moved = pad[1, m : m + rows, lanes]
            for q in range(0, rows, TILE):
                tap = filt_ref[q + m - 1 : q + m, lanes]
                part = total[: rows - q] + tap * moved[q:]
                total = part if q == 0 else jnp.concatenate([part, total[rows - q :]], axis=0)
        grad_ref[:, lanes] = total


def finish_kernel(
    place_ref, proj_ref, taps_ref, rates_ref, res_ref, skip_ref, conv_ref, grad_ref,
    near_ref, far_ref, hidden_ref, out_ref, ext, feat,
):
    rates = rates_ref[...]
    res_all = res_ref[...]
    skip = skip_ref[...]
    order, width = rates.shape
    rows = conv_ref.shape[0]
    block = rows - TILE
    group, member = place_ref[0], place_ref[1]
    groups, members = far_ref.shape[0], near_ref.shape[0]
    fade = fader(rates, block)
    fwd, bwd, firsts, lasts, near, far = group_states(block, taps_ref, rates, near_ref)

    def rows_of(ref, index, start, there):
        got = ref[jnp.where(there, index, 0)].astype(F32)
        return jnp.where(there, got[start : start + TILE], 0.0)

    nothing = jnp.zeros((TILE, width), F32)
    whole = [far_ref[i].astype(F32) for i in range(groups)]
    head = [w[order : order + TILE] for w in whole] + [nothing]
    tail = [nothing] + [w[order + TILE :] for w in whole]
    ahead = jnp.zeros_like(rates)
    behind = jnp.zeros_like(rates)
    for i in range(groups):
        gated, _ = joint(taps_ref, head[i], tail[i])
        total = whole[i][:order] + fade(members - 1) * (far * gated[0] + near * gated[1])
        ahead = ahead + jnp.where(i < group, fade(members * (group - 1 - i)) * total, 0.0)
        _, grad_conv = joint(taps_ref, head[i + 1], tail[i + 1])
        total = whole[i][:order] + fade(members - 1) * (near * grad_conv[0] + far * grad_conv[1])
        behind = behind + jnp.where(i > group, fade(members * (i - 1 - group)) * total, 0.0)
    tail_before = rows_of(far_ref, group - 1, order + TILE, group > 0)
    head_behind = rows_of(far_ref, group + 1, order, group < groups - 1)
    gated, _ = joint(taps_ref, firsts[0], tail_before)
    _, grad_conv = joint(taps_ref, head_behind, lasts[-1])
    fwd[0] = fwd[0] + far * gated[0] + near * gated[1]
    bwd[-1] = bwd[-1] + near * grad_conv[0] + far * grad_conv[1]
    ahead = fade(member) * ahead
    behind = fade(members - 1 - member) * behind
    for j in range(members):
        ahead = ahead + jnp.where(j < member, fade(member - 1 - j) * fwd[j], 0.0)
        behind = behind + jnp.where(j > member, fade(j - 1 - member) * bwd[j], 0.0)

    last = rows_of(near_ref, member - 1, 2 * order + TILE, member > 0)
    last = jnp.where(member > 0, last, tail_before)
    first = rows_of(near_ref, member + 1, 2 * order, member < members - 1)
    first = jnp.where(member < members - 1, first, head_behind)
    query, key_part, value_part = features(ext, proj_ref, taps_ref, rows, last, first)
    row = lax.broadcasted_iota(jnp.int32, (TILE, 1), 0)
    next_back = jnp.where(row < AHEAD, pltpu.roll(first, AHEAD, 0), 0.0)
    back = jnp.concatenate([proj_ref[3].astype(F32), next_back], axis=0)
    gated = key_part * value_part
    grad_conv = back * query

    g = [gated[i : i + 1] for i in (0, 1, block, block + 1)]
    h = [grad_conv[i : i + 1] for i in (0, 1, block, block + 1)]
    grow = jnp.exp(rates)
    ahead = ahead + grow * g[0] + (grow * grow) * g[1]
    behind = behind + (grow * grow) * h[2] + grow * h[3]
    lag0 = skip + jnp.sum(res_all, axis=0, keepdims=True)
    lag1 = jnp.sum(res_all * jnp.exp(-rates), axis=0, keepdims=True)
    less = jnp.sum(res_all * grow, axis=0, keepdims=True)

    def two(a, b):
        return jnp.where(row == 0, a, jnp.where(row == 1, b, 0.0))

    def with_ends(array, top, bottom):
        return jnp.concatenate(
            [array[:TILE] + top, array[TILE:block], array[block:] + bottom], axis=0
        )

    conv_out = with_ends(
        conv_ref[...],
        two(skip * g[0] - less * g[1], skip * g[1]),
        two(lag0 * g[2], lag0 * g[3] + lag1 * g[2]),
    )
    grad_gated = with_ends(
        grad_ref[...],
        two(lag0 * h[0] + lag1 * h[1], lag0 * h[1]),
        two(skip * h[2], skip * h[3] - less * h[2]),
    )
    time = lax.broadcasted_iota(jnp.int32, (rows, 1), 0).astype(F32)
    ahead = res_all * ahead
    behind = res_all * behind
    for r in range(order):
        rate = rates[r : r + 1]
        conv_out = conv_out + ahead[r : r + 1] * jnp.exp(-rate * (time + 1.0))
        past = jnp.exp(-rate * (block + AHEAD - time))
        grad_gated = grad_gated + behind[r : r + 1] * past
    hidden_ref[...] = (query * conv_out)[:block].astype(BF16)
    feat[0] = back * conv_out
    feat[1] = grad_gated * value_part
    feat[2] = grad_gated * key_part
    for p in range(3):
        total = taps_ref[p, 0:1, :] * feat[p, :block]
        for k in range(1, 3):
            total = total + taps_ref[p, k : k + 1, :] * feat[p, k : k + block]
        out_ref[p] = total.astype(BF16)


def in_hbm(array):
    return pltpu.with_memory_space_constraint(array, pltpu.HBM)


def call(kernel, outs, scratch, *args, flops=0, hbm=0):
    whole = pl.BlockSpec(memory_space=pltpu.VMEM)
    far = pl.BlockSpec(memory_space=pltpu.HBM)
    scalar = pl.BlockSpec(memory_space=pltpu.SMEM)
    specs = [
        scalar if a.dtype == jnp.int32 else far if i >= len(args) - hbm else whole
        for i, a in enumerate(args)
    ]
    cost = pl.CostEstimate(flops=flops, bytes_accessed=0, transcendentals=0) if flops else None
    return pl.pallas_call(
        kernel,
        out_shape=outs,
        scratch_shapes=scratch,
        in_specs=specs,
        out_specs=jax.tree.map(lambda _: whole, outs),
        cost_estimate=cost,
        compiler_params=pltpu.CompilerParams(vmem_limit_bytes=GRANT),
    )(*args)


def load_weights(blocks, weight_in, weight_out, held_in, held_out, sems, ahead=2):
    span = held_in.shape[1]
    width = weight_out.shape[0]
    part = span // PAIR
    copies = []
    for s, block in enumerate(blocks):
        at = pl.ds(pl.multiple_of(block * part, part), span)
        moves = [
            pltpu.make_async_copy(
                weight_in.at[p, at, :],
                held_in.at[s, :, pl.ds(p * width, width)],
                sems.at[s, p],
            )
            for p in range(3)
        ]
        moves.append(
            pltpu.make_async_copy(weight_out.at[:, at], held_out.at[s], sems.at[s, 3])
        )
        copies.append(moves)

    def start(s):
        for copy in copies[s]:
            copy.start()

    for s in range(min(ahead, len(copies))):
        start(s)

    def ready(s):
        for copy in copies[s]:
            copy.wait()
        if s + ahead < len(copies):
            start(s + ahead)

    return ready


def held_weights(count, part, width):
    return [
        pltpu.VMEM((count, PAIR * part, 3 * width), BF16),
        pltpu.VMEM((count, width, PAIR * part), BF16),
        pltpu.SemaphoreType.DMA((count, 4)),
    ]


def set_base(sizes, place, steps):
    n_x, n_zl = sizes["x"], sizes["zl"]
    x, core = place[2], place[3]
    return lax.rem(x + jnp.where(core == 0, n_x - steps, steps), n_x) * n_zl


def project(sizes, steps, place, pieces, weights, old, total, held_in, held_out, sems):
    block = pieces.shape[1] // 2
    width = total.shape[2]
    starts = range(0, pieces.shape[0], PAIR)
    base = set_base(sizes, place, steps)
    ready = load_weights([base + j for j in starts], *weights, held_in, held_out, sems)
    for s, j in enumerate(starts):
        run = range(j, j + PAIR)
        part_in = jnp.concatenate([pieces[i, :block] for i in run], axis=1)
        part_grad = jnp.concatenate([pieces[i, block:] for i in run], axis=1)
        ready(s)
        term = jnp.dot(part_in, held_in[s], preferred_element_type=F32)
        back = lax.dot_general(
            part_grad, held_out[s], (((1,), (1,)), ((), ())), preferred_element_type=F32
        )
        terms = [term[:, p * width : (p + 1) * width] for p in range(3)] + [back]
        for p in range(4):
            if s == 0 and old is None:
                total[p] = terms[p]
            else:
                total[p] = (old if s == 0 else total)[p] + terms[p]


def first_kernel(sizes, place, pieces, weight_in, weight_out, total, *held):
    project(sizes, 0, place, pieces, (weight_in, weight_out), None, total, *held)


def next_kernel(sizes, steps, place, pieces, old, weight_in, weight_out, total, *held):
    project(sizes, steps, place, pieces, (weight_in, weight_out), old, total, *held)


def far_kernel(
    sizes, steps, place, pieces, old, taps, rates, weight_in, weight_out,
    proj, send, total, ext, pack, *held,
):
    project(sizes, steps, place, pieces, (weight_in, weight_out), old, total, *held)
    proj[...] = total[...].astype(BF16)
    state_kernel(proj, taps, rates, send, ext, pack)


def partials(held, out, hidden, grad, ready):
    held_in, held_out = held[:2]
    block = hidden.shape[0]
    part = out.shape[2]
    for j in range(0, out.shape[0], PAIR):
        s = j // PAIR
        grads = jnp.concatenate([grad[p] for p in range(3)], axis=1)
        ready(s)
        mixed = jnp.dot(hidden[...], held_out[s], preferred_element_type=F32)
        total = lax.dot_general(
            grads, held_in[s], (((1,), (1,)), ((), ())), preferred_element_type=F32
        )
        for i in range(PAIR):
            out[j + i, :block] = mixed[:, i * part : (i + 1) * part].astype(BF16)
            out[j + i, block:] = total[:, i * part : (i + 1) * part].astype(BF16)


def partials_kernel(sizes, steps, place, hidden, grad, weight_in, weight_out, out, *held):
    base = set_base(sizes, place, steps)
    starts = range(0, out.shape[0], PAIR)
    ready = load_weights([base + j for j in starts], weight_in, weight_out, *held)
    partials(held, out, hidden, grad, ready)


def last_kernel(
    sizes, place, proj, taps, rates, res, skip, conv, grad, near, far, weight_in, weight_out,
    hidden, out, terms, ext, feat, *held,
):
    base = set_base(sizes, place, 1)
    starts = range(0, terms.shape[0], PAIR)
    ready = load_weights([base + j for j in starts], weight_in, weight_out, *held)
    finish_kernel(
        place, proj, taps, rates, res, skip, conv, grad, near, far, hidden, out, ext, feat
    )
    partials(held, terms, hidden, out, ready)


def shape(*dims, dtype=F32):
    return jax.ShapeDtypeStruct(dims, dtype)


def shards(
    sizes,
    tokens,
    cotangent,
    input_weight,
    output_weight,
    short_taps,
    residues,
    decay_rates,
    skip_gain,
):
    n_x, n_zl = sizes["x"], sizes["zl"]
    block, part = tokens.shape
    width = output_weight.shape[0]
    order = residues.shape[1]
    rows = block + TILE
    taps = short_taps.transpose(0, 2, 1)
    rates = decay_rates.T
    res = residues.T
    skip = skip_gain[None]
    place = jnp.stack(
        [
            lax.axis_index("y"),
            lax.axis_index("zh") * sizes["core"] + lax.axis_index("core"),
            lax.axis_index("x"),
            lax.axis_index("core"),
        ]
    ).astype(jnp.int32)
    copies = call(
        copy_kernel,
        shape(n_zl, 2 * block, part, dtype=BF16),
        [pltpu.SemaphoreType.DMA((n_zl, 2))],
        in_hbm(tokens),
        in_hbm(cotangent),
        hbm=2,
    )
    pieces = lax.all_to_all(copies, "zl", 0, 0, tiled=True)
    ring = [
        (c * n_x + i, c * n_x + (i + 1 - 2 * c) % n_x) for c in range(2) for i in range(n_x)
    ]

    def onward(array):
        return lax.ppermute(array, ("core", "x"), ring)

    def products(count):
        return 8 * count * block * part * width

    right = [(i, (i + 1) % n_x) for i in range(n_x)]
    left = [(i, (i - 1) % n_x) for i in range(n_x)]
    weights = (in_hbm(input_weight.transpose(1, 0, 2)), in_hbm(output_weight))
    held = held_weights(n_zl // PAIR, part, width)
    arrived = onward(pieces)
    total = call(
        functools.partial(first_kernel, sizes),
        shape(4, block, width),
        held,
        place,
        pieces,
        *weights,
        flops=products(n_zl),
        hbm=2,
    )
    for step in range(1, n_x - 1):
        arrived, total = lax.optimization_barrier((arrived, total))
        following = onward(arrived)
        total = call(
            functools.partial(next_kernel, sizes, step),
            shape(4, block, width),
            held,
            place,
            arrived,
            total,
            *weights,
            flops=products(n_zl),
            hbm=2,
        )
        arrived = following
    ext = pltpu.VMEM((3, rows + TILE, width), F32)
    members = sizes["zh"] * sizes["core"]
    pack = 2 * order + 2 * TILE
    proj, send = call(
        functools.partial(far_kernel, sizes, n_x - 1),
        [shape(4, block, width, dtype=BF16), shape(members, pack, width, dtype=BF16)],
        [pltpu.VMEM((4, block, width), F32), ext, pltpu.VMEM((pack, width), F32)]
        + held,
        place,
        arrived,
        total,
        taps,
        rates,
        *weights,
        flops=products(n_zl),
        hbm=2,
    )
    conv, grad = call(
        local_kernel,
        [shape(rows, width), shape(rows, width)],
        [ext, pltpu.VMEM((2, rows + TILE, width), F32), pltpu.VMEM((rows, width), F32)],
        proj,
        taps,
        rates,
        res,
        skip,
        flops=3 * 10**9,
    )
    near_states = lax.all_to_all(send, ("zh", "core"), 0, 0, tiled=True)
    send = call(
        functools.partial(chain_kernel, block),
        shape(sizes["y"], order + 2 * TILE, width, dtype=BF16),
        [],
        place,
        taps,
        rates,
        near_states,
    )
    far_states = lax.all_to_all(send, "y", 0, 0, tiled=True)
    piece = shape(n_zl, 2 * block, part, dtype=BF16)
    hidden, grad_proj, terms = call(
        functools.partial(last_kernel, sizes),
        [
            shape(block, width, dtype=BF16),
            shape(3, block, width, dtype=BF16),
            piece,
        ],
        [ext, pltpu.VMEM((3, rows, width), F32)] + held,
        place,
        proj,
        taps,
        rates,
        res,
        skip,
        conv,
        grad,
        near_states,
        far_states,
        *weights,
        flops=products(n_zl),
        hbm=2,
    )
    for step in range(2, n_x + 1):
        got = onward(terms)
        own = call(
            functools.partial(partials_kernel, sizes, step % n_x),
            piece,
            held,
            place,
            hidden,
            grad_proj,
            *weights,
            flops=products(n_zl),
            hbm=2,
        )
        got, place = lax.optimization_barrier((got, place))
        terms = (own.astype(F32) + got.astype(F32)).astype(BF16)
    summed = terms
    summed = lax.all_to_all(summed, "zl", 0, 0, tiled=True)
    total = jnp.sum(summed.astype(F32), axis=0).astype(BF16)
    return total[:block], total[block:]


def solution(mesh, dims=(8, 4, 2, 4, 4)):
    fine = Mesh(mesh.devices.reshape(dims), CTX + TP)
    sizes = dict(zip(CTX + TP, dims))
    return jax.shard_map(
        functools.partial(shards, sizes),
        mesh=fine,
        in_specs=(
            P(CTX, TP),
            P(CTX, TP),
            P(None, None, TP),
            P(TP, None),
            P(None, TP, None),
            P(TP, None),
            P(TP, None),
            P(TP),
        ),
        out_specs=(P(CTX, TP), P(CTX, TP)),
        check_vma=False,
    )
```

```python
import functools

import jax
import jax.numpy as jnp
from jax import lax
from jax.experimental import pallas as pl
from jax.experimental.pallas import tpu as pltpu
from jax.sharding import Mesh
from jax.sharding import PartitionSpec as P

CTX = ("y", "zh", "core")
TP = ("x", "zl")
TILE = 8
AHEAD = 2
GRANT = 16 * 2**20
PAIR = 2
BF16 = jnp.bfloat16
F32 = jnp.float32


def copy_kernel(tokens, cotangent, copies, sems):
    block = tokens.shape[0]
    moves = []
    for i in range(copies.shape[0]):
        for k, rows in enumerate((tokens, cotangent)):
            there = copies.at[i, pl.ds(k * block, block)]
            moves.append(pltpu.make_async_copy(rows, there, sems.at[i, k]))
            moves[-1].start()
    for move in moves:
        move.wait()


def features(ext, proj_ref, taps_ref, rows, last=None, first=None):
    block, width = proj_ref.shape[1:]
    zero = jnp.zeros((TILE, width), F32)
    out = []
    for p in range(3):
        ext[p, :TILE] = zero
        ext[p, TILE : TILE + block] = proj_ref[p].astype(F32)
        ext[p, TILE + block :] = zero
        if last is not None:
            ext[p, TILE - AHEAD : TILE] = last[AHEAD * p : AHEAD * (p + 1)]
            ext[p, TILE + block : TILE + block + AHEAD] = first[AHEAD * p : AHEAD * (p + 1)]
        total = taps_ref[p, 0:1, :] * ext[p, TILE : TILE + rows]
        for k in range(1, 3):
            total = total + taps_ref[p, k : k + 1, :] * ext[p, TILE - k : TILE - k + rows]
        out.append(total)
    return out


def inner_rows(ext, proj_ref, taps_ref, rows):
    block, width = proj_ref.shape[1:]
    query, key_part, value_part = features(ext, proj_ref, taps_ref, rows)
    row = lax.broadcasted_iota(jnp.int32, (rows, 1), 0)
    inside = (row >= AHEAD) & (row < block)
    back = jnp.concatenate([proj_ref[3].astype(F32), jnp.zeros((TILE, width), F32)], axis=0)
    gated = jnp.where(inside, key_part * value_part, 0.0)
    return gated, jnp.where(inside, back * query, 0.0), row.astype(F32)


def state_kernel(proj_ref, taps_ref, rates_ref, send_ref, ext, pack):
    order = rates_ref.shape[0]
    block = proj_ref.shape[1]
    gated, grad_conv, time = inner_rows(ext, proj_ref, taps_ref, block + TILE)
    time = time[:TILE]
    for r in range(order):
        rate = rates_ref[r : r + 1, :]
        fade = jnp.exp(-rate * TILE)
        fwd = gated[:TILE]
        bwd = grad_conv[block - TILE : block]
        for q in range(TILE, block, TILE):
            fwd = fwd * fade + gated[q : q + TILE]
            bwd = bwd * fade + grad_conv[block - TILE - q : block - q]
        fwd = jnp.exp(-rate * (TILE - 1.0 - time)) * fwd
        bwd = jnp.exp(-rate * (time - AHEAD)) * bwd
        pack[r : r + 1] = jnp.sum(fwd, axis=0, keepdims=True)
        pack[order + r : order + r + 1] = jnp.sum(bwd, axis=0, keepdims=True)
    at = 2 * order
    pack[at + TILE :] = jnp.zeros((TILE, pack.shape[1]), F32)
    for p in range(4):
        rows = proj_ref[p].astype(F32)
        pack[at + AHEAD * p : at + AHEAD * (p + 1)] = rows[:AHEAD]
        if p < 3:
            ends = at + TILE + AHEAD * p
            pack[ends : ends + AHEAD] = rows[block - AHEAD :]
    for i in range(send_ref.shape[0]):
        send_ref[i] = pack[...].astype(BF16)


def joint(taps_ref, first, last):
    row = []
    for p in range(3):
        a, b = first[AHEAD * p : AHEAD * p + 1], first[AHEAD * p + 1 : AHEAD * p + 2]
        c, d = last[AHEAD * p : AHEAD * p + 1], last[AHEAD * p + 1 : AHEAD * p + 2]
        t = [taps_ref[p, k : k + 1, :] for k in range(3)]
        row.append((t[0] * a + t[1] * d + t[2] * c, t[0] * b + t[1] * a + t[2] * d))
    back = (first[3 * AHEAD : 3 * AHEAD + 1], first[3 * AHEAD + 1 : 3 * AHEAD + 2])
    gated = tuple(row[1][i] * row[2][i] for i in range(AHEAD))
    return gated, tuple(back[i] * row[0][i] for i in range(AHEAD))


def fader(rates, block):
    def fade(blocks):
        if isinstance(blocks, int):
            return jnp.exp(-rates * float(block * blocks))
        return jnp.exp(-rates * (block * jnp.maximum(blocks, 0)).astype(F32))

    return fade


def group_states(block, taps_ref, rates, got_ref):
    order = rates.shape[0]
    members = got_ref.shape[0]
    fwd, bwd, firsts, lasts = [], [], [], []
    for j in range(members):
        got = got_ref[j].astype(F32)
        fwd.append(got[:order])
        bwd.append(got[order : 2 * order])
        firsts.append(got[2 * order : 2 * order + TILE])
        lasts.append(got[2 * order + TILE :])
    near, far = jnp.exp(-rates * (block - 2.0)), jnp.exp(-rates * (block - 1.0))
    for j in range(1, members):
        gated, grad_conv = joint(taps_ref, firsts[j], lasts[j - 1])
        fwd[j] = fwd[j] + far * gated[0] + near * gated[1]
        bwd[j - 1] = bwd[j - 1] + near * grad_conv[0] + far * grad_conv[1]
    return fwd, bwd, firsts, lasts, near, far


def chain_kernel(block, place_ref, taps_ref, rates_ref, got_ref, send_ref):
    rates = rates_ref[...]
    order = rates.shape[0]
    fade = fader(rates, block)
    fwd, bwd, firsts, lasts, _, _ = group_states(block, taps_ref, rates, got_ref)
    members = len(fwd)
    step = fade(1)
    total_fwd, total_bwd = fwd[0], bwd[-1]
    for j in range(1, members):
        total_fwd = total_fwd * step + fwd[j]
        total_bwd = total_bwd * step + bwd[members - 1 - j]
    ends = jnp.concatenate([firsts[0], lasts[-1]], axis=0).astype(BF16)
    for i in range(send_ref.shape[0]):
        send_ref[i, :order] = jnp.where(place_ref[0] < i, total_fwd, total_bwd).astype(BF16)
        send_ref[i, order:] = ends


def local_kernel(
    proj_ref, taps_ref, rates_ref, res_ref, skip_ref, conv_ref, grad_ref, ext, pad, filt_ref
):
    rows, width = conv_ref.shape
    gated, grad_conv, time = inner_rows(ext, proj_ref, taps_ref, rows)
    taps = jnp.zeros((rows, width), F32)
    for r in range(rates_ref.shape[0]):
        taps = taps + res_ref[r : r + 1, :] * jnp.exp(-rates_ref[r : r + 1, :] * (time + 1.0))
    filt_ref[...] = taps
    zero = jnp.zeros((TILE, width), F32)
    pad[0, :TILE] = zero
    pad[0, TILE:] = gated
    pad[1, :rows] = grad_conv
    pad[1, rows:] = zero
    direct = skip_ref[...] + jnp.sum(res_ref[...], axis=0, keepdims=True)
    for lane in range(0, width, 128):
        lanes = slice(lane, lane + 128)
        total = direct[:, lanes] * pad[0, TILE:, lanes]
        for m in range(1, TILE + 1):
            moved = pad[0, TILE - m : TILE - m + rows, lanes]
            for q in range(0, rows, TILE):
                tap = filt_ref[q + m - 1 : q + m, lanes]
                part = total[q:] + tap * moved[: rows - q]
                total = part if q == 0 else jnp.concatenate([total[:q], part], axis=0)
        conv_ref[:, lanes] = total
        total = direct[:, lanes] * pad[1, :rows, lanes]
        for m in range(1, TILE + 1):
            moved = pad[1, m : m + rows, lanes]
            for q in range(0, rows, TILE):
                tap = filt_ref[q + m - 1 : q + m, lanes]
                part = total[: rows - q] + tap * moved[q:]
                total = part if q == 0 else jnp.concatenate([part, total[rows - q :]], axis=0)
        grad_ref[:, lanes] = total


def finish_kernel(
    place_ref, proj_ref, taps_ref, rates_ref, res_ref, skip_ref, conv_ref, grad_ref,
    near_ref, far_ref, hidden_ref, out_ref, ext, feat,
):
    rates = rates_ref[...]
    res_all = res_ref[...]
    skip = skip_ref[...]
    order, width = rates.shape
    rows = conv_ref.shape[0]
    block = rows - TILE
    group, member = place_ref[0], place_ref[1]
    groups, members = far_ref.shape[0], near_ref.shape[0]
    fade = fader(rates, block)
    fwd, bwd, firsts, lasts, near, far = group_states(block, taps_ref, rates, near_ref)

    def rows_of(ref, index, start, there):
        got = ref[jnp.where(there, index, 0)].astype(F32)
        return jnp.where(there, got[start : start + TILE], 0.0)

    nothing = jnp.zeros((TILE, width), F32)
    whole = [far_ref[i].astype(F32) for i in range(groups)]
    head = [w[order : order + TILE] for w in whole] + [nothing]
    tail = [nothing] + [w[order + TILE :] for w in whole]
    ahead = jnp.zeros_like(rates)
    behind = jnp.zeros_like(rates)
    step, stride, most = fade(1), fade(members), fade(members - 1)
    for i in range(groups):
        gated, _ = joint(taps_ref, head[i], tail[i])
        total = whole[i][:order] + most * (far * gated[0] + near * gated[1])
        ahead = jnp.where(i < group, ahead * stride + total, ahead)
        j = groups - 1 - i
        _, grad_conv = joint(taps_ref, head[j + 1], tail[j + 1])
        total = whole[j][:order] + most * (near * grad_conv[0] + far * grad_conv[1])
        behind = jnp.where(j > group, behind * stride + total, behind)
    tail_before = rows_of(far_ref, group - 1, order + TILE, group > 0)
    head_behind = rows_of(far_ref, group + 1, order, group < groups - 1)
    gated, _ = joint(taps_ref, firsts[0], tail_before)
    _, grad_conv = joint(taps_ref, head_behind, lasts[-1])
    fwd[0] = fwd[0] + far * gated[0] + near * gated[1]
    bwd[-1] = bwd[-1] + near * grad_conv[0] + far * grad_conv[1]
    for j in range(members):
        ahead = jnp.where(j < member, ahead * step + fwd[j], ahead)
        i = members - 1 - j
        behind = jnp.where(i > member, behind * step + bwd[i], behind)

    last = rows_of(near_ref, member - 1, 2 * order + TILE, member > 0)
    last = jnp.where(member > 0, last, tail_before)
    first = rows_of(near_ref, member + 1, 2 * order, member < members - 1)
    first = jnp.where(member < members - 1, first, head_behind)
    query, key_part, value_part = features(ext, proj_ref, taps_ref, rows, last, first)
    row = lax.broadcasted_iota(jnp.int32, (TILE, 1), 0)
    next_back = jnp.where(row < AHEAD, pltpu.roll(first, AHEAD, 0), 0.0)
    back = jnp.concatenate([proj_ref[3].astype(F32), next_back], axis=0)
    gated = key_part * value_part
    grad_conv = back * query

    g = [gated[i : i + 1] for i in (0, 1, block, block + 1)]
    h = [grad_conv[i : i + 1] for i in (0, 1, block, block + 1)]
    grow = jnp.exp(rates)
    ahead = ahead + grow * g[0] + (grow * grow) * g[1]
    behind = behind + (grow * grow) * h[2] + grow * h[3]
    lag0 = skip + jnp.sum(res_all, axis=0, keepdims=True)
    lag1 = jnp.sum(res_all * jnp.exp(-rates), axis=0, keepdims=True)
    less = jnp.sum(res_all * grow, axis=0, keepdims=True)

    def two(a, b):
        return jnp.where(row == 0, a, jnp.where(row == 1, b, 0.0))

    def with_ends(array, top, bottom):
        return jnp.concatenate(
            [array[:TILE] + top, array[TILE:block], array[block:] + bottom], axis=0
        )

    conv_out = with_ends(
        conv_ref[...],
        two(skip * g[0] - less * g[1], skip * g[1]),
        two(lag0 * g[2], lag0 * g[3] + lag1 * g[2]),
    )
    grad_gated = with_ends(
        grad_ref[...],
        two(lag0 * h[0] + lag1 * h[1], lag0 * h[1]),
        two(skip * h[2], skip * h[3] - less * h[2]),
    )
    time = row.astype(F32)
    ahead = res_all * ahead
    behind = res_all * behind
    conv_tiles = [[] for _ in range(0, rows, TILE)]
    grad_tiles = [[] for _ in range(0, rows, TILE)]
    for lane in range(0, width, 128):
        lanes = slice(lane, lane + 128)
        conv_sum = [conv_out[q : q + TILE, lanes] for q in range(0, rows, TILE)]
        grad_sum = [grad_gated[q : q + TILE, lanes] for q in range(0, rows, TILE)]
        for r in range(order):
            rate = rates[r : r + 1, lanes]
            fall = jnp.exp(-rate * TILE)
            later = ahead[r : r + 1, lanes] * jnp.exp(-rate * (time + 1.0))
            sooner = behind[r : r + 1, lanes] * jnp.exp(-rate * (AHEAD - time))
            for q in range(len(conv_sum)):
                conv_sum[q] = conv_sum[q] + later
                grad_sum[-1 - q] = grad_sum[-1 - q] + sooner
                later = later * fall
                sooner = sooner * fall
        for q in range(len(conv_sum)):
            conv_tiles[q].append(conv_sum[q])
            grad_tiles[q].append(grad_sum[q])
    conv_out = jnp.concatenate([jnp.concatenate(t, axis=1) for t in conv_tiles], axis=0)
    grad_gated = jnp.concatenate([jnp.concatenate(t, axis=1) for t in grad_tiles], axis=0)
    hidden_ref[...] = (query * conv_out)[:block].astype(BF16)
    feat[0] = back * conv_out
    feat[1] = grad_gated * value_part
    feat[2] = grad_gated * key_part
    for p in range(3):
        total = taps_ref[p, 0:1, :] * feat[p, :block]
        for k in range(1, 3):
            total = total + taps_ref[p, k : k + 1, :] * feat[p, k : k + block]
        out_ref[p] = total.astype(BF16)


def in_hbm(array):
    return pltpu.with_memory_space_constraint(array, pltpu.HBM)


def call(kernel, outs, scratch, *args, flops=0, hbm=0):
    whole = pl.BlockSpec(memory_space=pltpu.VMEM)
    far = pl.BlockSpec(memory_space=pltpu.HBM)
    scalar = pl.BlockSpec(memory_space=pltpu.SMEM)
    specs = [
        scalar if a.dtype == jnp.int32 else far if i >= len(args) - hbm else whole
        for i, a in enumerate(args)
    ]
    cost = pl.CostEstimate(flops=flops, bytes_accessed=0, transcendentals=0) if flops else None
    return pl.pallas_call(
        kernel,
        out_shape=outs,
        scratch_shapes=scratch,
        in_specs=specs,
        out_specs=jax.tree.map(lambda _: whole, outs),
        cost_estimate=cost,
        compiler_params=pltpu.CompilerParams(vmem_limit_bytes=GRANT),
    )(*args)


def load_weights(blocks, weight_in, weight_out, held_in, held_out, sems, ahead=2):
    span = held_in.shape[1]
    width = weight_out.shape[0]
    part = span // PAIR
    copies = []
    for s, block in enumerate(blocks):
        at = pl.ds(pl.multiple_of(block * part, part), span)
        moves = [
            pltpu.make_async_copy(
                weight_in.at[p, at, :],
                held_in.at[s, :, pl.ds(p * width, width)],
                sems.at[s, p],
            )
            for p in range(3)
        ]
        moves.append(
            pltpu.make_async_copy(weight_out.at[:, at], held_out.at[s], sems.at[s, 3])
        )
        copies.append(moves)

    def start(s):
        for copy in copies[s]:
            copy.start()

    for s in range(min(ahead, len(copies))):
        start(s)

    def ready(s):
        for copy in copies[s]:
            copy.wait()
        if s + ahead < len(copies):
            start(s + ahead)

    return ready


def held_weights(count, part, width):
    return [
        pltpu.VMEM((count, PAIR * part, 3 * width), BF16),
        pltpu.VMEM((count, width, PAIR * part), BF16),
        pltpu.SemaphoreType.DMA((count, 4)),
    ]


def project(sizes, offsets, place_ref, pieces, weights, old, total, held_in, held_out, sems):
    n_x, n_zl = sizes["x"], sizes["zl"]
    block = pieces[0].shape[1] // 2
    width = total.shape[2]
    work = [
        (piece, j, lax.rem(place_ref[2] + k, n_x) * n_zl + start + j)
        for piece, (k, start) in zip(pieces, offsets)
        for j in range(0, piece.shape[0], PAIR)
    ]
    ready = load_weights([w[2] for w in work], *weights, held_in, held_out, sems)
    for s, (piece, j, _) in enumerate(work):
        run = range(j, j + PAIR)
        part_in = jnp.concatenate([piece[i, :block] for i in run], axis=1)
        part_grad = jnp.concatenate([piece[i, block:] for i in run], axis=1)
        ready(s)
        term = jnp.dot(part_in, held_in[s], preferred_element_type=F32)
        back = lax.dot_general(
            part_grad, held_out[s], (((1,), (1,)), ((), ())), preferred_element_type=F32
        )
        terms = [term[:, p * width : (p + 1) * width] for p in range(3)] + [back]
        for p in range(4):
            if s == 0 and old is None:
                total[p] = terms[p]
            else:
                total[p] = (old if s == 0 else total)[p] + terms[p]


def near_kernel(sizes, place, piece, weight_in, weight_out, total, *held):
    project(sizes, [(0, 0)], place, [piece], (weight_in, weight_out), None, total, *held)


def side_kernel(sizes, place, left, right, old, weight_in, weight_out, total, *held):
    offsets = [(sizes["x"] - 1, 0), (1, 0)]
    weights = (weight_in, weight_out)
    project(sizes, offsets, place, [left, right], weights, old, total, *held)


def far_kernel(
    sizes, place, left, right, old, taps, rates, weight_in, weight_out, proj, send, total, ext, pack, *held
):
    offsets = [(2, 0), (2, left.shape[0])]
    weights = (weight_in, weight_out)
    project(sizes, offsets, place, [left, right], weights, old, total, *held)
    proj[...] = total[...].astype(BF16)
    state_kernel(proj, taps, rates, send, ext, pack)


def partials(held, start, out, hidden, grad, ready):
    held_in, held_out = held[:2]
    block = hidden.shape[0]
    part = out.shape[2]
    for j in range(0, out.shape[0], PAIR):
        s = start + j // PAIR
        grads = jnp.concatenate([grad[p] for p in range(3)], axis=1)
        ready(s)
        mixed = jnp.dot(hidden[...], held_out[s], preferred_element_type=F32)
        total = lax.dot_general(
            grads, held_in[s], (((1,), (1,)), ((), ())), preferred_element_type=F32
        )
        for i in range(PAIR):
            out[j + i, :block] = mixed[:, i * part : (i + 1) * part].astype(BF16)
            out[j + i, block:] = total[:, i * part : (i + 1) * part].astype(BF16)


def partials_kernel(sizes, offsets, place, hidden, grad, weight_in, weight_out, *refs):
    outs, held = refs[:-3], refs[-3:]
    n_x, n_zl = sizes["x"], sizes["zl"]
    blocks = [
        lax.rem(place[2] + k, n_x) * n_zl + j
        for k, out in zip(offsets, outs)
        for j in range(0, out.shape[0], PAIR)
    ]
    ready = load_weights(blocks, weight_in, weight_out, *held)
    start = 0
    for out in outs:
        partials(held, start, out, hidden, grad, ready)
        start += out.shape[0] // PAIR


def last_kernel(
    sizes, place, proj, taps, rates, res, skip, conv, grad, near, far, weight_in, weight_out,
    hidden, out, to_right, to_left, ext, feat, *held,
):
    n_x, n_zl = sizes["x"], sizes["zl"]
    blocks = [lax.rem(place[2] + 2, n_x) * n_zl + j for j in range(0, n_zl, PAIR)]
    ready = load_weights(blocks, weight_in, weight_out, *held)
    finish_kernel(
        place, proj, taps, rates, res, skip, conv, grad, near, far, hidden, out, ext, feat
    )
    partials(held, 0, to_right, hidden, out, ready)
    partials(held, to_right.shape[0] // PAIR, to_left, hidden, out, ready)


def join_kernel(start, terms, got, out):
    count = got.shape[0]
    for i in range(terms.shape[0]):
        if start <= i < start + count:
            both = terms[i].astype(F32) + got[i - start].astype(F32)
            out[i] = both.astype(BF16)
        else:
            out[i] = terms[i]


def shape(*dims, dtype=F32):
    return jax.ShapeDtypeStruct(dims, dtype)


def shards(
    sizes,
    tokens,
    cotangent,
    input_weight,
    output_weight,
    short_taps,
    residues,
    decay_rates,
    skip_gain,
):
    n_x, n_zl = sizes["x"], sizes["zl"]
    block, part = tokens.shape
    width = output_weight.shape[0]
    order = residues.shape[1]
    rows = block + TILE
    taps = short_taps.transpose(0, 2, 1)
    rates = decay_rates.T
    res = residues.T
    skip = skip_gain[None]
    place = jnp.stack(
        [
            lax.axis_index("y"),
            lax.axis_index("zh") * sizes["core"] + lax.axis_index("core"),
            lax.axis_index("x"),
        ]
    ).astype(jnp.int32)
    copies = call(
        copy_kernel,
        shape(n_zl, 2 * block, part, dtype=BF16),
        [pltpu.SemaphoreType.DMA((n_zl, 2))],
        in_hbm(tokens),
        in_hbm(cotangent),
        hbm=2,
    )
    pieces = lax.all_to_all(copies, "zl", 0, 0, tiled=True)
    half = n_zl // 2

    def products(count):
        return 8 * count * block * part * width

    right = [(i, (i + 1) % n_x) for i in range(n_x)]
    left = [(i, (i - 1) % n_x) for i in range(n_x)]
    from_left = lax.ppermute(pieces, "x", right)
    from_right = lax.ppermute(pieces, "x", left)
    weights = (in_hbm(input_weight.transpose(1, 0, 2)), in_hbm(output_weight))
    total = call(
        functools.partial(near_kernel, sizes),
        shape(4, block, width),
        held_weights(n_zl // PAIR, part, width),
        place,
        pieces,
        *weights,
        flops=products(n_zl),
        hbm=2,
    )
    from_left, _ = lax.optimization_barrier((from_left, total))
    from_right, _ = lax.optimization_barrier((from_right, total))
    far_left = lax.ppermute(from_left[:half], "x", right)
    far_right = lax.ppermute(from_right[half:], "x", left)
    total = call(
        functools.partial(side_kernel, sizes),
        shape(4, block, width),
        held_weights(2 * n_zl // PAIR, part, width),
        place,
        from_left,
        from_right,
        total,
        *weights,
        flops=products(2 * n_zl),
        hbm=2,
    )
    ext = pltpu.VMEM((3, rows + TILE, width), F32)
    members = sizes["zh"] * sizes["core"]
    pack = 2 * order + 2 * TILE
    proj, send = call(
        functools.partial(far_kernel, sizes),
        [shape(4, block, width, dtype=BF16), shape(members, pack, width, dtype=BF16)],
        [pltpu.VMEM((4, block, width), F32), ext, pltpu.VMEM((pack, width), F32)]
        + held_weights(n_zl // PAIR, part, width),
        place,
        far_left,
        far_right,
        total,
        taps,
        rates,
        *weights,
        flops=products(n_zl),
        hbm=2,
    )
    conv, grad = call(
        local_kernel,
        [shape(rows, width), shape(rows, width)],
        [ext, pltpu.VMEM((2, rows + TILE, width), F32), pltpu.VMEM((rows, width), F32)],
        proj,
        taps,
        rates,
        res,
        skip,
        flops=3 * 10**9,
    )
    near_states = lax.all_to_all(send, ("zh", "core"), 0, 0, tiled=True)
    send = call(
        functools.partial(chain_kernel, block),
        shape(sizes["y"], order + 2 * TILE, width, dtype=BF16),
        [],
        place,
        taps,
        rates,
        near_states,
    )
    far_states = lax.all_to_all(send, "y", 0, 0, tiled=True)
    piece = shape(n_zl, 2 * block, part, dtype=BF16)
    half_piece = shape(half, 2 * block, part, dtype=BF16)
    hidden, grad_proj, to_right, to_left = call(
        functools.partial(last_kernel, sizes),
        [
            shape(block, width, dtype=BF16),
            shape(3, block, width, dtype=BF16),
            half_piece,
            half_piece,
        ],
        [ext, pltpu.VMEM((3, rows, width), F32)] + held_weights(n_zl // PAIR, part, width),
        place,
        proj,
        taps,
        rates,
        res,
        skip,
        conv,
        grad,
        near_states,
        far_states,
        *weights,
        flops=products(n_zl),
        hbm=2,
    )
    far_right = lax.ppermute(to_right, "x", right)
    far_left = lax.ppermute(to_left, "x", left)
    to_right, to_left = call(
        functools.partial(partials_kernel, sizes, [1, n_x - 1]),
        [piece, piece],
        held_weights(2 * n_zl // PAIR, part, width),
        place,
        hidden,
        grad_proj,
        *weights,
        flops=products(2 * n_zl),
        hbm=2,
    )
    to_right = call(functools.partial(join_kernel, 0), piece, [], to_right, far_right)
    from_left = lax.ppermute(to_right, "x", right)
    to_left = call(functools.partial(join_kernel, half), piece, [], to_left, far_left)
    from_right = lax.ppermute(to_left, "x", left)
    (own,) = call(
        functools.partial(partials_kernel, sizes, [0]),
        [piece],
        held_weights(n_zl // PAIR, part, width),
        place,
        hidden,
        grad_proj,
        *weights,
        flops=products(n_zl),
        hbm=2,
    )
    summed = sum(a.astype(F32) for a in (own, from_left, from_right)).astype(BF16)
    summed = lax.all_to_all(summed, "zl", 0, 0, tiled=True)
    total = jnp.sum(summed.astype(F32), axis=0).astype(BF16)
    return total[:block], total[block:]


def solution(mesh, dims=(8, 4, 2, 4, 4)):
    fine = Mesh(mesh.devices.reshape(dims), CTX + TP)
    sizes = dict(zip(CTX + TP, dims))
    return jax.shard_map(
        functools.partial(shards, sizes),
        mesh=fine,
        in_specs=(
            P(CTX, TP),
            P(CTX, TP),
            P(None, None, TP),
            P(TP, None),
            P(None, TP, None),
            P(TP, None),
            P(TP, None),
            P(TP),
        ),
        out_specs=(P(CTX, TP), P(CTX, TP)),
        check_vma=False,
    )
```

```python
import functools

import jax
import jax.numpy as jnp
from jax import lax
from jax.experimental import pallas as pl
from jax.experimental.pallas import tpu as pltpu
from jax.sharding import Mesh
from jax.sharding import PartitionSpec as P

CTX = ("y", "zh", "core")
TP = ("x", "zl")
TILE = 8
AHEAD = 2
GRANT = 16 * 2**20
PAIR = 2
BF16 = jnp.bfloat16
F32 = jnp.float32


def copy_kernel(tokens, cotangent, copies, sems):
    block = tokens.shape[0]
    moves = []
    for i in range(copies.shape[0]):
        for k, rows in enumerate((tokens, cotangent)):
            there = copies.at[i, pl.ds(k * block, block)]
            moves.append(pltpu.make_async_copy(rows, there, sems.at[i, k]))
            moves[-1].start()
    for move in moves:
        move.wait()


def features(ext, proj_ref, taps_ref, rows, last=None, first=None):
    block, width = proj_ref.shape[1:]
    zero = jnp.zeros((TILE, width), F32)
    out = []
    for p in range(3):
        ext[p, :TILE] = zero
        ext[p, TILE : TILE + block] = proj_ref[p].astype(F32)
        ext[p, TILE + block :] = zero
        if last is not None:
            ext[p, TILE - AHEAD : TILE] = last[AHEAD * p : AHEAD * (p + 1)]
            ext[p, TILE + block : TILE + block + AHEAD] = first[AHEAD * p : AHEAD * (p + 1)]
        total = taps_ref[p, 0:1, :] * ext[p, TILE : TILE + rows]
        for k in range(1, 3):
            total = total + taps_ref[p, k : k + 1, :] * ext[p, TILE - k : TILE - k + rows]
        out.append(total)
    return out


def inner_rows(ext, proj_ref, taps_ref, rows):
    block, width = proj_ref.shape[1:]
    query, key_part, value_part = features(ext, proj_ref, taps_ref, rows)
    row = lax.broadcasted_iota(jnp.int32, (rows, 1), 0)
    inside = (row >= AHEAD) & (row < block)
    back = jnp.concatenate([proj_ref[3].astype(F32), jnp.zeros((TILE, width), F32)], axis=0)
    gated = jnp.where(inside, key_part * value_part, 0.0)
    return gated, jnp.where(inside, back * query, 0.0), row.astype(F32)


def state_kernel(proj_ref, taps_ref, rates_ref, send_ref, ext, pack):
    order = rates_ref.shape[0]
    block = proj_ref.shape[1]
    gated, grad_conv, time = inner_rows(ext, proj_ref, taps_ref, block + TILE)
    time = time[:TILE]
    for r in range(order):
        rate = rates_ref[r : r + 1, :]
        fade = jnp.exp(-rate * TILE)
        fwd = gated[:TILE]
        bwd = grad_conv[block - TILE : block]
        for q in range(TILE, block, TILE):
            fwd = fwd * fade + gated[q : q + TILE]
            bwd = bwd * fade + grad_conv[block - TILE - q : block - q]
        fwd = jnp.exp(-rate * (TILE - 1.0 - time)) * fwd
        bwd = jnp.exp(-rate * (time - AHEAD)) * bwd
        pack[r : r + 1] = jnp.sum(fwd, axis=0, keepdims=True)
        pack[order + r : order + r + 1] = jnp.sum(bwd, axis=0, keepdims=True)
    at = 2 * order
    pack[at + TILE :] = jnp.zeros((TILE, pack.shape[1]), F32)
    for p in range(4):
        rows = proj_ref[p].astype(F32)
        pack[at + AHEAD * p : at + AHEAD * (p + 1)] = rows[:AHEAD]
        if p < 3:
            ends = at + TILE + AHEAD * p
            pack[ends : ends + AHEAD] = rows[block - AHEAD :]
    for i in range(send_ref.shape[0]):
        send_ref[i] = pack[...].astype(BF16)


def joint(taps_ref, first, last):
    row = []
    for p in range(3):
        a, b = first[AHEAD * p : AHEAD * p + 1], first[AHEAD * p + 1 : AHEAD * p + 2]
        c, d = last[AHEAD * p : AHEAD * p + 1], last[AHEAD * p + 1 : AHEAD * p + 2]
        t = [taps_ref[p, k : k + 1, :] for k in range(3)]
        row.append((t[0] * a + t[1] * d + t[2] * c, t[0] * b + t[1] * a + t[2] * d))
    back = (first[3 * AHEAD : 3 * AHEAD + 1], first[3 * AHEAD + 1 : 3 * AHEAD + 2])
    gated = tuple(row[1][i] * row[2][i] for i in range(AHEAD))
    return gated, tuple(back[i] * row[0][i] for i in range(AHEAD))


def fader(rates, block):
    def fade(blocks):
        if isinstance(blocks, int):
            return jnp.exp(-rates * float(block * blocks))
        return jnp.exp(-rates * (block * jnp.maximum(blocks, 0)).astype(F32))

    return fade


def group_states(block, taps_ref, rates, got_ref):
    order = rates.shape[0]
    members = got_ref.shape[0]
    fwd, bwd, firsts, lasts = [], [], [], []
    for j in range(members):
        got = got_ref[j].astype(F32)
        fwd.append(got[:order])
        bwd.append(got[order : 2 * order])
        firsts.append(got[2 * order : 2 * order + TILE])
        lasts.append(got[2 * order + TILE :])
    near, far = jnp.exp(-rates * (block - 2.0)), jnp.exp(-rates * (block - 1.0))
    for j in range(1, members):
        gated, grad_conv = joint(taps_ref, firsts[j], lasts[j - 1])
        fwd[j] = fwd[j] + far * gated[0] + near * gated[1]
        bwd[j - 1] = bwd[j - 1] + near * grad_conv[0] + far * grad_conv[1]
    return fwd, bwd, firsts, lasts, near, far


def chain_kernel(block, place_ref, taps_ref, rates_ref, got_ref, send_ref):
    rates = rates_ref[...]
    order = rates.shape[0]
    fade = fader(rates, block)
    fwd, bwd, firsts, lasts, _, _ = group_states(block, taps_ref, rates, got_ref)
    members = len(fwd)
    step = fade(1)
    total_fwd, total_bwd = fwd[0], bwd[-1]
    for j in range(1, members):
        total_fwd = total_fwd * step + fwd[j]
        total_bwd = total_bwd * step + bwd[members - 1 - j]
    ends = jnp.concatenate([firsts[0], lasts[-1]], axis=0).astype(BF16)
    for i in range(send_ref.shape[0]):
        send_ref[i, :order] = jnp.where(place_ref[0] < i, total_fwd, total_bwd).astype(BF16)
        send_ref[i, order:] = ends


def local_kernel(
    proj_ref, taps_ref, rates_ref, res_ref, skip_ref, conv_ref, grad_ref, ext, pad, filt_ref
):
    rows, width = conv_ref.shape
    gated, grad_conv, time = inner_rows(ext, proj_ref, taps_ref, rows)
    taps = jnp.zeros((rows, width), F32)
    for r in range(rates_ref.shape[0]):
        taps = taps + res_ref[r : r + 1, :] * jnp.exp(-rates_ref[r : r + 1, :] * (time + 1.0))
    filt_ref[...] = taps
    zero = jnp.zeros((TILE, width), F32)
    pad[0, :TILE] = zero
    pad[0, TILE:] = gated
    pad[1, :rows] = grad_conv
    pad[1, rows:] = zero
    direct = skip_ref[...] + jnp.sum(res_ref[...], axis=0, keepdims=True)
    for lane in range(0, width, 128):
        lanes = slice(lane, lane + 128)
        total = direct[:, lanes] * pad[0, TILE:, lanes]
        for m in range(1, TILE + 1):
            moved = pad[0, TILE - m : TILE - m + rows, lanes]
            for q in range(0, rows, TILE):
                tap = filt_ref[q + m - 1 : q + m, lanes]
                part = total[q:] + tap * moved[: rows - q]
                total = part if q == 0 else jnp.concatenate([total[:q], part], axis=0)
        conv_ref[:, lanes] = total
        total = direct[:, lanes] * pad[1, :rows, lanes]
        for m in range(1, TILE + 1):
            moved = pad[1, m : m + rows, lanes]
            for q in range(0, rows, TILE):
                tap = filt_ref[q + m - 1 : q + m, lanes]
                part = total[: rows - q] + tap * moved[q:]
                total = part if q == 0 else jnp.concatenate([part, total[rows - q :]], axis=0)
        grad_ref[:, lanes] = total


def finish_kernel(
    place_ref, proj_ref, taps_ref, rates_ref, res_ref, skip_ref, conv_ref, grad_ref,
    near_ref, far_ref, hidden_ref, out_ref, ext, feat,
):
    rates = rates_ref[...]
    res_all = res_ref[...]
    skip = skip_ref[...]
    order, width = rates.shape
    rows = conv_ref.shape[0]
    block = rows - TILE
    group, member = place_ref[0], place_ref[1]
    groups, members = far_ref.shape[0], near_ref.shape[0]
    fade = fader(rates, block)
    fwd, bwd, firsts, lasts, near, far = group_states(block, taps_ref, rates, near_ref)

    def rows_of(ref, index, start, there):
        got = ref[jnp.where(there, index, 0)].astype(F32)
        return jnp.where(there, got[start : start + TILE], 0.0)

    nothing = jnp.zeros((TILE, width), F32)
    whole = [far_ref[i].astype(F32) for i in range(groups)]
    head = [w[order : order + TILE] for w in whole] + [nothing]
    tail = [nothing] + [w[order + TILE :] for w in whole]
    ahead = jnp.zeros_like(rates)
    behind = jnp.zeros_like(rates)
    step, stride, most = fade(1), fade(members), fade(members - 1)
    for i in range(groups):
        gated, _ = joint(taps_ref, head[i], tail[i])
        total = whole[i][:order] + most * (far * gated[0] + near * gated[1])
        ahead = jnp.where(i < group, ahead * stride + total, ahead)
        j = groups - 1 - i
        _, grad_conv = joint(taps_ref, head[j + 1], tail[j + 1])
        total = whole[j][:order] + most * (near * grad_conv[0] + far * grad_conv[1])
        behind = jnp.where(j > group, behind * stride + total, behind)
    tail_before = rows_of(far_ref, group - 1, order + TILE, group > 0)
    head_behind = rows_of(far_ref, group + 1, order, group < groups - 1)
    gated, _ = joint(taps_ref, firsts[0], tail_before)
    _, grad_conv = joint(taps_ref, head_behind, lasts[-1])
    fwd[0] = fwd[0] + far * gated[0] + near * gated[1]
    bwd[-1] = bwd[-1] + near * grad_conv[0] + far * grad_conv[1]
    for j in range(members):
        ahead = jnp.where(j < member, ahead * step + fwd[j], ahead)
        i = members - 1 - j
        behind = jnp.where(i > member, behind * step + bwd[i], behind)

    last = rows_of(near_ref, member - 1, 2 * order + TILE, member > 0)
    last = jnp.where(member > 0, last, tail_before)
    first = rows_of(near_ref, member + 1, 2 * order, member < members - 1)
    first = jnp.where(member < members - 1, first, head_behind)
    query, key_part, value_part = features(ext, proj_ref, taps_ref, rows, last, first)
    row = lax.broadcasted_iota(jnp.int32, (TILE, 1), 0)
    next_back = jnp.where(row < AHEAD, pltpu.roll(first, AHEAD, 0), 0.0)
    back = jnp.concatenate([proj_ref[3].astype(F32), next_back], axis=0)
    gated = key_part * value_part
    grad_conv = back * query

    g = [gated[i : i + 1] for i in (0, 1, block, block + 1)]
    h = [grad_conv[i : i + 1] for i in (0, 1, block, block + 1)]
    grow = jnp.exp(rates)
    ahead = ahead + grow * g[0] + (grow * grow) * g[1]
    behind = behind + (grow * grow) * h[2] + grow * h[3]
    lag0 = skip + jnp.sum(res_all, axis=0, keepdims=True)
    lag1 = jnp.sum(res_all * jnp.exp(-rates), axis=0, keepdims=True)
    less = jnp.sum(res_all * grow, axis=0, keepdims=True)

    def two(a, b):
        return jnp.where(row == 0, a, jnp.where(row == 1, b, 0.0))

    def with_ends(array, top, bottom):
        return jnp.concatenate(
            [array[:TILE] + top, array[TILE:block], array[block:] + bottom], axis=0
        )

    conv_out = with_ends(
        conv_ref[...],
        two(skip * g[0] - less * g[1], skip * g[1]),
        two(lag0 * g[2], lag0 * g[3] + lag1 * g[2]),
    )
    grad_gated = with_ends(
        grad_ref[...],
        two(lag0 * h[0] + lag1 * h[1], lag0 * h[1]),
        two(skip * h[2], skip * h[3] - less * h[2]),
    )
    time = row.astype(F32)
    ahead = res_all * ahead
    behind = res_all * behind
    conv_tiles = [[] for _ in range(0, rows, TILE)]
    grad_tiles = [[] for _ in range(0, rows, TILE)]
    for lane in range(0, width, 128):
        lanes = slice(lane, lane + 128)
        conv_sum = [conv_out[q : q + TILE, lanes] for q in range(0, rows, TILE)]
        grad_sum = [grad_gated[q : q + TILE, lanes] for q in range(0, rows, TILE)]
        for r in range(order):
            rate = rates[r : r + 1, lanes]
            fall = jnp.exp(-rate * TILE)
            later = ahead[r : r + 1, lanes] * jnp.exp(-rate * (time + 1.0))
            sooner = behind[r : r + 1, lanes] * jnp.exp(-rate * (AHEAD - time))
            for q in range(len(conv_sum)):
                conv_sum[q] = conv_sum[q] + later
                grad_sum[-1 - q] = grad_sum[-1 - q] + sooner
                later = later * fall
                sooner = sooner * fall
        for q in range(len(conv_sum)):
            conv_tiles[q].append(conv_sum[q])
            grad_tiles[q].append(grad_sum[q])
    conv_out = jnp.concatenate([jnp.concatenate(t, axis=1) for t in conv_tiles], axis=0)
    grad_gated = jnp.concatenate([jnp.concatenate(t, axis=1) for t in grad_tiles], axis=0)
    hidden_ref[...] = (query * conv_out)[:block].astype(BF16)
    feat[0] = back * conv_out
    feat[1] = grad_gated * value_part
    feat[2] = grad_gated * key_part
    for p in range(3):
        total = taps_ref[p, 0:1, :] * feat[p, :block]
        for k in range(1, 3):
            total = total + taps_ref[p, k : k + 1, :] * feat[p, k : k + block]
        out_ref[p] = total.astype(BF16)


def in_hbm(array):
    return pltpu.with_memory_space_constraint(array, pltpu.HBM)


def call(kernel, outs, scratch, *args, flops=0, hbm=0):
    whole = pl.BlockSpec(memory_space=pltpu.VMEM)
    far = pl.BlockSpec(memory_space=pltpu.HBM)
    scalar = pl.BlockSpec(memory_space=pltpu.SMEM)
    specs = [
        scalar if a.dtype == jnp.int32 else far if i >= len(args) - hbm else whole
        for i, a in enumerate(args)
    ]
    cost = pl.CostEstimate(flops=flops, bytes_accessed=0, transcendentals=0) if flops else None
    return pl.pallas_call(
        kernel,
        out_shape=outs,
        scratch_shapes=scratch,
        in_specs=specs,
        out_specs=jax.tree.map(lambda _: whole, outs),
        cost_estimate=cost,
        compiler_params=pltpu.CompilerParams(vmem_limit_bytes=GRANT),
    )(*args)


def load_weights(blocks, weight_in, weight_out, held_in, held_out, sems, ahead=2):
    span = held_in.shape[1]
    width = weight_out.shape[0]
    part = span // PAIR
    copies = []
    for s, block in enumerate(blocks):
        at = pl.ds(pl.multiple_of(block * part, part), span)
        moves = [
            pltpu.make_async_copy(
                weight_in.at[p, at, :],
                held_in.at[s, :, pl.ds(p * width, width)],
                sems.at[s, p],
            )
            for p in range(3)
        ]
        moves.append(
            pltpu.make_async_copy(weight_out.at[:, at], held_out.at[s], sems.at[s, 3])
        )
        copies.append(moves)

    def start(s):
        for copy in copies[s]:
            copy.start()

    for s in range(min(ahead, len(copies))):
        start(s)

    def ready(s):
        for copy in copies[s]:
            copy.wait()
        if s + ahead < len(copies):
            start(s + ahead)

    return ready


def at_once(s):
    pass


def held_weights(count, part, width):
    return [
        pltpu.VMEM((count, PAIR * part, 3 * width), BF16),
        pltpu.VMEM((count, width, PAIR * part), BF16),
        pltpu.SemaphoreType.DMA((count, 4)),
    ]


def project(
    sizes, offsets, place_ref, pieces, weights, old, total, held_in, held_out, sems=None, also=None
):
    n_x, n_zl = sizes["x"], sizes["zl"]
    block = pieces[0].shape[1] // 2
    width = total.shape[2]
    work = [
        (piece, j, lax.rem(place_ref[2] + k, n_x) * n_zl + start + j)
        for piece, (k, start) in zip(pieces, offsets)
        for j in range(0, piece.shape[0], PAIR)
    ]
    ready = at_once
    if sems is not None:
        ready = load_weights([w[2] for w in work], *weights, held_in, held_out, sems)
    if also is not None:
        also()
    for s, (piece, j, _) in enumerate(work):
        run = range(j, j + PAIR)
        part_in = jnp.concatenate([piece[i, :block] for i in run], axis=1)
        part_grad = jnp.concatenate([piece[i, block:] for i in run], axis=1)
        ready(s)
        term = jnp.dot(part_in, held_in[s], preferred_element_type=F32)
        back = lax.dot_general(
            part_grad, held_out[s], (((1,), (1,)), ((), ())), preferred_element_type=F32
        )
        terms = [term[:, p * width : (p + 1) * width] for p in range(3)] + [back]
        for p in range(4):
            if s == 0 and old is None:
                total[p] = terms[p]
            else:
                total[p] = (old if s == 0 else total)[p] + terms[p]


def near_kernel(sizes, place, piece, weight_in, weight_out, total, *held):
    project(sizes, [(0, 0)], place, [piece], (weight_in, weight_out), None, total, *held)


def side_kernel(
    sizes, place, left, right, old, weight_in, weight_out, total, far_in, far_out, *held
):
    n_x, n_zl = sizes["x"], sizes["zl"]
    offsets = [(n_x - 1, 0), (1, 0)]
    weights = (weight_in, weight_out)
    blocks = [lax.rem(place[2] + 2, n_x) * n_zl + j for j in range(0, n_zl, PAIR)]
    waits = []

    def fetch():
        waits.append(load_weights(blocks, *weights, far_in, far_out, held[3], ahead=len(blocks)))

    project(sizes, offsets, place, [left, right], weights, old, total, *held[:3], also=fetch)
    for s in range(len(blocks)):
        waits[0](s)


def far_kernel(
    sizes, place, left, right, old, taps, rates, far_in, far_out, proj, send, total, ext, pack
):
    offsets = [(2, 0), (2, left.shape[0])]
    project(sizes, offsets, place, [left, right], None, old, total, far_in, far_out)
    proj[...] = total[...].astype(BF16)
    state_kernel(proj, taps, rates, send, ext, pack)


def partials(held, start, out, hidden, grad, ready):
    held_in, held_out = held[:2]
    block = hidden.shape[0]
    part = out.shape[2]
    for j in range(0, out.shape[0], PAIR):
        s = start + j // PAIR
        grads = jnp.concatenate([grad[p] for p in range(3)], axis=1)
        ready(s)
        mixed = jnp.dot(hidden[...], held_out[s], preferred_element_type=F32)
        total = lax.dot_general(
            grads, held_in[s], (((1,), (1,)), ((), ())), preferred_element_type=F32
        )
        for i in range(PAIR):
            out[j + i, :block] = mixed[:, i * part : (i + 1) * part].astype(BF16)
            out[j + i, block:] = total[:, i * part : (i + 1) * part].astype(BF16)


def partials_kernel(sizes, offset, place, hidden, grad, weight_in, weight_out, out, *held):
    n_x, n_zl = sizes["x"], sizes["zl"]
    base = lax.rem(place[2] + offset, n_x) * n_zl
    blocks = [base + j for j in range(0, out.shape[0], PAIR)]
    ready = load_weights(blocks, weight_in, weight_out, *held)
    partials(held, 0, out, hidden, grad, ready)


def side_partials_kernel(hidden, grad, side_in, side_out, to_right, to_left):
    held = (side_in, side_out)
    partials(held, 0, to_right, hidden, grad, at_once)
    partials(held, to_right.shape[0] // PAIR, to_left, hidden, grad, at_once)


def last_kernel(
    sizes, place, proj, taps, rates, res, skip, conv, grad, near, far, weight_in, weight_out,
    hidden, out, to_right, to_left, side_in, side_out, ext, feat, *held,
):
    n_x, n_zl = sizes["x"], sizes["zl"]
    blocks, *side = [
        [lax.rem(place[2] + k, n_x) * n_zl + j for j in range(0, n_zl, PAIR)]
        for k in (2, 1, n_x - 1)
    ]
    side = side[0] + side[1]
    weights = (weight_in, weight_out)
    ready = load_weights(blocks, *weights, *held[:3], ahead=len(blocks))
    ready_side = load_weights(side, *weights, side_in, side_out, held[3], ahead=len(side))
    finish_kernel(
        place, proj, taps, rates, res, skip, conv, grad, near, far, hidden, out, ext, feat
    )
    partials(held, 0, to_right, hidden, out, ready)
    partials(held, to_right.shape[0] // PAIR, to_left, hidden, out, ready)
    for s in range(len(side)):
        ready_side(s)


def join_kernel(start, terms, got, out):
    count = got.shape[0]
    for i in range(terms.shape[0]):
        if start <= i < start + count:
            both = terms[i].astype(F32) + got[i - start].astype(F32)
            out[i] = both.astype(BF16)
        else:
            out[i] = terms[i]


def shape(*dims, dtype=F32):
    return jax.ShapeDtypeStruct(dims, dtype)


def shards(
    sizes,
    tokens,
    cotangent,
    input_weight,
    output_weight,
    short_taps,
    residues,
    decay_rates,
    skip_gain,
):
    n_x, n_zl = sizes["x"], sizes["zl"]
    block, part = tokens.shape
    width = output_weight.shape[0]
    order = residues.shape[1]
    rows = block + TILE
    taps = short_taps.transpose(0, 2, 1)
    rates = decay_rates.T
    res = residues.T
    skip = skip_gain[None]
    place = jnp.stack(
        [
            lax.axis_index("y"),
            lax.axis_index("zh") * sizes["core"] + lax.axis_index("core"),
            lax.axis_index("x"),
        ]
    ).astype(jnp.int32)
    copies = call(
        copy_kernel,
        shape(n_zl, 2 * block, part, dtype=BF16),
        [pltpu.SemaphoreType.DMA((n_zl, 2))],
        in_hbm(tokens),
        in_hbm(cotangent),
        hbm=2,
    )
    pieces = lax.all_to_all(copies, "zl", 0, 0, tiled=True)
    half = n_zl // 2

    def products(count):
        return 8 * count * block * part * width

    right = [(i, (i + 1) % n_x) for i in range(n_x)]
    left = [(i, (i - 1) % n_x) for i in range(n_x)]
    from_left = lax.ppermute(pieces, "x", right)
    from_right = lax.ppermute(pieces, "x", left)
    weights = (in_hbm(input_weight.transpose(1, 0, 2)), in_hbm(output_weight))
    total = call(
        functools.partial(near_kernel, sizes),
        shape(4, block, width),
        held_weights(n_zl // PAIR, part, width),
        place,
        pieces,
        *weights,
        flops=products(n_zl),
        hbm=2,
    )
    from_left, _ = lax.optimization_barrier((from_left, total))
    from_right, _ = lax.optimization_barrier((from_right, total))
    far_left = lax.ppermute(from_left[:half], "x", right)
    far_right = lax.ppermute(from_right[half:], "x", left)
    runs = n_zl // PAIR
    held_shapes = [
        shape(runs, PAIR * part, 3 * width, dtype=BF16),
        shape(runs, width, PAIR * part, dtype=BF16),
    ]
    total, far_in, far_out = call(
        functools.partial(side_kernel, sizes),
        [shape(4, block, width), *held_shapes],
        held_weights(2 * runs, part, width) + [pltpu.SemaphoreType.DMA((runs, 4))],
        place,
        from_left,
        from_right,
        total,
        *weights,
        flops=products(2 * n_zl),
        hbm=2,
    )
    ext = pltpu.VMEM((3, rows + TILE, width), F32)
    members = sizes["zh"] * sizes["core"]
    pack = 2 * order + 2 * TILE
    proj, send = call(
        functools.partial(far_kernel, sizes),
        [shape(4, block, width, dtype=BF16), shape(members, pack, width, dtype=BF16)],
        [pltpu.VMEM((4, block, width), F32), ext, pltpu.VMEM((pack, width), F32)],
        place,
        far_left,
        far_right,
        total,
        taps,
        rates,
        far_in,
        far_out,
        flops=products(n_zl),
    )
    conv, grad = call(
        local_kernel,
        [shape(rows, width), shape(rows, width)],
        [ext, pltpu.VMEM((2, rows + TILE, width), F32), pltpu.VMEM((rows, width), F32)],
        proj,
        taps,
        rates,
        res,
        skip,
        flops=3 * 10**9,
    )
    near_states = lax.all_to_all(send, ("zh", "core"), 0, 0, tiled=True)
    send = call(
        functools.partial(chain_kernel, block),
        shape(sizes["y"], order + 2 * TILE, width, dtype=BF16),
        [],
        place,
        taps,
        rates,
        near_states,
    )
    far_states = lax.all_to_all(send, "y", 0, 0, tiled=True)
    piece = shape(n_zl, 2 * block, part, dtype=BF16)
    half_piece = shape(half, 2 * block, part, dtype=BF16)
    side_shapes = [
        shape(2 * runs, PAIR * part, 3 * width, dtype=BF16),
        shape(2 * runs, width, PAIR * part, dtype=BF16),
    ]
    hidden, grad_proj, to_right, to_left, side_in, side_out = call(
        functools.partial(last_kernel, sizes),
        [
            shape(block, width, dtype=BF16),
            shape(3, block, width, dtype=BF16),
            half_piece,
            half_piece,
            *side_shapes,
        ],
        [ext, pltpu.VMEM((3, rows, width), F32)]
        + held_weights(runs, part, width)
        + [pltpu.SemaphoreType.DMA((2 * runs, 4))],
        place,
        proj,
        taps,
        rates,
        res,
        skip,
        conv,
        grad,
        near_states,
        far_states,
        *weights,
        flops=products(n_zl),
        hbm=2,
    )
    far_right = lax.ppermute(to_right, "x", right)
    far_left = lax.ppermute(to_left, "x", left)
    to_right, to_left = call(
        side_partials_kernel,
        [piece, piece],
        [],
        hidden,
        grad_proj,
        side_in,
        side_out,
        flops=products(2 * n_zl),
    )
    to_right = call(functools.partial(join_kernel, 0), piece, [], to_right, far_right)
    from_left = lax.ppermute(to_right, "x", right)
    to_left = call(functools.partial(join_kernel, half), piece, [], to_left, far_left)
    from_right = lax.ppermute(to_left, "x", left)
    own = call(
        functools.partial(partials_kernel, sizes, 0),
        piece,
        held_weights(runs, part, width),
        place,
        hidden,
        grad_proj,
        *weights,
        flops=products(n_zl),
        hbm=2,
    )
    summed = sum(a.astype(F32) for a in (own, from_left, from_right)).astype(BF16)
    summed = lax.all_to_all(summed, "zl", 0, 0, tiled=True)
    total = jnp.sum(summed.astype(F32), axis=0).astype(BF16)
    return total[:block], total[block:]


def solution(mesh, dims=(8, 4, 2, 4, 4)):
    fine = Mesh(mesh.devices.reshape(dims), CTX + TP)
    sizes = dict(zip(CTX + TP, dims))
    return jax.shard_map(
        functools.partial(shards, sizes),
        mesh=fine,
        in_specs=(
            P(CTX, TP),
            P(CTX, TP),
            P(None, None, TP),
            P(TP, None),
            P(None, TP, None),
            P(TP, None),
            P(TP, None),
            P(TP),
        ),
        out_specs=(P(CTX, TP), P(CTX, TP)),
        check_vma=False,
    )
```

```python
import functools

import jax
import jax.numpy as jnp
from jax import lax
from jax.experimental import pallas as pl
from jax.experimental.pallas import tpu as pltpu
from jax.sharding import Mesh
from jax.sharding import PartitionSpec as P

CTX = ("y", "zh", "core")
TP = ("x", "zl")
TILE = 8
AHEAD = 2
GRANT = 16 * 2**20
PAIR = 2
BF16 = jnp.bfloat16
F32 = jnp.float32


def copy_kernel(tokens, cotangent, copies, sems):
    block = tokens.shape[0]
    moves = []
    for i in range(copies.shape[0]):
        for k, rows in enumerate((tokens, cotangent)):
            there = copies.at[i, pl.ds(k * block, block)]
            moves.append(pltpu.make_async_copy(rows, there, sems.at[i, k]))
            moves[-1].start()
    for move in moves:
        move.wait()


def features(ext, proj_ref, taps_ref, rows, last=None, first=None):
    block, width = proj_ref.shape[1:]
    zero = jnp.zeros((TILE, width), F32)
    out = []
    for p in range(3):
        ext[p, :TILE] = zero
        ext[p, TILE : TILE + block] = proj_ref[p].astype(F32)
        ext[p, TILE + block :] = zero
        if last is not None:
            ext[p, TILE - AHEAD : TILE] = last[AHEAD * p : AHEAD * (p + 1)]
            ext[p, TILE + block : TILE + block + AHEAD] = first[AHEAD * p : AHEAD * (p + 1)]
        total = taps_ref[p, 0:1, :] * ext[p, TILE : TILE + rows]
        for k in range(1, 3):
            total = total + taps_ref[p, k : k + 1, :] * ext[p, TILE - k : TILE - k + rows]
        out.append(total)
    return out


def inner_rows(ext, proj_ref, taps_ref, rows):
    block, width = proj_ref.shape[1:]
    query, key_part, value_part = features(ext, proj_ref, taps_ref, rows)
    row = lax.broadcasted_iota(jnp.int32, (rows, 1), 0)
    inside = (row >= AHEAD) & (row < block)
    back = jnp.concatenate([proj_ref[3].astype(F32), jnp.zeros((TILE, width), F32)], axis=0)
    gated = jnp.where(inside, key_part * value_part, 0.0)
    return gated, jnp.where(inside, back * query, 0.0), row.astype(F32)


def state_kernel(proj_ref, taps_ref, rates_ref, send_ref, ext, pack):
    order = rates_ref.shape[0]
    block = proj_ref.shape[1]
    gated, grad_conv, time = inner_rows(ext, proj_ref, taps_ref, block + TILE)
    time = time[:TILE]
    for r in range(order):
        rate = rates_ref[r : r + 1, :]
        fade = jnp.exp(-rate * TILE)
        fwd = gated[:TILE]
        bwd = grad_conv[block - TILE : block]
        for q in range(TILE, block, TILE):
            fwd = fwd * fade + gated[q : q + TILE]
            bwd = bwd * fade + grad_conv[block - TILE - q : block - q]
        fwd = jnp.exp(-rate * (TILE - 1.0 - time)) * fwd
        bwd = jnp.exp(-rate * (time - AHEAD)) * bwd
        pack[r : r + 1] = jnp.sum(fwd, axis=0, keepdims=True)
        pack[order + r : order + r + 1] = jnp.sum(bwd, axis=0, keepdims=True)
    at = 2 * order
    pack[at + TILE :] = jnp.zeros((TILE, pack.shape[1]), F32)
    for p in range(4):
        rows = proj_ref[p].astype(F32)
        pack[at + AHEAD * p : at + AHEAD * (p + 1)] = rows[:AHEAD]
        if p < 3:
            ends = at + TILE + AHEAD * p
            pack[ends : ends + AHEAD] = rows[block - AHEAD :]
    for i in range(send_ref.shape[0]):
        send_ref[i] = pack[...].astype(BF16)


def joint(taps_ref, first, last):
    row = []
    for p in range(3):
        a, b = first[AHEAD * p : AHEAD * p + 1], first[AHEAD * p + 1 : AHEAD * p + 2]
        c, d = last[AHEAD * p : AHEAD * p + 1], last[AHEAD * p + 1 : AHEAD * p + 2]
        t = [taps_ref[p, k : k + 1, :] for k in range(3)]
        row.append((t[0] * a + t[1] * d + t[2] * c, t[0] * b + t[1] * a + t[2] * d))
    back = (first[3 * AHEAD : 3 * AHEAD + 1], first[3 * AHEAD + 1 : 3 * AHEAD + 2])
    gated = tuple(row[1][i] * row[2][i] for i in range(AHEAD))
    return gated, tuple(back[i] * row[0][i] for i in range(AHEAD))


def fader(rates, block):
    def fade(blocks):
        if isinstance(blocks, int):
            return jnp.exp(-rates * float(block * blocks))
        return jnp.exp(-rates * (block * jnp.maximum(blocks, 0)).astype(F32))

    return fade


def group_states(block, taps_ref, rates, got_ref):
    order = rates.shape[0]
    members = got_ref.shape[0]
    fwd, bwd, firsts, lasts = [], [], [], []
    for j in range(members):
        got = got_ref[j].astype(F32)
        fwd.append(got[:order])
        bwd.append(got[order : 2 * order])
        firsts.append(got[2 * order : 2 * order + TILE])
        lasts.append(got[2 * order + TILE :])
    near, far = jnp.exp(-rates * (block - 2.0)), jnp.exp(-rates * (block - 1.0))
    for j in range(1, members):
        gated, grad_conv = joint(taps_ref, firsts[j], lasts[j - 1])
        fwd[j] = fwd[j] + far * gated[0] + near * gated[1]
        bwd[j - 1] = bwd[j - 1] + near * grad_conv[0] + far * grad_conv[1]
    return fwd, bwd, firsts, lasts, near, far


def chain_kernel(block, place_ref, taps_ref, rates_ref, got_ref, send_ref):
    rates = rates_ref[...]
    order = rates.shape[0]
    fade = fader(rates, block)
    fwd, bwd, firsts, lasts, _, _ = group_states(block, taps_ref, rates, got_ref)
    members = len(fwd)
    step = fade(1)
    total_fwd, total_bwd = fwd[0], bwd[-1]
    for j in range(1, members):
        total_fwd = total_fwd * step + fwd[j]
        total_bwd = total_bwd * step + bwd[members - 1 - j]
    ends = jnp.concatenate([firsts[0], lasts[-1]], axis=0).astype(BF16)
    for i in range(send_ref.shape[0]):
        send_ref[i, :order] = jnp.where(place_ref[0] < i, total_fwd, total_bwd).astype(BF16)
        send_ref[i, order:] = ends


def local_kernel(
    proj_ref, taps_ref, rates_ref, res_ref, skip_ref, conv_ref, grad_ref, ext, pad, filt_ref
):
    rows, width = conv_ref.shape
    gated, grad_conv, time = inner_rows(ext, proj_ref, taps_ref, rows)
    taps = jnp.zeros((rows, width), F32)
    for r in range(rates_ref.shape[0]):
        taps = taps + res_ref[r : r + 1, :] * jnp.exp(-rates_ref[r : r + 1, :] * (time + 1.0))
    filt_ref[...] = taps
    zero = jnp.zeros((TILE, width), F32)
    pad[0, :TILE] = zero
    pad[0, TILE:] = gated
    pad[1, :rows] = grad_conv
    pad[1, rows:] = zero
    direct = skip_ref[...] + jnp.sum(res_ref[...], axis=0, keepdims=True)
    for lane in range(0, width, 128):
        lanes = slice(lane, lane + 128)
        total = direct[:, lanes] * pad[0, TILE:, lanes]
        for m in range(1, TILE + 1):
            moved = pad[0, TILE - m : TILE - m + rows, lanes]
            for q in range(0, rows, TILE):
                tap = filt_ref[q + m - 1 : q + m, lanes]
                part = total[q:] + tap * moved[: rows - q]
                total = part if q == 0 else jnp.concatenate([total[:q], part], axis=0)
        conv_ref[:, lanes] = total
        total = direct[:, lanes] * pad[1, :rows, lanes]
        for m in range(1, TILE + 1):
            moved = pad[1, m : m + rows, lanes]
            for q in range(0, rows, TILE):
                tap = filt_ref[q + m - 1 : q + m, lanes]
                part = total[: rows - q] + tap * moved[q:]
                total = part if q == 0 else jnp.concatenate([part, total[rows - q :]], axis=0)
        grad_ref[:, lanes] = total


def finish_kernel(
    place_ref, proj_ref, taps_ref, rates_ref, res_ref, skip_ref, conv_ref, grad_ref,
    near_ref, far_ref, hidden_ref, out_ref, ext, feat,
):
    rates = rates_ref[...]
    res_all = res_ref[...]
    skip = skip_ref[...]
    order, width = rates.shape
    rows = conv_ref.shape[0]
    block = rows - TILE
    group, member = place_ref[0], place_ref[1]
    groups, members = far_ref.shape[0], near_ref.shape[0]
    fade = fader(rates, block)
    fwd, bwd, firsts, lasts, near, far = group_states(block, taps_ref, rates, near_ref)

    def rows_of(ref, index, start, there):
        got = ref[jnp.where(there, index, 0)].astype(F32)
        return jnp.where(there, got[start : start + TILE], 0.0)

    nothing = jnp.zeros((TILE, width), F32)
    whole = [far_ref[i].astype(F32) for i in range(groups)]
    head = [w[order : order + TILE] for w in whole] + [nothing]
    tail = [nothing] + [w[order + TILE :] for w in whole]
    ahead = jnp.zeros_like(rates)
    behind = jnp.zeros_like(rates)
    step, stride, most = fade(1), fade(members), fade(members - 1)
    for i in range(groups):
        gated, _ = joint(taps_ref, head[i], tail[i])
        total = whole[i][:order] + most * (far * gated[0] + near * gated[1])
        ahead = jnp.where(i < group, ahead * stride + total, ahead)
        j = groups - 1 - i
        _, grad_conv = joint(taps_ref, head[j + 1], tail[j + 1])
        total = whole[j][:order] + most * (near * grad_conv[0] + far * grad_conv[1])
        behind = jnp.where(j > group, behind * stride + total, behind)
    tail_before = rows_of(far_ref, group - 1, order + TILE, group > 0)
    head_behind = rows_of(far_ref, group + 1, order, group < groups - 1)
    gated, _ = joint(taps_ref, firsts[0], tail_before)
    _, grad_conv = joint(taps_ref, head_behind, lasts[-1])
    fwd[0] = fwd[0] + far * gated[0] + near * gated[1]
    bwd[-1] = bwd[-1] + near * grad_conv[0] + far * grad_conv[1]
    for j in range(members):
        ahead = jnp.where(j < member, ahead * step + fwd[j], ahead)
        i = members - 1 - j
        behind = jnp.where(i > member, behind * step + bwd[i], behind)

    last = rows_of(near_ref, member - 1, 2 * order + TILE, member > 0)
    last = jnp.where(member > 0, last, tail_before)
    first = rows_of(near_ref, member + 1, 2 * order, member < members - 1)
    first = jnp.where(member < members - 1, first, head_behind)
    query, key_part, value_part = features(ext, proj_ref, taps_ref, rows, last, first)
    row = lax.broadcasted_iota(jnp.int32, (TILE, 1), 0)
    next_back = jnp.where(row < AHEAD, pltpu.roll(first, AHEAD, 0), 0.0)
    back = jnp.concatenate([proj_ref[3].astype(F32), next_back], axis=0)
    gated = key_part * value_part
    grad_conv = back * query

    g = [gated[i : i + 1] for i in (0, 1, block, block + 1)]
    h = [grad_conv[i : i + 1] for i in (0, 1, block, block + 1)]
    grow = jnp.exp(rates)
    ahead = ahead + grow * g[0] + (grow * grow) * g[1]
    behind = behind + (grow * grow) * h[2] + grow * h[3]
    lag0 = skip + jnp.sum(res_all, axis=0, keepdims=True)
    lag1 = jnp.sum(res_all * jnp.exp(-rates), axis=0, keepdims=True)
    less = jnp.sum(res_all * grow, axis=0, keepdims=True)

    def two(a, b):
        return jnp.where(row == 0, a, jnp.where(row == 1, b, 0.0))

    def with_ends(array, top, bottom):
        return jnp.concatenate(
            [array[:TILE] + top, array[TILE:block], array[block:] + bottom], axis=0
        )

    conv_out = with_ends(
        conv_ref[...],
        two(skip * g[0] - less * g[1], skip * g[1]),
        two(lag0 * g[2], lag0 * g[3] + lag1 * g[2]),
    )
    grad_gated = with_ends(
        grad_ref[...],
        two(lag0 * h[0] + lag1 * h[1], lag0 * h[1]),
        two(skip * h[2], skip * h[3] - less * h[2]),
    )
    time = row.astype(F32)
    ahead = res_all * ahead
    behind = res_all * behind
    conv_tiles = [[] for _ in range(0, rows, TILE)]
    grad_tiles = [[] for _ in range(0, rows, TILE)]
    for lane in range(0, width, 128):
        lanes = slice(lane, lane + 128)
        conv_sum = [conv_out[q : q + TILE, lanes] for q in range(0, rows, TILE)]
        grad_sum = [grad_gated[q : q + TILE, lanes] for q in range(0, rows, TILE)]
        for r in range(order):
            rate = rates[r : r + 1, lanes]
            fall = jnp.exp(-rate * TILE)
            later = ahead[r : r + 1, lanes] * jnp.exp(-rate * (time + 1.0))
            sooner = behind[r : r + 1, lanes] * jnp.exp(-rate * (AHEAD - time))
            for q in range(len(conv_sum)):
                conv_sum[q] = conv_sum[q] + later
                grad_sum[-1 - q] = grad_sum[-1 - q] + sooner
                later = later * fall
                sooner = sooner * fall
        for q in range(len(conv_sum)):
            conv_tiles[q].append(conv_sum[q])
            grad_tiles[q].append(grad_sum[q])
    conv_out = jnp.concatenate([jnp.concatenate(t, axis=1) for t in conv_tiles], axis=0)
    grad_gated = jnp.concatenate([jnp.concatenate(t, axis=1) for t in grad_tiles], axis=0)
    hidden_ref[...] = (query * conv_out)[:block].astype(BF16)
    feat[0] = back * conv_out
    feat[1] = grad_gated * value_part
    feat[2] = grad_gated * key_part
    for p in range(3):
        total = taps_ref[p, 0:1, :] * feat[p, :block]
        for k in range(1, 3):
            total = total + taps_ref[p, k : k + 1, :] * feat[p, k : k + block]
        out_ref[p] = total.astype(BF16)


def in_hbm(array):
    return pltpu.with_memory_space_constraint(array, pltpu.HBM)


def call(kernel, outs, scratch, *args, flops=0, hbm=0):
    whole = pl.BlockSpec(memory_space=pltpu.VMEM)
    far = pl.BlockSpec(memory_space=pltpu.HBM)
    scalar = pl.BlockSpec(memory_space=pltpu.SMEM)
    specs = [
        scalar if a.dtype == jnp.int32 else far if i >= len(args) - hbm else whole
        for i, a in enumerate(args)
    ]
    cost = pl.CostEstimate(flops=flops, bytes_accessed=0, transcendentals=0) if flops else None
    return pl.pallas_call(
        kernel,
        out_shape=outs,
        scratch_shapes=scratch,
        in_specs=specs,
        out_specs=jax.tree.map(lambda _: whole, outs),
        cost_estimate=cost,
        compiler_params=pltpu.CompilerParams(vmem_limit_bytes=GRANT),
    )(*args)


def load_weights(blocks, weight_in, weight_out, held_in, held_out, sems, ahead=2):
    span = held_in.shape[1]
    width = weight_out.shape[0]
    part = span // PAIR
    copies = []
    for s, block in enumerate(blocks):
        at = pl.ds(pl.multiple_of(block * part, part), span)
        moves = [
            pltpu.make_async_copy(
                weight_in.at[p, at, :],
                held_in.at[s, :, pl.ds(p * width, width)],
                sems.at[s, p],
            )
            for p in range(3)
        ]
        moves.append(
            pltpu.make_async_copy(weight_out.at[:, at], held_out.at[s], sems.at[s, 3])
        )
        copies.append(moves)

    def start(s):
        for copy in copies[s]:
            copy.start()

    for s in range(min(ahead, len(copies))):
        start(s)

    def ready(s):
        for copy in copies[s]:
            copy.wait()
        if s + ahead < len(copies):
            start(s + ahead)

    return ready


def at_once(s):
    pass


def held_weights(count, part, width):
    return [
        pltpu.VMEM((count, PAIR * part, 3 * width), BF16),
        pltpu.VMEM((count, width, PAIR * part), BF16),
        pltpu.SemaphoreType.DMA((count, 4)),
    ]


def project(
    sizes, offsets, place_ref, pieces, weights, old, total, held_in, held_out, sems=None, also=None
):
    n_x, n_zl = sizes["x"], sizes["zl"]
    block = pieces[0].shape[1] // 2
    width = total.shape[2]
    work = [
        (piece, j, lax.rem(place_ref[2] + k, n_x) * n_zl + start + j)
        for piece, (k, start) in zip(pieces, offsets)
        for j in range(0, piece.shape[0], PAIR)
    ]
    ready = at_once
    if sems is not None:
        ready = load_weights([w[2] for w in work], *weights, held_in, held_out, sems)
    if also is not None:
        also()
    for s, (piece, j, _) in enumerate(work):
        run = range(j, j + PAIR)
        part_in = jnp.concatenate([piece[i, :block] for i in run], axis=1)
        part_grad = jnp.concatenate([piece[i, block:] for i in run], axis=1)
        ready(s)
        term = jnp.dot(part_in, held_in[s], preferred_element_type=F32)
        back = lax.dot_general(
            part_grad, held_out[s], (((1,), (1,)), ((), ())), preferred_element_type=F32
        )
        terms = [term[:, p * width : (p + 1) * width] for p in range(3)] + [back]
        for p in range(4):
            if s == 0 and old is None:
                total[p] = terms[p]
            else:
                total[p] = (old if s == 0 else total)[p] + terms[p]


def runs_of(sizes, place, offsets):
    n_x, n_zl = sizes["x"], sizes["zl"]
    return [
        lax.rem(place[2] + k, n_x) * n_zl + j for k in offsets for j in range(0, n_zl, PAIR)
    ]


def fetch(blocks, weights, held):
    ready = load_weights(blocks, *weights, *held, ahead=len(blocks))

    def wait():
        for s in range(len(blocks)):
            ready(s)

    return wait


def near_kernel(
    sizes, place, piece, weight_in, weight_out,
    total, side_in, side_out, far_in, far_out, own_in, own_out, own_sems, side_sems, far_sems,
):
    weights = (weight_in, weight_out)
    waits = []

    def also():
        side = runs_of(sizes, place, [sizes["x"] - 1, 1])
        waits.append(fetch(side, weights, (side_in, side_out, side_sems)))
        far = runs_of(sizes, place, [2])
        waits.append(fetch(far, weights, (far_in, far_out, far_sems)))

    project(
        sizes, [(0, 0)], place, [piece], weights, None, total, own_in, own_out, own_sems, also
    )
    for wait in waits:
        wait()


def side_kernel(sizes, place, left, right, old, side_in, side_out, total):
    offsets = [(sizes["x"] - 1, 0), (1, 0)]
    project(sizes, offsets, place, [left, right], None, old, total, side_in, side_out)


def far_kernel(
    sizes, place, left, right, old, taps, rates, far_in, far_out, proj, send, total, ext, pack
):
    offsets = [(2, 0), (2, left.shape[0])]
    project(sizes, offsets, place, [left, right], None, old, total, far_in, far_out)
    proj[...] = total[...].astype(BF16)
    state_kernel(proj, taps, rates, send, ext, pack)


def partials(held, start, out, hidden, grad, ready):
    held_in, held_out = held[:2]
    block = hidden.shape[0]
    part = out.shape[2]
    for j in range(0, out.shape[0], PAIR):
        s = start + j // PAIR
        grads = jnp.concatenate([grad[p] for p in range(3)], axis=1)
        ready(s)
        mixed = jnp.dot(hidden[...], held_out[s], preferred_element_type=F32)
        total = lax.dot_general(
            grads, held_in[s], (((1,), (1,)), ((), ())), preferred_element_type=F32
        )
        for i in range(PAIR):
            out[j + i, :block] = mixed[:, i * part : (i + 1) * part].astype(BF16)
            out[j + i, block:] = total[:, i * part : (i + 1) * part].astype(BF16)


def own_partials_kernel(hidden, grad, own_in, own_out, out):
    partials((own_in, own_out), 0, out, hidden, grad, at_once)


def side_partials_kernel(hidden, grad, side_in, side_out, to_right, to_left):
    held = (side_in, side_out)
    partials(held, 0, to_right, hidden, grad, at_once)
    partials(held, to_right.shape[0] // PAIR, to_left, hidden, grad, at_once)


def last_kernel(
    place, proj, taps, rates, res, skip, conv, grad, near, far, far_in, far_out,
    hidden, out, to_right, to_left, ext, feat,
):
    finish_kernel(
        place, proj, taps, rates, res, skip, conv, grad, near, far, hidden, out, ext, feat
    )
    held = (far_in, far_out)
    partials(held, 0, to_right, hidden, out, at_once)
    partials(held, to_right.shape[0] // PAIR, to_left, hidden, out, at_once)


def local_fetch_kernel(
    sizes, place, proj, taps, rates, res, skip, weight_in, weight_out,
    conv, grad, far_in, far_out, side_in, side_out, own_in, own_out,
    ext, pad, filt, far_sems, side_sems, own_sems,
):
    weights = (weight_in, weight_out)
    waits = [
        fetch(runs_of(sizes, place, [2]), weights, (far_in, far_out, far_sems)),
        fetch(
            runs_of(sizes, place, [1, sizes["x"] - 1]), weights, (side_in, side_out, side_sems)
        ),
        fetch(runs_of(sizes, place, [0]), weights, (own_in, own_out, own_sems)),
    ]
    local_kernel(proj, taps, rates, res, skip, conv, grad, ext, pad, filt)
    for wait in waits:
        wait()


def join_kernel(start, terms, got, out):
    count = got.shape[0]
    for i in range(terms.shape[0]):
        if start <= i < start + count:
            both = terms[i].astype(F32) + got[i - start].astype(F32)
            out[i] = both.astype(BF16)
        else:
            out[i] = terms[i]


def shape(*dims, dtype=F32):
    return jax.ShapeDtypeStruct(dims, dtype)


def shards(
    sizes,
    tokens,
    cotangent,
    input_weight,
    output_weight,
    short_taps,
    residues,
    decay_rates,
    skip_gain,
):
    n_x, n_zl = sizes["x"], sizes["zl"]
    block, part = tokens.shape
    width = output_weight.shape[0]
    order = residues.shape[1]
    rows = block + TILE
    taps = short_taps.transpose(0, 2, 1)
    rates = decay_rates.T
    res = residues.T
    skip = skip_gain[None]
    place = jnp.stack(
        [
            lax.axis_index("y"),
            lax.axis_index("zh") * sizes["core"] + lax.axis_index("core"),
            lax.axis_index("x"),
        ]
    ).astype(jnp.int32)
    copies = call(
        copy_kernel,
        shape(n_zl, 2 * block, part, dtype=BF16),
        [pltpu.SemaphoreType.DMA((n_zl, 2))],
        in_hbm(tokens),
        in_hbm(cotangent),
        hbm=2,
    )
    pieces = lax.all_to_all(copies, "zl", 0, 0, tiled=True)
    half = n_zl // 2

    def products(count):
        return 8 * count * block * part * width

    right = [(i, (i + 1) % n_x) for i in range(n_x)]
    left = [(i, (i - 1) % n_x) for i in range(n_x)]
    from_left = lax.ppermute(pieces, "x", right)
    from_right = lax.ppermute(pieces, "x", left)
    weights = (in_hbm(input_weight.transpose(1, 0, 2)), in_hbm(output_weight))
    runs = n_zl // PAIR

    def held_shapes(count):
        return [
            shape(count, PAIR * part, 3 * width, dtype=BF16),
            shape(count, width, PAIR * part, dtype=BF16),
        ]

    def sems(count):
        return pltpu.SemaphoreType.DMA((count, 4))

    total, side_in, side_out, far_in, far_out = call(
        functools.partial(near_kernel, sizes),
        [shape(4, block, width)] + held_shapes(2 * runs) + held_shapes(runs),
        held_weights(runs, part, width) + [sems(2 * runs), sems(runs)],
        place,
        pieces,
        *weights,
        flops=16 * products(n_zl),
        hbm=2,
    )
    from_right, _ = lax.optimization_barrier((from_right, total))
    to_far = from_right[half:]
    far_right = lax.ppermute(to_far, "x", left)
    from_left, _ = lax.optimization_barrier((from_left, to_far))
    far_left = lax.ppermute(from_left[:half], "x", right)
    total = call(
        functools.partial(side_kernel, sizes),
        shape(4, block, width),
        [],
        place,
        from_left,
        from_right,
        total,
        side_in,
        side_out,
        flops=16 * products(n_zl),
    )
    ext = pltpu.VMEM((3, rows + TILE, width), F32)
    members = sizes["zh"] * sizes["core"]
    pack = 2 * order + 2 * TILE
    proj, send = call(
        functools.partial(far_kernel, sizes),
        [shape(4, block, width, dtype=BF16), shape(members, pack, width, dtype=BF16)],
        [pltpu.VMEM((4, block, width), F32), ext, pltpu.VMEM((pack, width), F32)],
        place,
        far_left,
        far_right,
        total,
        taps,
        rates,
        far_in,
        far_out,
        flops=products(n_zl),
    )
    conv, grad, far_in, far_out, side_in, side_out, own_in, own_out = call(
        functools.partial(local_fetch_kernel, sizes),
        [shape(rows, width), shape(rows, width)]
        + held_shapes(runs)
        + held_shapes(2 * runs)
        + held_shapes(runs),
        [ext, pltpu.VMEM((2, rows + TILE, width), F32), pltpu.VMEM((rows, width), F32)]
        + [sems(runs), sems(2 * runs), sems(runs)],
        place,
        proj,
        taps,
        rates,
        res,
        skip,
        *weights,
        flops=3 * 10**9,
        hbm=2,
    )
    near_states = lax.all_to_all(send, ("zh", "core"), 0, 0, tiled=True)
    send = call(
        functools.partial(chain_kernel, block),
        shape(sizes["y"], order + 2 * TILE, width, dtype=BF16),
        [],
        place,
        taps,
        rates,
        near_states,
    )
    far_states = lax.all_to_all(send, "y", 0, 0, tiled=True)
    piece = shape(n_zl, 2 * block, part, dtype=BF16)
    half_piece = shape(half, 2 * block, part, dtype=BF16)
    hidden, grad_proj, to_right, to_left = call(
        last_kernel,
        [
            shape(block, width, dtype=BF16),
            shape(3, block, width, dtype=BF16),
            half_piece,
            half_piece,
        ],
        [ext, pltpu.VMEM((3, rows, width), F32)],
        place,
        proj,
        taps,
        rates,
        res,
        skip,
        conv,
        grad,
        near_states,
        far_states,
        far_in,
        far_out,
        flops=products(n_zl),
    )
    far_right = lax.ppermute(to_right, "x", right)
    far_left = lax.ppermute(to_left, "x", left)
    to_right, to_left = call(
        side_partials_kernel,
        [piece, piece],
        [],
        hidden,
        grad_proj,
        side_in,
        side_out,
        flops=products(2 * n_zl),
    )
    to_right = call(functools.partial(join_kernel, 0), piece, [], to_right, far_right)
    from_left = lax.ppermute(to_right, "x", right)
    to_left = call(functools.partial(join_kernel, half), piece, [], to_left, far_left)
    from_right = lax.ppermute(to_left, "x", left)
    own = call(
        own_partials_kernel,
        piece,
        [],
        hidden,
        grad_proj,
        own_in,
        own_out,
        flops=products(n_zl),
    )
    summed = sum(a.astype(F32) for a in (own, from_left, from_right)).astype(BF16)
    summed = lax.all_to_all(summed, "zl", 0, 0, tiled=True)
    total = jnp.sum(summed.astype(F32), axis=0).astype(BF16)
    return total[:block], total[block:]


def solution(mesh, dims=(8, 4, 2, 4, 4)):
    fine = Mesh(mesh.devices.reshape(dims), CTX + TP)
    sizes = dict(zip(CTX + TP, dims))
    return jax.shard_map(
        functools.partial(shards, sizes),
        mesh=fine,
        in_specs=(
            P(CTX, TP),
            P(CTX, TP),
            P(None, None, TP),
            P(TP, None),
            P(None, TP, None),
            P(TP, None),
            P(TP, None),
            P(TP),
        ),
        out_specs=(P(CTX, TP), P(CTX, TP)),
        check_vma=False,
    )
```

```python
import functools

import jax
import jax.numpy as jnp
from jax import lax
from jax.experimental import pallas as pl
from jax.experimental.pallas import tpu as pltpu
from jax.sharding import Mesh
from jax.sharding import PartitionSpec as P

CTX = ("y", "zh", "core")
TP = ("x", "zl")
TILE = 8
AHEAD = 2
GRANT = 16 * 2**20
PAIR = 2
BF16 = jnp.bfloat16
F32 = jnp.float32


def copy_kernel(tokens, cotangent, copies, sems):
    block = tokens.shape[0]
    moves = []
    for i in range(copies.shape[0]):
        for k, rows in enumerate((tokens, cotangent)):
            there = copies.at[i, pl.ds(k * block, block)]
            moves.append(pltpu.make_async_copy(rows, there, sems.at[i, k]))
            moves[-1].start()
    for move in moves:
        move.wait()


def features(ext, proj_ref, taps_ref, rows, last=None, first=None):
    block, width = proj_ref.shape[1:]
    zero = jnp.zeros((TILE, width), F32)
    out = []
    for p in range(3):
        ext[p, :TILE] = zero
        ext[p, TILE : TILE + block] = proj_ref[p].astype(F32)
        ext[p, TILE + block :] = zero
        if last is not None:
            ext[p, TILE - AHEAD : TILE] = last[AHEAD * p : AHEAD * (p + 1)]
            ext[p, TILE + block : TILE + block + AHEAD] = first[AHEAD * p : AHEAD * (p + 1)]
        total = taps_ref[p, 0:1, :] * ext[p, TILE : TILE + rows]
        for k in range(1, 3):
            total = total + taps_ref[p, k : k + 1, :] * ext[p, TILE - k : TILE - k + rows]
        out.append(total)
    return out


def inner_rows(ext, proj_ref, taps_ref, rows):
    block, width = proj_ref.shape[1:]
    query, key_part, value_part = features(ext, proj_ref, taps_ref, rows)
    row = lax.broadcasted_iota(jnp.int32, (rows, 1), 0)
    inside = (row >= AHEAD) & (row < block)
    back = jnp.concatenate([proj_ref[3].astype(F32), jnp.zeros((TILE, width), F32)], axis=0)
    gated = jnp.where(inside, key_part * value_part, 0.0)
    return gated, jnp.where(inside, back * query, 0.0), row.astype(F32)


def state_kernel(proj_ref, taps_ref, rates_ref, send_ref, ext, pack):
    order = rates_ref.shape[0]
    block = proj_ref.shape[1]
    gated, grad_conv, time = inner_rows(ext, proj_ref, taps_ref, block + TILE)
    time = time[:TILE]
    for r in range(order):
        rate = rates_ref[r : r + 1, :]
        fade = jnp.exp(-rate * TILE)
        fwd = gated[:TILE]
        bwd = grad_conv[block - TILE : block]
        for q in range(TILE, block, TILE):
            fwd = fwd * fade + gated[q : q + TILE]
            bwd = bwd * fade + grad_conv[block - TILE - q : block - q]
        fwd = jnp.exp(-rate * (TILE - 1.0 - time)) * fwd
        bwd = jnp.exp(-rate * (time - AHEAD)) * bwd
        pack[r : r + 1] = jnp.sum(fwd, axis=0, keepdims=True)
        pack[order + r : order + r + 1] = jnp.sum(bwd, axis=0, keepdims=True)
    at = 2 * order
    pack[at + TILE :] = jnp.zeros((TILE, pack.shape[1]), F32)
    for p in range(4):
        rows = proj_ref[p].astype(F32)
        pack[at + AHEAD * p : at + AHEAD * (p + 1)] = rows[:AHEAD]
        if p < 3:
            ends = at + TILE + AHEAD * p
            pack[ends : ends + AHEAD] = rows[block - AHEAD :]
    for i in range(send_ref.shape[0]):
        send_ref[i] = pack[...].astype(BF16)


def joint(taps_ref, first, last):
    row = []
    for p in range(3):
        a, b = first[AHEAD * p : AHEAD * p + 1], first[AHEAD * p + 1 : AHEAD * p + 2]
        c, d = last[AHEAD * p : AHEAD * p + 1], last[AHEAD * p + 1 : AHEAD * p + 2]
        t = [taps_ref[p, k : k + 1, :] for k in range(3)]
        row.append((t[0] * a + t[1] * d + t[2] * c, t[0] * b + t[1] * a + t[2] * d))
    back = (first[3 * AHEAD : 3 * AHEAD + 1], first[3 * AHEAD + 1 : 3 * AHEAD + 2])
    gated = tuple(row[1][i] * row[2][i] for i in range(AHEAD))
    return gated, tuple(back[i] * row[0][i] for i in range(AHEAD))


def fader(rates, block):
    def fade(blocks):
        if isinstance(blocks, int):
            return jnp.exp(-rates * float(block * blocks))
        return jnp.exp(-rates * (block * jnp.maximum(blocks, 0)).astype(F32))

    return fade


def group_states(block, taps_ref, rates, got_ref):
    order = rates.shape[0]
    members = got_ref.shape[0]
    fwd, bwd, firsts, lasts = [], [], [], []
    for j in range(members):
        got = got_ref[j].astype(F32)
        fwd.append(got[:order])
        bwd.append(got[order : 2 * order])
        firsts.append(got[2 * order : 2 * order + TILE])
        lasts.append(got[2 * order + TILE :])
    near, far = jnp.exp(-rates * (block - 2.0)), jnp.exp(-rates * (block - 1.0))
    for j in range(1, members):
        gated, grad_conv = joint(taps_ref, firsts[j], lasts[j - 1])
        fwd[j] = fwd[j] + far * gated[0] + near * gated[1]
        bwd[j - 1] = bwd[j - 1] + near * grad_conv[0] + far * grad_conv[1]
    return fwd, bwd, firsts, lasts, near, far


def chain_kernel(block, place_ref, taps_ref, rates_ref, got_ref, send_ref):
    rates = rates_ref[...]
    order = rates.shape[0]
    fade = fader(rates, block)
    fwd, bwd, firsts, lasts, _, _ = group_states(block, taps_ref, rates, got_ref)
    members = len(fwd)
    step = fade(1)
    total_fwd, total_bwd = fwd[0], bwd[-1]
    for j in range(1, members):
        total_fwd = total_fwd * step + fwd[j]
        total_bwd = total_bwd * step + bwd[members - 1 - j]
    ends = jnp.concatenate([firsts[0], lasts[-1]], axis=0).astype(BF16)
    for i in range(send_ref.shape[0]):
        send_ref[i, :order] = jnp.where(place_ref[0] < i, total_fwd, total_bwd).astype(BF16)
        send_ref[i, order:] = ends


def local_kernel(
    proj_ref, taps_ref, rates_ref, res_ref, skip_ref, conv_ref, grad_ref, ext, pad, filt_ref
):
    rows, width = conv_ref.shape
    gated, grad_conv, time = inner_rows(ext, proj_ref, taps_ref, rows)
    taps = jnp.zeros((rows, width), F32)
    for r in range(rates_ref.shape[0]):
        taps = taps + res_ref[r : r + 1, :] * jnp.exp(-rates_ref[r : r + 1, :] * (time + 1.0))
    filt_ref[...] = taps
    zero = jnp.zeros((TILE, width), F32)
    pad[0, :TILE] = zero
    pad[0, TILE:] = gated
    pad[1, :rows] = grad_conv
    pad[1, rows:] = zero
    direct = skip_ref[...] + jnp.sum(res_ref[...], axis=0, keepdims=True)
    for lane in range(0, width, 128):
        lanes = slice(lane, lane + 128)
        total = direct[:, lanes] * pad[0, TILE:, lanes]
        for m in range(1, TILE + 1):
            moved = pad[0, TILE - m : TILE - m + rows, lanes]
            for q in range(0, rows, TILE):
                tap = filt_ref[q + m - 1 : q + m, lanes]
                part = total[q:] + tap * moved[: rows - q]
                total = part if q == 0 else jnp.concatenate([total[:q], part], axis=0)
        conv_ref[:, lanes] = total
        total = direct[:, lanes] * pad[1, :rows, lanes]
        for m in range(1, TILE + 1):
            moved = pad[1, m : m + rows, lanes]
            for q in range(0, rows, TILE):
                tap = filt_ref[q + m - 1 : q + m, lanes]
                part = total[: rows - q] + tap * moved[q:]
                total = part if q == 0 else jnp.concatenate([part, total[rows - q :]], axis=0)
        grad_ref[:, lanes] = total


def finish_kernel(
    place_ref, proj_ref, taps_ref, rates_ref, res_ref, skip_ref, conv_ref, grad_ref,
    near_ref, far_ref, hidden_ref, out_ref, ext, feat,
):
    rates = rates_ref[...]
    res_all = res_ref[...]
    skip = skip_ref[...]
    order, width = rates.shape
    rows = conv_ref.shape[0]
    block = rows - TILE
    group, member = place_ref[0], place_ref[1]
    groups, members = far_ref.shape[0], near_ref.shape[0]
    fade = fader(rates, block)
    fwd, bwd, firsts, lasts, near, far = group_states(block, taps_ref, rates, near_ref)

    def rows_of(ref, index, start, there):
        got = ref[jnp.where(there, index, 0)].astype(F32)
        return jnp.where(there, got[start : start + TILE], 0.0)

    nothing = jnp.zeros((TILE, width), F32)
    whole = [far_ref[i].astype(F32) for i in range(groups)]
    head = [w[order : order + TILE] for w in whole] + [nothing]
    tail = [nothing] + [w[order + TILE :] for w in whole]
    ahead = jnp.zeros_like(rates)
    behind = jnp.zeros_like(rates)
    step, stride, most = fade(1), fade(members), fade(members - 1)
    for i in range(groups):
        gated, _ = joint(taps_ref, head[i], tail[i])
        total = whole[i][:order] + most * (far * gated[0] + near * gated[1])
        ahead = jnp.where(i < group, ahead * stride + total, ahead)
        j = groups - 1 - i
        _, grad_conv = joint(taps_ref, head[j + 1], tail[j + 1])
        total = whole[j][:order] + most * (near * grad_conv[0] + far * grad_conv[1])
        behind = jnp.where(j > group, behind * stride + total, behind)
    tail_before = rows_of(far_ref, group - 1, order + TILE, group > 0)
    head_behind = rows_of(far_ref, group + 1, order, group < groups - 1)
    gated, _ = joint(taps_ref, firsts[0], tail_before)
    _, grad_conv = joint(taps_ref, head_behind, lasts[-1])
    fwd[0] = fwd[0] + far * gated[0] + near * gated[1]
    bwd[-1] = bwd[-1] + near * grad_conv[0] + far * grad_conv[1]
    for j in range(members):
        ahead = jnp.where(j < member, ahead * step + fwd[j], ahead)
        i = members - 1 - j
        behind = jnp.where(i > member, behind * step + bwd[i], behind)

    last = rows_of(near_ref, member - 1, 2 * order + TILE, member > 0)
    last = jnp.where(member > 0, last, tail_before)
    first = rows_of(near_ref, member + 1, 2 * order, member < members - 1)
    first = jnp.where(member < members - 1, first, head_behind)
    query, key_part, value_part = features(ext, proj_ref, taps_ref, rows, last, first)
    row = lax.broadcasted_iota(jnp.int32, (TILE, 1), 0)
    next_back = jnp.where(row < AHEAD, pltpu.roll(first, AHEAD, 0), 0.0)
    back = jnp.concatenate([proj_ref[3].astype(F32), next_back], axis=0)
    gated = key_part * value_part
    grad_conv = back * query

    g = [gated[i : i + 1] for i in (0, 1, block, block + 1)]
    h = [grad_conv[i : i + 1] for i in (0, 1, block, block + 1)]
    grow = jnp.exp(rates)
    ahead = ahead + grow * g[0] + (grow * grow) * g[1]
    behind = behind + (grow * grow) * h[2] + grow * h[3]
    lag0 = skip + jnp.sum(res_all, axis=0, keepdims=True)
    lag1 = jnp.sum(res_all * jnp.exp(-rates), axis=0, keepdims=True)
    less = jnp.sum(res_all * grow, axis=0, keepdims=True)

    def two(a, b):
        return jnp.where(row == 0, a, jnp.where(row == 1, b, 0.0))

    def with_ends(array, top, bottom):
        return jnp.concatenate(
            [array[:TILE] + top, array[TILE:block], array[block:] + bottom], axis=0
        )

    conv_out = with_ends(
        conv_ref[...],
        two(skip * g[0] - less * g[1], skip * g[1]),
        two(lag0 * g[2], lag0 * g[3] + lag1 * g[2]),
    )
    grad_gated = with_ends(
        grad_ref[...],
        two(lag0 * h[0] + lag1 * h[1], lag0 * h[1]),
        two(skip * h[2], skip * h[3] - less * h[2]),
    )
    time = row.astype(F32)
    ahead = res_all * ahead
    behind = res_all * behind
    conv_tiles = [[] for _ in range(0, rows, TILE)]
    grad_tiles = [[] for _ in range(0, rows, TILE)]
    for lane in range(0, width, 128):
        lanes = slice(lane, lane + 128)
        conv_sum = [conv_out[q : q + TILE, lanes] for q in range(0, rows, TILE)]
        grad_sum = [grad_gated[q : q + TILE, lanes] for q in range(0, rows, TILE)]
        for r in range(order):
            rate = rates[r : r + 1, lanes]
            fall = jnp.exp(-rate * TILE)
            later = ahead[r : r + 1, lanes] * jnp.exp(-rate * (time + 1.0))
            sooner = behind[r : r + 1, lanes] * jnp.exp(-rate * (AHEAD - time))
            for q in range(len(conv_sum)):
                conv_sum[q] = conv_sum[q] + later
                grad_sum[-1 - q] = grad_sum[-1 - q] + sooner
                later = later * fall
                sooner = sooner * fall
        for q in range(len(conv_sum)):
            conv_tiles[q].append(conv_sum[q])
            grad_tiles[q].append(grad_sum[q])
    conv_out = jnp.concatenate([jnp.concatenate(t, axis=1) for t in conv_tiles], axis=0)
    grad_gated = jnp.concatenate([jnp.concatenate(t, axis=1) for t in grad_tiles], axis=0)
    hidden_ref[...] = (query * conv_out)[:block].astype(BF16)
    feat[0] = back * conv_out
    feat[1] = grad_gated * value_part
    feat[2] = grad_gated * key_part
    for p in range(3):
        total = taps_ref[p, 0:1, :] * feat[p, :block]
        for k in range(1, 3):
            total = total + taps_ref[p, k : k + 1, :] * feat[p, k : k + block]
        out_ref[p] = total.astype(BF16)


def in_hbm(array):
    return pltpu.with_memory_space_constraint(array, pltpu.HBM)


def call(kernel, outs, scratch, *args, flops=0, hbm=0):
    whole = pl.BlockSpec(memory_space=pltpu.VMEM)
    far = pl.BlockSpec(memory_space=pltpu.HBM)
    scalar = pl.BlockSpec(memory_space=pltpu.SMEM)
    specs = [
        scalar if a.dtype == jnp.int32 else far if i >= len(args) - hbm else whole
        for i, a in enumerate(args)
    ]
    cost = pl.CostEstimate(flops=flops, bytes_accessed=0, transcendentals=0) if flops else None
    return pl.pallas_call(
        kernel,
        out_shape=outs,
        scratch_shapes=scratch,
        in_specs=specs,
        out_specs=jax.tree.map(lambda _: whole, outs),
        cost_estimate=cost,
        compiler_params=pltpu.CompilerParams(vmem_limit_bytes=GRANT),
    )(*args)


def load_weights(blocks, weight_in, weight_out, held_in, held_out, sems, ahead=2):
    span = held_in.shape[1]
    width = weight_out.shape[0]
    part = span // PAIR
    copies = []
    for s, block in enumerate(blocks):
        at = pl.ds(pl.multiple_of(block * part, part), span)
        moves = [
            pltpu.make_async_copy(
                weight_in.at[p, at, :],
                held_in.at[s, :, pl.ds(p * width, width)],
                sems.at[s, p],
            )
            for p in range(3)
        ]
        moves.append(
            pltpu.make_async_copy(weight_out.at[:, at], held_out.at[s], sems.at[s, 3])
        )
        copies.append(moves)

    def start(s):
        for copy in copies[s]:
            copy.start()

    for s in range(min(ahead, len(copies))):
        start(s)

    def ready(s):
        for copy in copies[s]:
            copy.wait()
        if s + ahead < len(copies):
            start(s + ahead)

    return ready


def at_once(s):
    pass


def held_weights(count, part, width):
    return [
        pltpu.VMEM((count, PAIR * part, 3 * width), BF16),
        pltpu.VMEM((count, width, PAIR * part), BF16),
        pltpu.SemaphoreType.DMA((count, 4)),
    ]


def project(
    sizes, offsets, place_ref, pieces, weights, old, total, held_in, held_out, sems=None, also=None
):
    n_x, n_zl = sizes["x"], sizes["zl"]
    block = pieces[0].shape[1] // 2
    width = total.shape[2]
    work = [
        (piece, j, lax.rem(place_ref[2] + k, n_x) * n_zl + start + j)
        for piece, (k, start) in zip(pieces, offsets)
        for j in range(0, piece.shape[0], PAIR)
    ]
    ready = at_once
    if sems is not None:
        ready = load_weights([w[2] for w in work], *weights, held_in, held_out, sems)
    if also is not None:
        also()
    for s, (piece, j, _) in enumerate(work):
        run = range(j, j + PAIR)
        part_in = jnp.concatenate([piece[i, :block] for i in run], axis=1)
        part_grad = jnp.concatenate([piece[i, block:] for i in run], axis=1)
        ready(s)
        term = jnp.dot(part_in, held_in[s], preferred_element_type=F32)
        back = lax.dot_general(
            part_grad, held_out[s], (((1,), (1,)), ((), ())), preferred_element_type=F32
        )
        terms = [term[:, p * width : (p + 1) * width] for p in range(3)] + [back]
        for p in range(4):
            if s == 0 and old is None:
                total[p] = terms[p]
            else:
                total[p] = (old if s == 0 else total)[p] + terms[p]


def near_kernel(sizes, place, piece, weight_in, weight_out, total, *held):
    project(sizes, [(0, 0)], place, [piece], (weight_in, weight_out), None, total, *held)


def side_kernel(
    sizes, place, left, right, old, weight_in, weight_out, total, far_in, far_out, *held
):
    n_x, n_zl = sizes["x"], sizes["zl"]
    offsets = [(n_x - 1, 0), (1, 0)]
    weights = (weight_in, weight_out)
    blocks = [lax.rem(place[2] + 2, n_x) * n_zl + j for j in range(0, n_zl, PAIR)]
    waits = []

    def fetch():
        waits.append(load_weights(blocks, *weights, far_in, far_out, held[3], ahead=len(blocks)))

    project(sizes, offsets, place, [left, right], weights, old, total, *held[:3], also=fetch)
    for s in range(len(blocks)):
        waits[0](s)


def far_kernel(
    sizes, place, left, right, old, taps, rates, far_in, far_out, proj, send, total, ext, pack
):
    offsets = [(2, 0), (2, left.shape[0])]
    project(sizes, offsets, place, [left, right], None, old, total, far_in, far_out)
    proj[...] = total[...].astype(BF16)
    state_kernel(proj, taps, rates, send, ext, pack)


def partials(held, start, out, hidden, grad, ready):
    held_in, held_out = held[:2]
    block = hidden.shape[0]
    part = out.shape[2]
    for j in range(0, out.shape[0], PAIR):
        s = start + j // PAIR
        grads = jnp.concatenate([grad[p] for p in range(3)], axis=1)
        ready(s)
        mixed = jnp.dot(hidden[...], held_out[s], preferred_element_type=F32)
        total = lax.dot_general(
            grads, held_in[s], (((1,), (1,)), ((), ())), preferred_element_type=F32
        )
        for i in range(PAIR):
            out[j + i, :block] = mixed[:, i * part : (i + 1) * part].astype(BF16)
            out[j + i, block:] = total[:, i * part : (i + 1) * part].astype(BF16)


def partials_kernel(sizes, offset, place, hidden, grad, weight_in, weight_out, out, *held):
    n_x, n_zl = sizes["x"], sizes["zl"]
    base = lax.rem(place[2] + offset, n_x) * n_zl
    blocks = [base + j for j in range(0, out.shape[0], PAIR)]
    ready = load_weights(blocks, weight_in, weight_out, *held)
    partials(held, 0, out, hidden, grad, ready)


def side_partials_kernel(hidden, grad, side_in, side_out, to_right, to_left):
    held = (side_in, side_out)
    partials(held, 0, to_right, hidden, grad, at_once)
    partials(held, to_right.shape[0] // PAIR, to_left, hidden, grad, at_once)


def last_kernel(
    sizes, place, proj, taps, rates, res, skip, conv, grad, near, far, far_in, far_out,
    weight_in, weight_out,
    hidden, out, to_right, to_left, side_in, side_out, ext, feat, sems,
):
    n_x, n_zl = sizes["x"], sizes["zl"]
    side = [
        lax.rem(place[2] + k, n_x) * n_zl + j for k in (1, n_x - 1) for j in range(0, n_zl, PAIR)
    ]
    ready = load_weights(side, weight_in, weight_out, side_in, side_out, sems, ahead=len(side))
    finish_kernel(
        place, proj, taps, rates, res, skip, conv, grad, near, far, hidden, out, ext, feat
    )
    held = (far_in, far_out)
    partials(held, 0, to_right, hidden, out, at_once)
    partials(held, to_right.shape[0] // PAIR, to_left, hidden, out, at_once)
    for s in range(len(side)):
        ready(s)


def local_fetch_kernel(
    sizes, place, proj, taps, rates, res, skip, weight_in, weight_out,
    conv, grad, far_in, far_out, ext, pad, filt, sems,
):
    n_x, n_zl = sizes["x"], sizes["zl"]
    far = [lax.rem(place[2] + 2, n_x) * n_zl + j for j in range(0, n_zl, PAIR)]
    ready = load_weights(far, weight_in, weight_out, far_in, far_out, sems, ahead=len(far))
    local_kernel(proj, taps, rates, res, skip, conv, grad, ext, pad, filt)
    for s in range(len(far)):
        ready(s)


def join_kernel(start, terms, got, out):
    count = got.shape[0]
    for i in range(terms.shape[0]):
        if start <= i < start + count:
            both = terms[i].astype(F32) + got[i - start].astype(F32)
            out[i] = both.astype(BF16)
        else:
            out[i] = terms[i]


def shape(*dims, dtype=F32):
    return jax.ShapeDtypeStruct(dims, dtype)


def shards(
    sizes,
    tokens,
    cotangent,
    input_weight,
    output_weight,
    short_taps,
    residues,
    decay_rates,
    skip_gain,
):
    n_x, n_zl = sizes["x"], sizes["zl"]
    block, part = tokens.shape
    width = output_weight.shape[0]
    order = residues.shape[1]
    rows = block + TILE
    taps = short_taps.transpose(0, 2, 1)
    rates = decay_rates.T
    res = residues.T
    skip = skip_gain[None]
    place = jnp.stack(
        [
            lax.axis_index("y"),
            lax.axis_index("zh") * sizes["core"] + lax.axis_index("core"),
            lax.axis_index("x"),
        ]
    ).astype(jnp.int32)
    copies = call(
        copy_kernel,
        shape(n_zl, 2 * block, part, dtype=BF16),
        [pltpu.SemaphoreType.DMA((n_zl, 2))],
        in_hbm(tokens),
        in_hbm(cotangent),
        hbm=2,
    )
    pieces = lax.all_to_all(copies, "zl", 0, 0, tiled=True)
    half = n_zl // 2

    def products(count):
        return 8 * count * block * part * width

    right = [(i, (i + 1) % n_x) for i in range(n_x)]
    left = [(i, (i - 1) % n_x) for i in range(n_x)]
    from_left = lax.ppermute(pieces, "x", right)
    from_right = lax.ppermute(pieces, "x", left)
    weights = (in_hbm(input_weight.transpose(1, 0, 2)), in_hbm(output_weight))
    total = call(
        functools.partial(near_kernel, sizes),
        shape(4, block, width),
        held_weights(n_zl // PAIR, part, width),
        place,
        pieces,
        *weights,
        flops=products(n_zl),
        hbm=2,
    )
    from_left, _ = lax.optimization_barrier((from_left, total))
    from_right, _ = lax.optimization_barrier((from_right, total))
    far_left = lax.ppermute(from_left[:half], "x", right)
    far_right = lax.ppermute(from_right[half:], "x", left)
    runs = n_zl // PAIR
    held_shapes = [
        shape(runs, PAIR * part, 3 * width, dtype=BF16),
        shape(runs, width, PAIR * part, dtype=BF16),
    ]
    total, far_in, far_out = call(
        functools.partial(side_kernel, sizes),
        [shape(4, block, width), *held_shapes],
        held_weights(2 * runs, part, width) + [pltpu.SemaphoreType.DMA((runs, 4))],
        place,
        from_left,
        from_right,
        total,
        *weights,
        flops=products(2 * n_zl),
        hbm=2,
    )
    ext = pltpu.VMEM((3, rows + TILE, width), F32)
    members = sizes["zh"] * sizes["core"]
    pack = 2 * order + 2 * TILE
    proj, send = call(
        functools.partial(far_kernel, sizes),
        [shape(4, block, width, dtype=BF16), shape(members, pack, width, dtype=BF16)],
        [pltpu.VMEM((4, block, width), F32), ext, pltpu.VMEM((pack, width), F32)],
        place,
        far_left,
        far_right,
        total,
        taps,
        rates,
        far_in,
        far_out,
        flops=products(n_zl),
    )
    conv, grad, far_in, far_out = call(
        functools.partial(local_fetch_kernel, sizes),
        [shape(rows, width), shape(rows, width), *held_shapes],
        [
            ext,
            pltpu.VMEM((2, rows + TILE, width), F32),
            pltpu.VMEM((rows, width), F32),
            pltpu.SemaphoreType.DMA((runs, 4)),
        ],
        place,
        proj,
        taps,
        rates,
        res,
        skip,
        *weights,
        flops=3 * 10**9,
        hbm=2,
    )
    near_states = lax.all_to_all(send, ("zh", "core"), 0, 0, tiled=True)
    send = call(
        functools.partial(chain_kernel, block),
        shape(sizes["y"], order + 2 * TILE, width, dtype=BF16),
        [],
        place,
        taps,
        rates,
        near_states,
    )
    far_states = lax.all_to_all(send, "y", 0, 0, tiled=True)
    piece = shape(n_zl, 2 * block, part, dtype=BF16)
    half_piece = shape(half, 2 * block, part, dtype=BF16)
    side_shapes = [
        shape(2 * runs, PAIR * part, 3 * width, dtype=BF16),
        shape(2 * runs, width, PAIR * part, dtype=BF16),
    ]
    hidden, grad_proj, to_right, to_left, side_in, side_out = call(
        functools.partial(last_kernel, sizes),
        [
            shape(block, width, dtype=BF16),
            shape(3, block, width, dtype=BF16),
            half_piece,
            half_piece,
            *side_shapes,
        ],
        [ext, pltpu.VMEM((3, rows, width), F32)]
        + [pltpu.SemaphoreType.DMA((2 * runs, 4))],
        place,
        proj,
        taps,
        rates,
        res,
        skip,
        conv,
        grad,
        near_states,
        far_states,
        far_in,
        far_out,
        *weights,
        flops=products(n_zl),
        hbm=2,
    )
    far_right = lax.ppermute(to_right, "x", right)
    far_left = lax.ppermute(to_left, "x", left)
    to_right, to_left = call(
        side_partials_kernel,
        [piece, piece],
        [],
        hidden,
        grad_proj,
        side_in,
        side_out,
        flops=products(2 * n_zl),
    )
    to_right = call(functools.partial(join_kernel, 0), piece, [], to_right, far_right)
    from_left = lax.ppermute(to_right, "x", right)
    to_left = call(functools.partial(join_kernel, half), piece, [], to_left, far_left)
    from_right = lax.ppermute(to_left, "x", left)
    own = call(
        functools.partial(partials_kernel, sizes, 0),
        piece,
        held_weights(runs, part, width),
        place,
        hidden,
        grad_proj,
        *weights,
        flops=products(n_zl),
        hbm=2,
    )
    summed = sum(a.astype(F32) for a in (own, from_left, from_right)).astype(BF16)
    summed = lax.all_to_all(summed, "zl", 0, 0, tiled=True)
    total = jnp.sum(summed.astype(F32), axis=0).astype(BF16)
    return total[:block], total[block:]


def solution(mesh, dims=(8, 4, 2, 4, 4)):
    fine = Mesh(mesh.devices.reshape(dims), CTX + TP)
    sizes = dict(zip(CTX + TP, dims))
    return jax.shard_map(
        functools.partial(shards, sizes),
        mesh=fine,
        in_specs=(
            P(CTX, TP),
            P(CTX, TP),
            P(None, None, TP),
            P(TP, None),
            P(None, TP, None),
            P(TP, None),
            P(TP, None),
            P(TP),
        ),
        out_specs=(P(CTX, TP), P(CTX, TP)),
        check_vma=False,
    )
```
